32 devices in a mesh: depth: 4 (over y, core), lat: 8 (over z, x).
Axes of the slice: x: 2, y: 2, z: 4, core: 2. Of those that a mesh axis runs over, the one named last changes fastest.
Arguments:
- volume: float32 [128, 128, 128], P('depth', 'lat'), may hold values from -6 to 6
Outputs:
- diffused: float32 [128, 128, 128], P('depth', 'lat')
The draws below stay inside these ranges and needn't reach their ends.
All inputs are finite; a program needn't handle non-finite values.
Results may differ from the reference program's by a relative error of at most 0.0003.
Values sent between devices are 32-bit elements; how exact they have to be, the bound alone decides.
A program may use at most 64 MiB of HBM per device.

```python
import math
import jax
import jax.numpy as jnp
from jax import lax

NX = 128
NY = 128
NZ = 128


def draw_volume(key, part):
    key_freq, key_phase, key_noise = jax.random.split(key, 3)
    depth_pos = (jnp.arange(NZ, dtype=jnp.float32) / NZ)[:, None, None]
    row_pos = (jnp.arange(NY, dtype=jnp.float32) / NY)[None, :, None]
    column_pos = (jnp.arange(NX, dtype=jnp.float32) / NX)[None, None, :]
    frequencies = jax.random.uniform(key_freq, (3, 3), jnp.float32, 0.5, 2.5)
    phases = jax.random.uniform(key_phase, (3,), jnp.float32, 0.0, 2.0 * math.pi)
    smooth_part = jnp.zeros((NZ, NY, NX), jnp.float32)
    for index in range(3):
        angle_sum = frequencies[index, 0] * depth_pos + frequencies[index, 1] * row_pos + frequencies[index, 2] * column_pos
        smooth_part = smooth_part + 0.7 * jnp.cos(2.0 * math.pi * angle_sum + phases[index])
    noise = jnp.clip(jax.random.normal(key_noise, (NZ, NY, NX), jnp.float32), -6.0, 6.0) * 0.6
    return smooth_part + noise


def setup_inputs(seed: int = 0) -> dict:
    streams_of = jax.random.split(jax.random.key(seed), 2)
    volume = draw_volume(jax.random.fold_in(streams_of[1], 71), 0)
    return dict(volume=volume)


TAU = 300.0
LAMBDA = 0.5


def smooth_axis(field, axis):
    length = field.shape[axis]
    widths = [(0, 0)] * field.ndim
    widths[axis] = (1, 1)
    padded = jnp.pad(field, widths)
    before = lax.slice_in_dim(padded, 0, length, axis=axis)
    after = lax.slice_in_dim(padded, 2, length + 2, axis=axis)
    return 0.25 * (before + 2.0 * field + after)


def conductance(diff):
    ratio = diff / LAMBDA
    return 1.0 / (1.0 + ratio * ratio)


def forward_conductance(smoothed, axis):
    length = smoothed.shape[axis]
    diff = lax.slice_in_dim(smoothed, 1, length, axis=axis) - lax.slice_in_dim(smoothed, 0, length - 1, axis=axis)
    widths = [(0, 0)] * smoothed.ndim
    widths[axis] = (0, 1)
    return jnp.pad(conductance(diff), widths)


def thomas(forward, source):
    zero_row = jnp.zeros_like(forward[:1])
    lower = -3.0 * TAU * jnp.concatenate([zero_row, forward[:-1]], axis=0)
    upper = -3.0 * TAU * forward
    diag = 1.0 - lower - upper

    def sweep_down(carry, row):
        upper_prev, source_prev = carry
        low_val, diag_val, up_val, src_val = row
        pivot = diag_val - low_val * upper_prev
        upper_new = up_val / pivot
        source_new = (src_val - low_val * source_prev) / pivot
        return (upper_new, source_new), (upper_new, source_new)

    start = (jnp.zeros_like(source[0]), jnp.zeros_like(source[0]))
    _, (uppers, sources) = lax.scan(sweep_down, start, (lower, diag, upper, source))

    def sweep_up(later, row):
        up_val, src_val = row
        value = src_val - up_val * later
        return value, value

    _, values = lax.scan(sweep_up, jnp.zeros_like(source[0]), (uppers, sources), reverse=True)
    return values


def solve_columns(pair):
    forward, source = pair
    return thomas(forward.T, source.T).T


def solve_leading(pair):
    forward, source = pair
    return thomas(forward, source)


def reference(volume):
    smoothed = smooth_axis(smooth_axis(smooth_axis(volume, 2), 1), 0)
    cond_x = forward_conductance(smoothed, 2)
    cond_y = forward_conductance(smoothed, 1)
    cond_z = forward_conductance(smoothed, 0)
    solved_x = lax.map(solve_columns, (cond_x, volume))
    solved_y = lax.map(solve_leading, (cond_y, volume))
    moved = lax.map(solve_leading, (jnp.swapaxes(cond_z, 0, 1), jnp.swapaxes(volume, 0, 1)))
    solved_z = jnp.swapaxes(moved, 0, 1)
    return (solved_x + solved_y + solved_z) / 3.0
```

```python
import functools

import jax
import jax.numpy as jnp
from jax import lax
from jax.experimental import pallas as pl
from jax.experimental.pallas import tpu as pltpu
from jax.sharding import PartitionSpec as P

TAU = 300.0
LAMBDA = 0.5
MESH = pl.DeviceIdType.MESH
SCALE = (64.0 * LAMBDA) ** 2
PITCH = 24
BASE = 8
LEAF = 8


def round_up(value, to):
    return (value + to - 1) // to * to


def recip(value):
    guess = pl.reciprocal(value, approx=True)
    return guess * (2.0 - value * guess)


def coupling(diff):
    return (3.0 * TAU * SCALE) * recip(SCALE + diff * diff)


def smooth_x(field):
    lane = lax.broadcasted_iota(jnp.int32, field.shape, 1)
    width = field.shape[1]
    before = jnp.where(lane == 0, 0.0, pltpu.roll(field, 1, 1))
    after = jnp.where(lane == width - 1, 0.0, pltpu.roll(field, width - 1, 1))
    return (before + after) + (field + field)


def eliminate(lo, hi, couple, source, keep):
    starts = list(range(lo, hi, LEAF))
    state = []
    for start in starts:
        state.append([1.0, couple(start - 1), source(start), None, None])
    for step in range(LEAF - 1):
        for part, start in enumerate(starts):
            excess, fill, src, excess_low, src_low = state[part]
            cell = start + step
            after = couple(cell)
            inverse = recip(excess + fill + after)
            onward = after * inverse
            back = fill * inverse
            keep(cell, onward, back, src * inverse)
            add_excess = back * excess
            add_src = back * src
            state[part] = [
                1.0 + onward * excess,
                onward * fill,
                source(cell + 1) + onward * src,
                add_excess if excess_low is None else excess_low + add_excess,
                add_src if src_low is None else src_low + add_src,
            ]
    blocks = [(start, start + LEAF, part) for start, part in zip(starts, state)]
    while len(blocks) > 1:
        merged = []
        for first, second in zip(blocks[::2], blocks[1::2]):
            e1, f1, s1, el1, sl1 = first[2]
            e2, f2, s2, el2, sl2 = second[2]
            excess = e1 + el2
            src = s1 + sl2
            inverse = recip(excess + f1 + f2)
            onward = f2 * inverse
            back = f1 * inverse
            keep(first[1] - 1, onward, back, src * inverse)
            merged.append(
                (
                    first[0],
                    second[1],
                    [
                        e2 + onward * excess,
                        onward * f1,
                        s2 + onward * src,
                        el1 + back * excess,
                        sl1 + back * src,
                    ],
                )
            )
        blocks = merged
    e, f, s, el, sl = blocks[0][2]
    return el, sl, f, e, s


def substitute(lo, hi, before, last, load, emit):
    known = {lo - 1: before, hi - 1: last}
    emit(hi - 1, last)
    size = hi - lo
    while size > LEAF:
        for start in range(lo, hi, size):
            middle = start + size // 2 - 1
            onward, back, part = load(middle)
            value = part + back * known[start - 1] + onward * known[start + size - 1]
            known[middle] = value
            emit(middle, value)
        size = size // 2
    current = {start: known[start + LEAF - 1] for start in range(lo, hi, LEAF)}
    for step in range(LEAF - 2, -1, -1):
        for start in range(lo, hi, LEAF):
            onward, back, part = load(start + step)
            value = part + back * known[start - 1] + onward * current[start]
            current[start] = value
            emit(start + step, value)


def solve_reduced(count, rows, got):
    excess = got(0, 3)
    src = got(0, 4)
    onwards, parts = [], []
    for k in range(count - 1):
        couple = got(k + 1, 2)
        excess = excess + got(k + 1, 0)
        src = src + got(k + 1, 1)
        inverse = recip(excess + couple)
        onward = couple * inverse
        onwards.append(onward)
        parts.append(src * inverse)
        excess = got(k + 1, 3) + onward * excess
        src = got(k + 1, 4) + onward * src
    value = src * recip(excess)
    values = [value]
    for k in range(count - 2, -1, -1):
        value = parts[k] + onwards[k] * value
        values.append(value)
    return values[::-1]


def kernel(
    depth_total, lat_total, planes, rows,
    vol, out,
    pack, yh, zh, cn, sm_x, sm, yy,
    zw, zv, zg, yw, yv, yg,
    zsnd, zrcv, zret, zfin, zsep, ysnd, yrcv, yret, yfin, ysep,
    halo_send, halo_recv, zs_send, zs_recv, zr_send, zr_recv,
    ys_send, ys_recv, yr_send, yr_recv,
):
    dm = lax.axis_index("depth")
    lm = lax.axis_index("lat")
    has = {
        (-1, 0): dm > 0,
        (1, 0): dm < depth_total - 1,
        (0, -1): lm > 0,
        (0, 1): lm < lat_total - 1,
    }
    for dz in (-1, 1):
        for dy in (-1, 1):
            has[(dz, dy)] = jnp.logical_and(has[(dz, 0)], has[(0, dy)])
    corners = [(dz, dy) for dz in (-1, 1) for dy in (-1, 1)]

    barrier = pltpu.get_barrier_semaphore()
    for step in range(1, lat_total):
        pl.semaphore_signal(
            barrier, inc=1, device_id=(dm, lax.rem(lm + step, lat_total)), device_id_type=MESH
        )
    for step in range(1, depth_total):
        pl.semaphore_signal(
            barrier, inc=1, device_id=(lax.rem(dm + step, depth_total), lm), device_id_type=MESH
        )
    expected = jnp.int32(lat_total + depth_total - 2)
    for dz, dy in corners:
        expected = expected + has[(dz, dy)].astype(jnp.int32)

        @pl.when(has[(dz, dy)])
        def _():
            pl.semaphore_signal(
                barrier, inc=1, device_id=(dm + dz, lm + dy), device_id_type=MESH
            )

    for side, first in ((0, 0), (1, rows - 2)):
        for j in range(2):
            pack[side, pl.ds(j, planes, stride=2), :] = vol[
                pl.ds(first + j, planes, stride=rows), :
            ]
    pl.semaphore_wait(barrier, expected)

    def halo_copy(index, way):
        dz, dy = way
        zi, yi = (dz + 1) // 2, (dy + 1) // 2
        if dy == 0:
            src = vol.at[pl.ds(0 if dz < 0 else (planes - 2) * rows, 2 * rows)]
            dst = zh.at[1 - zi]
        elif dz == 0:
            src = pack.at[yi]
            dst = yh.at[1 - yi]
        else:
            src = pack.at[yi, pl.ds(0 if dz < 0 else 2 * planes - 8, 8)]
            dst = cn.at[1 - zi, 1 - yi]
        return pltpu.make_async_remote_copy(
            src_ref=src,
            dst_ref=dst,
            send_sem=halo_send.at[index],
            recv_sem=halo_recv.at[index],
            device_id=(dm + dz, lm + dy),
            device_id_type=MESH,
        )

    ways = [(0, -1), (0, 1), (-1, 0), (1, 0)] + corners
    opposite = {way: ways.index((-way[0], -way[1])) for way in ways}
    for index, way in enumerate(ways):

        @pl.when(has[way])
        def _():
            halo_copy(index, way).start()

    def at(plane, row):
        return BASE + PITCH * (plane + 2) + row

    for plane in range(planes):
        sm_x[pl.ds(at(plane, 0), rows), :] = smooth_x(vol[pl.ds(plane * rows, rows), :])

    for index, way in enumerate(ways):
        back = opposite[way]

        @pl.when(has[way])
        def _():
            halo_copy(index, way).wait_send()
            halo_copy(back, ways[back]).wait_recv()

        @pl.when(jnp.logical_not(has[way]))
        def _():
            dz, dy = way
            zi, yi = (dz + 1) // 2, (dy + 1) // 2
            if dy == 0:
                zh[zi] = jnp.zeros(zh.shape[1:], jnp.float32)
            elif dz == 0:
                yh[yi] = jnp.zeros(yh.shape[1:], jnp.float32)
            else:
                cn[zi, yi] = jnp.zeros(cn.shape[2:], jnp.float32)

    for side, first in ((0, -2), (1, planes)):
        for j in range(2):
            sm_x[pl.ds(at(first + j, 0), rows), :] = smooth_x(zh[side, pl.ds(j * rows, rows), :])
    for side, near, edge in ((0, -1, 0), (1, rows, rows - 1)):
        far_j, near_j = (0, 1) if side == 0 else (1, 0)
        near_row = smooth_x(yh[side, pl.ds(near_j, planes, stride=2), :])
        far_row = smooth_x(yh[side, pl.ds(far_j, planes, stride=2), :])
        sm_x[pl.ds(at(0, near), planes, stride=PITCH), :] = near_row
        edge_row = sm_x[pl.ds(at(0, edge), planes, stride=PITCH), :]
        yy[side, pl.ds(8, planes), :] = (far_row + edge_row) + (near_row + near_row)
        for zside, first, base in ((0, -2, 4), (1, planes, 0)):
            tile = smooth_x(cn[zside, side])
            for j in range(2):
                k = base + 2 * j + near_j
                sm_x[pl.ds(at(first + j, near), 1), :] = tile[k : k + 1]
            j = 1 if zside == 0 else 0
            k = base + 2 * j
            near_one = tile[k + near_j : k + near_j + 1]
            far_one = tile[k + far_j : k + far_j + 1]
            edge_one = sm_x[pl.ds(at(first + j, edge), 1), :]
            yy[side, pl.ds(8 + first + j, 1), :] = (far_one + edge_one) + (near_one + near_one)

    def smooth_y(plane):
        middle = sm_x[pl.ds(at(plane, 0), rows), :]
        ends = sm_x[pl.ds(at(plane, -1), rows), :] + sm_x[pl.ds(at(plane, 1), rows), :]
        return ends + (middle + middle)

    older, old = smooth_y(-2), smooth_y(-1)
    for plane in range(-1, planes + 1):
        new = smooth_y(plane + 1)
        sm[pl.ds((plane + 1) * rows, rows), :] = (older + new) + (old + old)
        older, old = old, new

    def group_copy(axis, src, dst, send, recv, step, total, me):
        other = lax.rem(me + step, total)
        device = (other, lm) if axis == "depth" else (dm, other)
        return pltpu.make_async_remote_copy(
            src_ref=src.at[other],
            dst_ref=dst.at[me],
            send_sem=send.at[step],
            recv_sem=recv.at[total - step],
            device_id=device,
            device_id_type=MESH,
        )

    def exchange(axis, src, dst, send, recv, total, me):
        for step in range(1, total):
            group_copy(axis, src, dst, send, recv, step, total, me).start()
        dst[me] = src[me]

    def finish(axis, src, dst, send, recv, total, me):
        for step in range(1, total):
            copy = group_copy(axis, src, dst, send, recv, step, total, me)
            copy.wait_send()
            copy.wait_recv()

    def row_smoothed(row):
        if 0 <= row < rows:
            return sm[pl.ds(rows + row, planes, stride=rows), :]
        side = 0 if row < 0 else 1
        middle = yy[side, pl.ds(8, planes), :]
        ends = yy[side, pl.ds(7, planes), :] + yy[side, pl.ds(9, planes), :]
        return ends + (middle + middle)

    y_couples = {}

    def y_couple(row):
        if row not in y_couples:
            value = coupling(row_smoothed(row + 1) - row_smoothed(row))
            if row == -1:
                value = value * jnp.where(has[(0, -1)], 1.0, 0.0)
            if row == rows - 1:
                value = value * jnp.where(has[(0, 1)], 1.0, 0.0)
            y_couples[row] = value
        return y_couples[row]

    def y_keep(row, onward, back, part):
        yw[row] = onward
        yv[row] = back
        yg[row] = part

    y_chunk = planes // lat_total
    results = eliminate(
        0, rows, y_couple, lambda row: vol[pl.ds(row, planes, stride=rows), :], y_keep
    )
    for q, value in enumerate(results):
        for k in range(lat_total):
            ysnd[k, pl.ds(q * y_chunk, y_chunk), :] = value[k * y_chunk : (k + 1) * y_chunk]
    exchange("lat", ysnd, yrcv, ys_send, ys_recv, lat_total, lm)

    z_couples = {}

    def z_couple(plane):
        if plane not in z_couples:
            diff = sm[pl.ds((plane + 2) * rows, rows), :] - sm[pl.ds((plane + 1) * rows, rows), :]
            value = coupling(diff)
            if plane == -1:
                value = value * jnp.where(has[(-1, 0)], 1.0, 0.0)
            if plane == planes - 1:
                value = value * jnp.where(has[(1, 0)], 1.0, 0.0)
            z_couples[plane] = value
        return z_couples[plane]

    def z_keep(plane, onward, back, part):
        zw[plane] = onward
        zv[plane] = back
        zg[plane] = part

    z_chunk = rows // depth_total
    results = eliminate(
        0, planes, z_couple, lambda plane: vol[pl.ds(plane * rows, rows), :], z_keep
    )
    for q, value in enumerate(results):
        for k in range(depth_total):
            zsnd[k, pl.ds(q * z_chunk, z_chunk), :] = value[k * z_chunk : (k + 1) * z_chunk]
    exchange("depth", zsnd, zrcv, zs_send, zs_recv, depth_total, dm)

    group = 4 * rows

    def solve_x(step, carry):
        start = pl.multiple_of(step * group, group)
        smoothed = sm[pl.ds(rows + start, group), :]
        src = vol[pl.ds(start, group), :]
        width = src.shape[1]
        lane = lax.broadcasted_iota(jnp.int32, src.shape, 1)
        couple = jnp.where(
            lane == width - 1, 0.0, coupling(pltpu.roll(smoothed, width - 1, 1) - smoothed)
        )
        diag = 1.0 + couple + pltpu.roll(couple, 1, 1)
        offset = 1
        while offset < width:
            inverse = recip(diag)
            scaled = couple * inverse
            after = couple * pltpu.roll(inverse, width - offset, 1)
            new_diag = diag - pltpu.roll(couple * scaled, offset, 1) - couple * after
            src = (
                src
                + pltpu.roll(scaled * src, offset, 1)
                + couple * pltpu.roll(inverse * src, width - offset, 1)
            )
            if 2 * offset < width:
                couple = couple * pltpu.roll(scaled, width - offset, 1)
            diag = new_diag
            offset = offset * 2
        out[pl.ds(start, group), :] = src * recip(diag)
        return carry

    x_steps = planes * rows // group
    lax.fori_loop(0, x_steps // 2, solve_x, 0)

    def reduce_and_return(axis, snd, rcv, ret, fin, sems, total, me, chunk):
        finish(axis, snd, rcv, sems[0], sems[1], total, me)
        values = solve_reduced(
            total, chunk, lambda k, q: rcv[k, pl.ds(q * chunk, chunk), :]
        )
        for k in range(total):
            ret[k, pl.ds(0, chunk), :] = values[k - 1] if k else jnp.zeros_like(values[0])
            ret[k, pl.ds(chunk, chunk), :] = values[k]
        exchange(axis, ret, fin, sems[2], sems[3], total, me)

    y_sems = (ys_send, ys_recv, yr_send, yr_recv)
    z_sems = (zs_send, zs_recv, zr_send, zr_recv)
    reduce_and_return("lat", ysnd, yrcv, yret, yfin, y_sems, lat_total, lm, y_chunk)
    reduce_and_return("depth", zsnd, zrcv, zret, zfin, z_sems, depth_total, dm, z_chunk)
    lax.fori_loop(x_steps // 2, x_steps, solve_x, 0)

    def gather(fin, sep, total, chunk):
        for k in range(total):
            for q in range(2):
                sep[q, pl.ds(k * chunk, chunk), :] = fin[k, pl.ds(q * chunk, chunk), :]

    finish("depth", zret, zfin, zr_send, zr_recv, depth_total, dm)
    gather(zfin, zsep, depth_total, z_chunk)

    def z_emit(plane, value):
        where = pl.ds(plane * rows, rows)
        out[where, :] = out[where, :] + value

    substitute(
        0, planes, zsep[0], zsep[1], lambda p: (zw[p], zv[p], zg[p]), z_emit
    )
    finish("lat", yret, yfin, yr_send, yr_recv, lat_total, lm)
    gather(yfin, ysep, lat_total, y_chunk)

    def y_emit(row, value):
        where = pl.ds(row, planes, stride=rows)
        out[where, :] = (out[where, :] + value) * (1.0 / 3.0)

    substitute(0, rows, ysep[0], ysep[1], lambda r: (yw[r], yv[r], yg[r]), y_emit)


def shards(depth_total, lat_total, volume):
    planes, rows, columns = volume.shape
    y_chunk = planes // lat_total
    z_chunk = rows // depth_total
    f32 = jnp.float32

    def vmem(*shape):
        return pltpu.VMEM(shape + (columns,), f32)

    def dma(count):
        return pltpu.SemaphoreType.DMA((count,))

    cells = planes * rows
    out = pl.pallas_call(
        functools.partial(kernel, depth_total, lat_total, planes, rows),
        out_shape=jax.ShapeDtypeStruct((cells, columns), f32),
        in_specs=[pl.BlockSpec(memory_space=pltpu.VMEM)],
        out_specs=pl.BlockSpec(memory_space=pltpu.VMEM),
        scratch_shapes=[
            vmem(2, 2 * planes),
            vmem(2, 2 * planes),
            vmem(2, 2 * rows),
            vmem(2, 2, 8),
            vmem(BASE + PITCH * (planes + 4)),
            vmem((planes + 2) * rows),
            vmem(2, planes + 16),
            vmem(planes, rows),
            vmem(planes, rows),
            vmem(planes, rows),
            vmem(rows, planes),
            vmem(rows, planes),
            vmem(rows, planes),
            vmem(depth_total, round_up(5 * z_chunk, 8)),
            vmem(depth_total, round_up(5 * z_chunk, 8)),
            vmem(depth_total, round_up(2 * z_chunk, 8)),
            vmem(depth_total, round_up(2 * z_chunk, 8)),
            vmem(2, rows),
            vmem(lat_total, round_up(5 * y_chunk, 8)),
            vmem(lat_total, round_up(5 * y_chunk, 8)),
            vmem(lat_total, round_up(2 * y_chunk, 8)),
            vmem(lat_total, round_up(2 * y_chunk, 8)),
            vmem(2, planes),
            dma(8),
            dma(8),
            dma(depth_total),
            dma(depth_total),
            dma(depth_total),
            dma(depth_total),
            dma(lat_total),
            dma(lat_total),
            dma(lat_total),
            dma(lat_total),
        ],
        compiler_params=pltpu.CompilerParams(
            collective_id=0, has_side_effects=True, vmem_limit_bytes=24 * 1024 * 1024
        ),
        cost_estimate=pl.CostEstimate(
            flops=400 * cells * columns, bytes_accessed=8 * cells * columns, transcendentals=0
        ),
    )(volume.reshape(cells, columns))
    return out.reshape(volume.shape)


def solution(mesh):
    placed = (P("depth", "lat", None),)
    return jax.shard_map(
        functools.partial(shards, mesh.shape["depth"], mesh.shape["lat"]),
        mesh=mesh,
        in_specs=placed,
        out_specs=P("depth", "lat", None),
        check_vma=False,
    )
```

```python
import functools

import jax
import jax.numpy as jnp
from jax import lax
from jax.experimental import pallas as pl
from jax.experimental.pallas import tpu as pltpu
from jax.sharding import PartitionSpec as P

TAU = 300.0
LAMBDA = 0.5
MESH = pl.DeviceIdType.MESH
SCALE = (64.0 * LAMBDA) ** 2
LEAF = 8


def round_up(value, to):
    return (value + to - 1) // to * to


def recip(value):
    guess = pl.reciprocal(value, approx=True)
    return guess * (2.0 - value * guess)


def coupling(diff):
    return (3.0 * TAU * SCALE) * recip(SCALE + diff * diff)


def smooth_x(field):
    lane = lax.broadcasted_iota(jnp.int32, field.shape, 1)
    width = field.shape[1]
    before = jnp.where(lane == 0, 0.0, pltpu.roll(field, 1, 1))
    after = jnp.where(lane == width - 1, 0.0, pltpu.roll(field, width - 1, 1))
    return (before + after) + (field + field)


def eliminate(lo, hi, couple, source, keep):
    starts = list(range(lo, hi, LEAF))
    state = []
    for start in starts:
        state.append([1.0, couple(start - 1), source(start), None, None])
    for step in range(LEAF - 1):
        for part, start in enumerate(starts):
            excess, fill, src, excess_low, src_low = state[part]
            cell = start + step
            after = couple(cell)
            inverse = recip(excess + fill + after)
            onward = after * inverse
            back = fill * inverse
            keep(cell, onward, back, src * inverse)
            add_excess = back * excess
            add_src = back * src
            state[part] = [
                1.0 + onward * excess,
                onward * fill,
                source(cell + 1) + onward * src,
                add_excess if excess_low is None else excess_low + add_excess,
                add_src if src_low is None else src_low + add_src,
            ]
    blocks = [(start, start + LEAF, part) for start, part in zip(starts, state)]
    while len(blocks) > 1:
        merged = []
        for first, second in zip(blocks[::2], blocks[1::2]):
            e1, f1, s1, el1, sl1 = first[2]
            e2, f2, s2, el2, sl2 = second[2]
            excess = e1 + el2
            src = s1 + sl2
            inverse = recip(excess + f1 + f2)
            onward = f2 * inverse
            back = f1 * inverse
            keep(first[1] - 1, onward, back, src * inverse)
            merged.append(
                (
                    first[0],
                    second[1],
                    [
                        e2 + onward * excess,
                        onward * f1,
                        s2 + onward * src,
                        el1 + back * excess,
                        sl1 + back * src,
                    ],
                )
            )
        blocks = merged
    e, f, s, el, sl = blocks[0][2]
    return el, sl, f, e, s


def substitute(lo, hi, before, last, load, emit):
    known = {lo - 1: before, hi - 1: last}
    emit(hi - 1, last)
    size = hi - lo
    while size > LEAF:
        for start in range(lo, hi, size):
            middle = start + size // 2 - 1
            onward, back, part = load(middle)
            value = part + back * known[start - 1] + onward * known[start + size - 1]
            known[middle] = value
            emit(middle, value)
        size = size // 2
    current = {start: known[start + LEAF - 1] for start in range(lo, hi, LEAF)}
    for step in range(LEAF - 2, -1, -1):
        for start in range(lo, hi, LEAF):
            onward, back, part = load(start + step)
            value = part + back * known[start - 1] + onward * current[start]
            current[start] = value
            emit(start + step, value)


def solve_reduced(count, rows, got):
    excess = got(0, 3)
    src = got(0, 4)
    onwards, parts = [], []
    for k in range(count - 1):
        couple = got(k + 1, 2)
        excess = excess + got(k + 1, 0)
        src = src + got(k + 1, 1)
        inverse = recip(excess + couple)
        onward = couple * inverse
        onwards.append(onward)
        parts.append(src * inverse)
        excess = got(k + 1, 3) + onward * excess
        src = got(k + 1, 4) + onward * src
    value = src * recip(excess)
    values = [value]
    for k in range(count - 2, -1, -1):
        value = parts[k] + onwards[k] * value
        values.append(value)
    return values[::-1]


def kernel(
    depth_total, lat_total, planes, rows,
    source, out,
    vol, pack, yh, zh, cn, sm_x, sm, yy, nn,
    vol_t, sm_t, x_out, xw, xv, xg, zw, zv, zg, yw, yv, yg,
    zsnd, zrcv, zret, zfin, zsep, ysnd, yrcv, yret, yfin, ysep,
    load_sem, halo_send, halo_recv, zs_send, zs_recv, zr_send, zr_recv,
    ys_send, ys_recv, yr_send, yr_recv,
):
    dm = lax.axis_index("depth")
    lm = lax.axis_index("lat")
    has = {
        (-1, 0): dm > 0,
        (1, 0): dm < depth_total - 1,
        (0, -1): lm > 0,
        (0, 1): lm < lat_total - 1,
    }
    for dz in (-1, 1):
        for dy in (-1, 1):
            has[(dz, dy)] = jnp.logical_and(has[(dz, 0)], has[(0, dy)])
    corners = [(dz, dy) for dz in (-1, 1) for dy in (-1, 1)]

    load = pltpu.make_async_copy(source, vol, load_sem)
    load.start()

    barrier = pltpu.get_barrier_semaphore()
    for step in range(1, lat_total):
        pl.semaphore_signal(
            barrier, inc=1, device_id=(dm, lax.rem(lm + step, lat_total)), device_id_type=MESH
        )
    for step in range(1, depth_total):
        pl.semaphore_signal(
            barrier, inc=1, device_id=(lax.rem(dm + step, depth_total), lm), device_id_type=MESH
        )
    expected = jnp.int32(lat_total + depth_total - 2)
    for dz, dy in corners:
        expected = expected + has[(dz, dy)].astype(jnp.int32)

        @pl.when(has[(dz, dy)])
        def _():
            pl.semaphore_signal(
                barrier, inc=1, device_id=(dm + dz, lm + dy), device_id_type=MESH
            )

    load.wait()
    for side, first in ((0, 0), (1, rows - 2)):
        for j in range(2):
            pack[side, pl.ds(j, planes, stride=2), :] = vol[
                pl.ds(first + j, planes, stride=rows), :
            ]
    pl.semaphore_wait(barrier, expected)

    def halo_copy(index, way):
        dz, dy = way
        zi, yi = (dz + 1) // 2, (dy + 1) // 2
        if dy == 0:
            src = vol.at[pl.ds(0 if dz < 0 else (planes - 2) * rows, 2 * rows)]
            dst = zh.at[1 - zi]
        elif dz == 0:
            src = pack.at[yi]
            dst = yh.at[1 - yi]
        else:
            src = pack.at[yi, pl.ds(0 if dz < 0 else 2 * planes - 8, 8)]
            dst = cn.at[1 - zi, 1 - yi]
        return pltpu.make_async_remote_copy(
            src_ref=src,
            dst_ref=dst,
            send_sem=halo_send.at[index],
            recv_sem=halo_recv.at[index],
            device_id=(dm + dz, lm + dy),
            device_id_type=MESH,
        )

    ways = [(0, -1), (0, 1), (-1, 0), (1, 0)] + corners
    opposite = {way: ways.index((-way[0], -way[1])) for way in ways}
    for index, way in enumerate(ways):

        @pl.when(has[way])
        def _():
            halo_copy(index, way).start()

    def smooth_y(field):
        row = lax.broadcasted_iota(jnp.int32, field.shape, 0)
        before = jnp.where(row == 0, 0.0, pltpu.roll(field, 1, 0))
        after = jnp.where(row == rows - 1, 0.0, pltpu.roll(field, rows - 1, 0))
        return (before + after) + (field + field)

    def plane_at(plane):
        return pl.ds((plane + 1) * rows, rows)

    older = old = None
    for plane in range(planes + 1):
        new = None
        if plane < planes:
            where = pl.ds(plane * rows, rows)
            along_x = smooth_x(vol[where, :])
            sm_x[where, :] = along_x
            new = smooth_y(along_x)
            if plane in (0, planes - 1):
                sm[plane_at(-1 if plane == 0 else planes), :] = new
        if old is not None:
            total = old + old
            total = total if older is None else total + older
            sm[plane_at(plane - 1), :] = total if new is None else total + new
        older, old = old, new
    tile = vol.shape[1]
    blocks = planes * rows // tile
    for block in range(blocks):
        where = pl.ds(block * tile, tile)
        vol_t[where, :] = vol[where, :].T

    for index, way in enumerate(ways):
        back = opposite[way]

        @pl.when(has[way])
        def _():
            halo_copy(index, way).wait_send()
            halo_copy(back, ways[back]).wait_recv()

        @pl.when(jnp.logical_not(has[way]))
        def _():
            dz, dy = way
            zi, yi = (dz + 1) // 2, (dy + 1) // 2
            if dy == 0:
                zh[zi] = jnp.zeros(zh.shape[1:], jnp.float32)
            elif dz == 0:
                yh[yi] = jnp.zeros(yh.shape[1:], jnp.float32)
            else:
                cn[zi, yi] = jnp.zeros(cn.shape[2:], jnp.float32)

    outer_x = {}
    for side, near, far, inner in ((0, -1, -2, 0), (1, planes, planes + 1, planes - 1)):
        near_j, far_j = (1, 0) if side == 0 else (0, 1)
        near_x = smooth_x(zh[side, pl.ds(near_j * rows, rows), :])
        far_x = smooth_x(zh[side, pl.ds(far_j * rows, rows), :])
        outer_x[side] = near_x
        near_y = smooth_y(near_x)
        sm[plane_at(near), :] = sm[plane_at(near), :] + smooth_y(far_x) + (near_y + near_y)
        sm[plane_at(inner), :] = sm[plane_at(inner), :] + near_y
    for side, edge in ((0, 0), (1, rows - 1)):
        near_j, far_j = (1, 0) if side == 0 else (0, 1)
        near_row = smooth_x(yh[side, pl.ds(near_j, planes, stride=2), :])
        far_row = smooth_x(yh[side, pl.ds(far_j, planes, stride=2), :])
        edge_row = sm_x[pl.ds(edge, planes, stride=rows), :]
        nn[side, pl.ds(8, planes), :] = near_row
        yy[side, pl.ds(8, planes), :] = (far_row + edge_row) + (near_row + near_row)
        for zside, plane, k_one, k_two in ((0, -1, 6, 4), (1, planes, 0, 2)):
            tile_x = smooth_x(cn[zside, side])
            near_one = tile_x[k_one + near_j : k_one + near_j + 1]
            near_two = tile_x[k_two + near_j : k_two + near_j + 1]
            far_one = tile_x[k_one + far_j : k_one + far_j + 1]
            edge_one = outer_x[zside][edge : edge + 1]
            nn[side, pl.ds(8 + plane, 1), :] = near_one
            yy[side, pl.ds(8 + plane, 1), :] = (far_one + edge_one) + (near_one + near_one)
            inner = 0 if zside == 0 else planes - 1
            where = pl.ds((plane + 1) * rows + edge, 1)
            sm[where, :] = (
                sm[where, :] + near_row[inner : inner + 1] + near_two + (near_one + near_one)
            )
        where = pl.ds(rows + edge, planes, stride=rows)
        ends = nn[side, pl.ds(7, planes), :] + nn[side, pl.ds(9, planes), :]
        sm[where, :] = sm[where, :] + ends + (near_row + near_row)

    def group_copy(axis, src, dst, send, recv, step, total, me):
        other = lax.rem(me + step, total)
        device = (other, lm) if axis == "depth" else (dm, other)
        return pltpu.make_async_remote_copy(
            src_ref=src.at[other],
            dst_ref=dst.at[me],
            send_sem=send.at[step],
            recv_sem=recv.at[total - step],
            device_id=device,
            device_id_type=MESH,
        )

    def exchange(axis, src, dst, send, recv, total, me):
        for step in range(1, total):
            group_copy(axis, src, dst, send, recv, step, total, me).start()
        dst[me] = src[me]

    def finish(axis, src, dst, send, recv, total, me):
        for step in range(1, total):
            copy = group_copy(axis, src, dst, send, recv, step, total, me)
            copy.wait_send()
            copy.wait_recv()

    def row_smoothed(row):
        if 0 <= row < rows:
            return sm[pl.ds(rows + row, planes, stride=rows), :]
        side = 0 if row < 0 else 1
        middle = yy[side, pl.ds(8, planes), :]
        ends = yy[side, pl.ds(7, planes), :] + yy[side, pl.ds(9, planes), :]
        return ends + (middle + middle)

    y_couples = {}

    def y_couple(row):
        if row not in y_couples:
            value = coupling(row_smoothed(row + 1) - row_smoothed(row))
            if row == -1:
                value = value * jnp.where(has[(0, -1)], 1.0, 0.0)
            if row == rows - 1:
                value = value * jnp.where(has[(0, 1)], 1.0, 0.0)
            y_couples[row] = value
        return y_couples[row]

    def y_keep(row, onward, back, part):
        yw[row] = onward
        yv[row] = back
        yg[row] = part

    y_chunk = planes // lat_total
    results = eliminate(
        0, rows, y_couple, lambda row: vol[pl.ds(row, planes, stride=rows), :], y_keep
    )
    for q, value in enumerate(results):
        for k in range(lat_total):
            ysnd[k, pl.ds(q * y_chunk, y_chunk), :] = value[k * y_chunk : (k + 1) * y_chunk]
    exchange("lat", ysnd, yrcv, ys_send, ys_recv, lat_total, lm)

    z_couples = {}

    def z_couple(plane):
        if plane not in z_couples:
            diff = sm[pl.ds((plane + 2) * rows, rows), :] - sm[pl.ds((plane + 1) * rows, rows), :]
            value = coupling(diff)
            if plane == -1:
                value = value * jnp.where(has[(-1, 0)], 1.0, 0.0)
            if plane == planes - 1:
                value = value * jnp.where(has[(1, 0)], 1.0, 0.0)
            z_couples[plane] = value
        return z_couples[plane]

    def z_keep(plane, onward, back, part):
        zw[plane] = onward
        zv[plane] = back
        zg[plane] = part

    z_chunk = rows // depth_total
    results = eliminate(
        0, planes, z_couple, lambda plane: vol[pl.ds(plane * rows, rows), :], z_keep
    )
    for q, value in enumerate(results):
        for k in range(depth_total):
            zsnd[k, pl.ds(q * z_chunk, z_chunk), :] = value[k * z_chunk : (k + 1) * z_chunk]
    exchange("depth", zsnd, zrcv, zs_send, zs_recv, depth_total, dm)

    for block in range(blocks):
        where = pl.ds(block * tile, tile)
        sm_t[where, :] = sm[pl.ds(rows + block * tile, tile), :].T
    cells = tile // 8
    spread = blocks * 8

    def x_at(cell):
        return pl.ds(cell, spread, stride=cells)

    def turn(field, by):
        return pltpu.roll(field.reshape(blocks, 8, tile), by, 1).reshape(spread, tile)

    x_couples = {}

    def x_couple(cell):
        if cell not in x_couples:
            if cell == -1:
                value = turn(x_couple(cells - 1), 1)
            elif cell == cells - 1:
                sub = lax.rem(lax.broadcasted_iota(jnp.int32, (spread, tile), 0), 8)
                diff = turn(sm_t[x_at(0), :], 7) - sm_t[x_at(cell), :]
                value = jnp.where(sub == 7, 0.0, coupling(diff))
            else:
                value = coupling(sm_t[x_at(cell + 1), :] - sm_t[x_at(cell), :])
            x_couples[cell] = value
        return x_couples[cell]

    def x_keep(cell, onward, back, part):
        xw[cell] = onward
        xv[cell] = back
        xg[cell] = part

    excess_low, src_low, couple, excess, src = eliminate(
        0, cells, x_couple, lambda cell: vol_t[x_at(cell), :], x_keep
    )
    diag = excess + turn(excess_low, 7) + couple
    src = src + turn(src_low, 7)
    couple = turn(couple, 7)
    diag = diag + couple
    offset = 1
    while offset < 8:
        inverse = recip(diag)
        scaled = couple * inverse
        after = couple * turn(inverse, 8 - offset)
        new_diag = diag - turn(couple * scaled, offset) - couple * after
        src = src + turn(scaled * src, offset) + couple * turn(inverse * src, 8 - offset)
        if 2 * offset < 8:
            couple = couple * turn(scaled, 8 - offset)
        diag = new_diag
        offset = offset * 2
    last = src * recip(diag)

    def x_emit(cell, value):
        x_out[x_at(cell), :] = value

    substitute(0, cells, turn(last, 1), last, lambda c: (xw[c], xv[c], xg[c]), x_emit)
    for block in range(blocks):
        where = pl.ds(block * tile, tile)
        out[where, :] = x_out[where, :].T

    def reduce_and_return(axis, snd, rcv, ret, fin, sems, total, me, chunk):
        finish(axis, snd, rcv, sems[0], sems[1], total, me)
        values = solve_reduced(
            total, chunk, lambda k, q: rcv[k, pl.ds(q * chunk, chunk), :]
        )
        for k in range(total):
            ret[k, pl.ds(0, chunk), :] = values[k - 1] if k else jnp.zeros_like(values[0])
            ret[k, pl.ds(chunk, chunk), :] = values[k]
        exchange(axis, ret, fin, sems[2], sems[3], total, me)

    y_sems = (ys_send, ys_recv, yr_send, yr_recv)
    z_sems = (zs_send, zs_recv, zr_send, zr_recv)
    reduce_and_return("lat", ysnd, yrcv, yret, yfin, y_sems, lat_total, lm, y_chunk)
    reduce_and_return("depth", zsnd, zrcv, zret, zfin, z_sems, depth_total, dm, z_chunk)

    def gather(fin, sep, total, chunk):
        for k in range(total):
            for q in range(2):
                sep[q, pl.ds(k * chunk, chunk), :] = fin[k, pl.ds(q * chunk, chunk), :]

    finish("depth", zret, zfin, zr_send, zr_recv, depth_total, dm)
    gather(zfin, zsep, depth_total, z_chunk)

    def z_emit(plane, value):
        where = pl.ds(plane * rows, rows)
        out[where, :] = out[where, :] + value

    substitute(
        0, planes, zsep[0], zsep[1], lambda p: (zw[p], zv[p], zg[p]), z_emit
    )
    finish("lat", yret, yfin, yr_send, yr_recv, lat_total, lm)
    gather(yfin, ysep, lat_total, y_chunk)

    def y_emit(row, value):
        where = pl.ds(row, planes, stride=rows)
        out[where, :] = (out[where, :] + value) * (1.0 / 3.0)

    substitute(0, rows, ysep[0], ysep[1], lambda r: (yw[r], yv[r], yg[r]), y_emit)


def shards(depth_total, lat_total, volume):
    planes, rows, columns = volume.shape
    y_chunk = planes // lat_total
    z_chunk = rows // depth_total
    f32 = jnp.float32

    def vmem(*shape):
        return pltpu.VMEM(shape + (columns,), f32)

    def dma(count):
        return pltpu.SemaphoreType.DMA((count,))

    cells = planes * rows
    out = pl.pallas_call(
        functools.partial(kernel, depth_total, lat_total, planes, rows),
        out_shape=jax.ShapeDtypeStruct((cells, columns), f32),
        in_specs=[pl.BlockSpec(memory_space=pltpu.HBM)],
        out_specs=pl.BlockSpec(memory_space=pltpu.VMEM),
        scratch_shapes=[
            vmem(cells),
            vmem(2, 2 * planes),
            vmem(2, 2 * planes),
            vmem(2, 2 * rows),
            vmem(2, 2, 8),
            vmem(cells),
            vmem((planes + 2) * rows),
            vmem(2, planes + 16),
            vmem(2, planes + 16),
            vmem(cells),
            vmem(cells),
            vmem(cells),
            vmem(columns // 8, cells * 8 // columns),
            vmem(columns // 8, cells * 8 // columns),
            vmem(columns // 8, cells * 8 // columns),
            vmem(planes, rows),
            vmem(planes, rows),
            vmem(planes, rows),
            vmem(rows, planes),
            vmem(rows, planes),
            vmem(rows, planes),
            vmem(depth_total, round_up(5 * z_chunk, 8)),
            vmem(depth_total, round_up(5 * z_chunk, 8)),
            vmem(depth_total, round_up(2 * z_chunk, 8)),
            vmem(depth_total, round_up(2 * z_chunk, 8)),
            vmem(2, rows),
            vmem(lat_total, round_up(5 * y_chunk, 8)),
            vmem(lat_total, round_up(5 * y_chunk, 8)),
            vmem(lat_total, round_up(2 * y_chunk, 8)),
            vmem(lat_total, round_up(2 * y_chunk, 8)),
            vmem(2, planes),
            pltpu.SemaphoreType.DMA,
            dma(8),
            dma(8),
            dma(depth_total),
            dma(depth_total),
            dma(depth_total),
            dma(depth_total),
            dma(lat_total),
            dma(lat_total),
            dma(lat_total),
            dma(lat_total),
        ],
        compiler_params=pltpu.CompilerParams(
            collective_id=0, has_side_effects=True, vmem_limit_bytes=24 * 1024 * 1024
        ),
        cost_estimate=pl.CostEstimate(
            flops=400 * cells * columns, bytes_accessed=8 * cells * columns, transcendentals=0
        ),
    )(volume.reshape(cells, columns))
    return out.reshape(volume.shape)


def solution(mesh):
    placed = (P("depth", "lat", None),)
    return jax.shard_map(
        functools.partial(shards, mesh.shape["depth"], mesh.shape["lat"]),
        mesh=mesh,
        in_specs=placed,
        out_specs=P("depth", "lat", None),
        check_vma=False,
    )
```

```python
import functools

import jax
import jax.numpy as jnp
from jax import lax
from jax.experimental import pallas as pl
from jax.experimental.pallas import tpu as pltpu
from jax.sharding import PartitionSpec as P

TAU = 300.0
LAMBDA = 0.5
MESH = pl.DeviceIdType.MESH
SCALE = (64.0 * LAMBDA) ** 2
LEAF = 8


def recip(value):
    guess = pl.reciprocal(value, approx=True)
    return guess * (2.0 - value * guess)


def coupling(diff):
    return (3.0 * TAU * SCALE) * recip(SCALE + diff * diff)


def smooth_x(field):
    lane = lax.broadcasted_iota(jnp.int32, field.shape, 1)
    width = field.shape[1]
    before = jnp.where(lane == 0, 0.0, pltpu.roll(field, 1, 1))
    after = jnp.where(lane == width - 1, 0.0, pltpu.roll(field, width - 1, 1))
    return (before + after) + (field + field)


def eliminate(lo, hi, couple, source, keep):
    starts = list(range(lo, hi, LEAF))
    state = []
    for start in starts:
        state.append([1.0, couple(start - 1), source(start), None, None])
    for step in range(LEAF - 1):
        for part, start in enumerate(starts):
            excess, fill, src, excess_low, src_low = state[part]
            cell = start + step
            after = couple(cell)
            inverse = recip(excess + fill + after)
            onward = after * inverse
            back = fill * inverse
            keep(cell, onward, back, src * inverse)
            add_excess = back * excess
            add_src = back * src
            state[part] = [
                1.0 + onward * excess,
                onward * fill,
                source(cell + 1) + onward * src,
                add_excess if excess_low is None else excess_low + add_excess,
                add_src if src_low is None else src_low + add_src,
            ]
    blocks = [(start, start + LEAF, part) for start, part in zip(starts, state)]
    while len(blocks) > 1:
        merged = []
        for first, second in zip(blocks[::2], blocks[1::2]):
            e1, f1, s1, el1, sl1 = first[2]
            e2, f2, s2, el2, sl2 = second[2]
            excess = e1 + el2
            src = s1 + sl2
            inverse = recip(excess + f1 + f2)
            onward = f2 * inverse
            back = f1 * inverse
            keep(first[1] - 1, onward, back, src * inverse)
            merged.append(
                (
                    first[0],
                    second[1],
                    [
                        e2 + onward * excess,
                        onward * f1,
                        s2 + onward * src,
                        el1 + back * excess,
                        sl1 + back * src,
                    ],
                )
            )
        blocks = merged
    e, f, s, el, sl = blocks[0][2]
    return el, sl, f, e, s


def substitute(lo, hi, before, last, load, emit):
    known = {lo - 1: before, hi - 1: last}
    emit(hi - 1, last)
    size = hi - lo
    while size > LEAF:
        for start in range(lo, hi, size):
            middle = start + size // 2 - 1
            onward, back, part = load(middle)
            value = part + back * known[start - 1] + onward * known[start + size - 1]
            known[middle] = value
            emit(middle, value)
        size = size // 2
    current = {start: known[start + LEAF - 1] for start in range(lo, hi, LEAF)}
    for step in range(LEAF - 2, -1, -1):
        for start in range(lo, hi, LEAF):
            onward, back, part = load(start + step)
            value = part + back * known[start - 1] + onward * current[start]
            current[start] = value
            emit(start + step, value)


def solve_reduced(count, rows, got):
    excess = got(0, 3)
    src = got(0, 4)
    onwards, parts = [], []
    for k in range(count - 1):
        couple = got(k + 1, 2)
        excess = excess + got(k + 1, 0)
        src = src + got(k + 1, 1)
        inverse = recip(excess + couple)
        onward = couple * inverse
        onwards.append(onward)
        parts.append(src * inverse)
        excess = got(k + 1, 3) + onward * excess
        src = got(k + 1, 4) + onward * src
    value = src * recip(excess)
    values = [value]
    for k in range(count - 2, -1, -1):
        value = parts[k] + onwards[k] * value
        values.append(value)
    return values[::-1]


def kernel(
    depth_total, lat_total, planes, rows,
    source, out,
    vol, pack, yh, zh, cn, sm_x, sm, yy, nn,
    vol_t, sm_t, x_out, xw, xv, xg, zw, zv, zg, yw, yv, yg,
    zsnd, zrcv, zret, zfin, zsep, ysnd, yrcv, yret, yfin, ysep,
    load_sem, halo_send, halo_recv, zs_send, zs_recv, zr_send, zr_recv,
    ys_send, ys_recv, yr_send, yr_recv,
):
    dm = lax.axis_index("depth")
    lm = lax.axis_index("lat")
    has = {
        (-1, 0): dm > 0,
        (1, 0): dm < depth_total - 1,
        (0, -1): lm > 0,
        (0, 1): lm < lat_total - 1,
    }
    for dz in (-1, 1):
        for dy in (-1, 1):
            has[(dz, dy)] = jnp.logical_and(has[(dz, 0)], has[(0, dy)])
    corners = [(dz, dy) for dz in (-1, 1) for dy in (-1, 1)]

    load = pltpu.make_async_copy(source, vol, load_sem)
    load.start()

    barrier = pltpu.get_barrier_semaphore()
    for step in range(1, lat_total):
        pl.semaphore_signal(
            barrier, inc=1, device_id=(dm, lax.rem(lm + step, lat_total)), device_id_type=MESH
        )
    for step in range(1, depth_total):
        pl.semaphore_signal(
            barrier, inc=1, device_id=(lax.rem(dm + step, depth_total), lm), device_id_type=MESH
        )
    expected = jnp.int32(lat_total + depth_total - 2)
    for dz, dy in corners:
        expected = expected + has[(dz, dy)].astype(jnp.int32)

        @pl.when(has[(dz, dy)])
        def _():
            pl.semaphore_signal(
                barrier, inc=1, device_id=(dm + dz, lm + dy), device_id_type=MESH
            )

    load.wait()
    for side, first in ((0, 0), (1, rows - 2)):
        for j in range(2):
            pack[side, pl.ds(j, planes, stride=2), :] = vol[
                pl.ds(first + j, planes, stride=rows), :
            ]
    pl.semaphore_wait(barrier, expected)

    def halo_copy(index, way):
        dz, dy = way
        zi, yi = (dz + 1) // 2, (dy + 1) // 2
        if dy == 0:
            src = vol.at[pl.ds(0 if dz < 0 else (planes - 2) * rows, 2 * rows)]
            dst = zh.at[1 - zi]
        elif dz == 0:
            src = pack.at[yi]
            dst = yh.at[1 - yi]
        else:
            src = pack.at[yi, pl.ds(0 if dz < 0 else 2 * planes - 8, 8)]
            dst = cn.at[1 - zi, 1 - yi]
        return pltpu.make_async_remote_copy(
            src_ref=src,
            dst_ref=dst,
            send_sem=halo_send.at[index],
            recv_sem=halo_recv.at[index],
            device_id=(dm + dz, lm + dy),
            device_id_type=MESH,
        )

    ways = [(0, -1), (0, 1), (-1, 0), (1, 0)] + corners
    opposite = {way: ways.index((-way[0], -way[1])) for way in ways}
    for index, way in enumerate(ways):

        @pl.when(has[way])
        def _():
            halo_copy(index, way).start()

    def smooth_y(field):
        row = lax.broadcasted_iota(jnp.int32, field.shape, 0)
        before = jnp.where(row == 0, 0.0, pltpu.roll(field, 1, 0))
        after = jnp.where(row == rows - 1, 0.0, pltpu.roll(field, rows - 1, 0))
        return (before + after) + (field + field)

    def plane_at(plane):
        return pl.ds((plane + 1) * rows, rows)

    older = old = None
    for plane in range(planes + 1):
        new = None
        if plane < planes:
            where = pl.ds(plane * rows, rows)
            along_x = smooth_x(vol[where, :])
            sm_x[where, :] = along_x
            new = smooth_y(along_x)
            if plane in (0, planes - 1):
                sm[plane_at(-1 if plane == 0 else planes), :] = new
        if old is not None:
            total = old + old
            total = total if older is None else total + older
            sm[plane_at(plane - 1), :] = total if new is None else total + new
        older, old = old, new
    tile = vol.shape[1]
    blocks = planes * rows // tile
    for block in range(blocks):
        where = pl.ds(block * tile, tile)
        vol_t[where, :] = vol[where, :].T

    for index, way in enumerate(ways):
        back = opposite[way]

        @pl.when(has[way])
        def _():
            halo_copy(back, ways[back]).wait_recv()

        @pl.when(jnp.logical_not(has[way]))
        def _():
            dz, dy = way
            zi, yi = (dz + 1) // 2, (dy + 1) // 2
            if dy == 0:
                zh[zi] = jnp.zeros(zh.shape[1:], jnp.float32)
            elif dz == 0:
                yh[yi] = jnp.zeros(yh.shape[1:], jnp.float32)
            else:
                cn[zi, yi] = jnp.zeros(cn.shape[2:], jnp.float32)

    outer_x = {}
    for side, near, far, inner in ((0, -1, -2, 0), (1, planes, planes + 1, planes - 1)):
        near_j, far_j = (1, 0) if side == 0 else (0, 1)
        near_x = smooth_x(zh[side, pl.ds(near_j * rows, rows), :])
        far_x = smooth_x(zh[side, pl.ds(far_j * rows, rows), :])
        outer_x[side] = near_x
        near_y = smooth_y(near_x)
        sm[plane_at(near), :] = sm[plane_at(near), :] + smooth_y(far_x) + (near_y + near_y)
        sm[plane_at(inner), :] = sm[plane_at(inner), :] + near_y
    for side, edge in ((0, 0), (1, rows - 1)):
        near_j, far_j = (1, 0) if side == 0 else (0, 1)
        near_row = smooth_x(yh[side, pl.ds(near_j, planes, stride=2), :])
        far_row = smooth_x(yh[side, pl.ds(far_j, planes, stride=2), :])
        edge_row = sm_x[pl.ds(edge, planes, stride=rows), :]
        nn[side, pl.ds(8, planes), :] = near_row
        yy[side, pl.ds(8, planes), :] = (far_row + edge_row) + (near_row + near_row)
        for zside, plane, k_one, k_two in ((0, -1, 6, 4), (1, planes, 0, 2)):
            tile_x = smooth_x(cn[zside, side])
            near_one = tile_x[k_one + near_j : k_one + near_j + 1]
            near_two = tile_x[k_two + near_j : k_two + near_j + 1]
            far_one = tile_x[k_one + far_j : k_one + far_j + 1]
            edge_one = outer_x[zside][edge : edge + 1]
            nn[side, pl.ds(8 + plane, 1), :] = near_one
            yy[side, pl.ds(8 + plane, 1), :] = (far_one + edge_one) + (near_one + near_one)
            inner = 0 if zside == 0 else planes - 1
            where = pl.ds((plane + 1) * rows + edge, 1)
            sm[where, :] = (
                sm[where, :] + near_row[inner : inner + 1] + near_two + (near_one + near_one)
            )
        where = pl.ds(rows + edge, planes, stride=rows)
        ends = nn[side, pl.ds(7, planes), :] + nn[side, pl.ds(9, planes), :]
        sm[where, :] = sm[where, :] + ends + (near_row + near_row)

    def exchange(axis, src, dst, sems, total, me):
        for step in range(1, total):
            other = lax.rem(me + step, total)
            pltpu.make_async_remote_copy(
                src_ref=src.at[other],
                dst_ref=dst.at[me],
                send_sem=sems[0],
                recv_sem=sems[1],
                device_id=(other, lm) if axis == "depth" else (dm, other),
                device_id_type=MESH,
            ).start()
        dst[me] = src[me]

    def wait_all(ref, sem, total):
        some = ref.at[pl.ds(0, total - 1)]
        pltpu.make_async_copy(some, some, sem).wait()

    def row_smoothed(row):
        if 0 <= row < rows:
            return sm[pl.ds(rows + row, planes, stride=rows), :]
        side = 0 if row < 0 else 1
        middle = yy[side, pl.ds(8, planes), :]
        ends = yy[side, pl.ds(7, planes), :] + yy[side, pl.ds(9, planes), :]
        return ends + (middle + middle)

    y_couples = {}

    def y_couple(row):
        if row not in y_couples:
            value = coupling(row_smoothed(row + 1) - row_smoothed(row))
            if row == -1:
                value = value * jnp.where(has[(0, -1)], 1.0, 0.0)
            if row == rows - 1:
                value = value * jnp.where(has[(0, 1)], 1.0, 0.0)
            y_couples[row] = value
        return y_couples[row]

    def y_keep(row, onward, back, part):
        yw[row] = onward
        yv[row] = back
        yg[row] = part

    y_chunk = planes // lat_total
    results = eliminate(
        0, rows, y_couple, lambda row: vol[pl.ds(row, planes, stride=rows), :], y_keep
    )
    for q, value in enumerate(results):
        for k in range(lat_total):
            ysnd[k, pl.ds(q * y_chunk, y_chunk), :] = value[k * y_chunk : (k + 1) * y_chunk]
    exchange("lat", ysnd, yrcv, (ys_send, ys_recv), lat_total, lm)

    z_couples = {}

    def z_couple(plane):
        if plane not in z_couples:
            diff = sm[pl.ds((plane + 2) * rows, rows), :] - sm[pl.ds((plane + 1) * rows, rows), :]
            value = coupling(diff)
            if plane == -1:
                value = value * jnp.where(has[(-1, 0)], 1.0, 0.0)
            if plane == planes - 1:
                value = value * jnp.where(has[(1, 0)], 1.0, 0.0)
            z_couples[plane] = value
        return z_couples[plane]

    def z_keep(plane, onward, back, part):
        zw[plane] = onward
        zv[plane] = back
        zg[plane] = part

    z_chunk = rows // depth_total
    results = eliminate(
        0, planes, z_couple, lambda plane: vol[pl.ds(plane * rows, rows), :], z_keep
    )
    for q, value in enumerate(results):
        for k in range(depth_total):
            zsnd[k, pl.ds(q * z_chunk, z_chunk), :] = value[k * z_chunk : (k + 1) * z_chunk]
    exchange("depth", zsnd, zrcv, (zs_send, zs_recv), depth_total, dm)

    for block in range(blocks):
        where = pl.ds(block * tile, tile)
        sm_t[where, :] = sm[pl.ds(rows + block * tile, tile), :].T
    cells = tile // 8
    spread = blocks * 8

    def x_at(cell):
        return pl.ds(cell, spread, stride=cells)

    def turn(field, by):
        return pltpu.roll(field.reshape(blocks, 8, tile), by, 1).reshape(spread, tile)

    x_couples = {}

    def x_couple(cell):
        if cell not in x_couples:
            if cell == -1:
                value = turn(x_couple(cells - 1), 1)
            elif cell == cells - 1:
                sub = lax.rem(lax.broadcasted_iota(jnp.int32, (spread, tile), 0), 8)
                diff = turn(sm_t[x_at(0), :], 7) - sm_t[x_at(cell), :]
                value = jnp.where(sub == 7, 0.0, coupling(diff))
            else:
                value = coupling(sm_t[x_at(cell + 1), :] - sm_t[x_at(cell), :])
            x_couples[cell] = value
        return x_couples[cell]

    def x_keep(cell, onward, back, part):
        xw[cell] = onward
        xv[cell] = back
        xg[cell] = part

    excess_low, src_low, couple, excess, src = eliminate(
        0, cells, x_couple, lambda cell: vol_t[x_at(cell), :], x_keep
    )
    diag = excess + turn(excess_low, 7) + couple
    src = src + turn(src_low, 7)
    couple = turn(couple, 7)
    diag = diag + couple
    offset = 1
    while offset < 8:
        inverse = recip(diag)
        scaled = couple * inverse
        after = couple * turn(inverse, 8 - offset)
        new_diag = diag - turn(couple * scaled, offset) - couple * after
        src = src + turn(scaled * src, offset) + couple * turn(inverse * src, 8 - offset)
        if 2 * offset < 8:
            couple = couple * turn(scaled, 8 - offset)
        diag = new_diag
        offset = offset * 2
    last = src * recip(diag)

    def x_emit(cell, value):
        x_out[x_at(cell), :] = value

    substitute(0, cells, turn(last, 1), last, lambda c: (xw[c], xv[c], xg[c]), x_emit)
    for block in range(blocks):
        where = pl.ds(block * tile, tile)
        out[where, :] = x_out[where, :].T

    def reduce_and_return(axis, rcv, ret, fin, recv, sems, total, me, chunk):
        wait_all(rcv, recv, total)
        values = solve_reduced(
            total, chunk, lambda k, q: rcv[k, pl.ds(q * chunk, chunk), :]
        )
        for k in range(total):
            ret[k, pl.ds(0, chunk), :] = values[k - 1] if k else jnp.zeros_like(values[0])
            ret[k, pl.ds(chunk, chunk), :] = values[k]
        exchange(axis, ret, fin, sems, total, me)

    y_sems = (yr_send, yr_recv)
    z_sems = (zr_send, zr_recv)
    reduce_and_return("lat", yrcv, yret, yfin, ys_recv, y_sems, lat_total, lm, y_chunk)
    reduce_and_return("depth", zrcv, zret, zfin, zs_recv, z_sems, depth_total, dm, z_chunk)

    def gather(fin, sep, total, chunk):
        for k in range(total):
            for q in range(2):
                sep[q, pl.ds(k * chunk, chunk), :] = fin[k, pl.ds(q * chunk, chunk), :]

    wait_all(zfin, zr_recv, depth_total)
    gather(zfin, zsep, depth_total, z_chunk)

    def z_emit(plane, value):
        where = pl.ds(plane * rows, rows)
        out[where, :] = out[where, :] + value

    substitute(
        0, planes, zsep[0], zsep[1], lambda p: (zw[p], zv[p], zg[p]), z_emit
    )
    wait_all(yfin, yr_recv, lat_total)
    gather(yfin, ysep, lat_total, y_chunk)

    def y_emit(row, value):
        where = pl.ds(row, planes, stride=rows)
        out[where, :] = (out[where, :] + value) * (1.0 / 3.0)

    substitute(0, rows, ysep[0], ysep[1], lambda r: (yw[r], yv[r], yg[r]), y_emit)
    for ref, sem, total in (
        (ysnd, ys_send, lat_total),
        (yret, yr_send, lat_total),
        (zsnd, zs_send, depth_total),
        (zret, zr_send, depth_total),
    ):
        wait_all(ref, sem, total)
    for index, way in enumerate(ways):

        @pl.when(has[way])
        def _():
            halo_copy(index, way).wait_send()


def shards(depth_total, lat_total, volume):
    planes, rows, columns = volume.shape
    y_chunk = planes // lat_total
    z_chunk = rows // depth_total
    f32 = jnp.float32

    def vmem(*shape):
        return pltpu.VMEM(shape + (columns,), f32)

    def dma(count):
        return pltpu.SemaphoreType.DMA((count,))

    cells = planes * rows
    out = pl.pallas_call(
        functools.partial(kernel, depth_total, lat_total, planes, rows),
        out_shape=jax.ShapeDtypeStruct((cells, columns), f32),
        in_specs=[pl.BlockSpec(memory_space=pltpu.HBM)],
        out_specs=pl.BlockSpec(memory_space=pltpu.VMEM),
        scratch_shapes=[
            vmem(cells),
            vmem(2, 2 * planes),
            vmem(2, 2 * planes),
            vmem(2, 2 * rows),
            vmem(2, 2, 8),
            vmem(cells),
            vmem((planes + 2) * rows),
            vmem(2, planes + 16),
            vmem(2, planes + 16),
            vmem(cells),
            vmem(cells),
            vmem(cells),
            vmem(columns // 8, cells * 8 // columns),
            vmem(columns // 8, cells * 8 // columns),
            vmem(columns // 8, cells * 8 // columns),
            vmem(planes, rows),
            vmem(planes, rows),
            vmem(planes, rows),
            vmem(rows, planes),
            vmem(rows, planes),
            vmem(rows, planes),
            vmem(depth_total, 5 * z_chunk),
            vmem(depth_total, 5 * z_chunk),
            vmem(depth_total, 2 * z_chunk),
            vmem(depth_total, 2 * z_chunk),
            vmem(2, rows),
            vmem(lat_total, 5 * y_chunk),
            vmem(lat_total, 5 * y_chunk),
            vmem(lat_total, 2 * y_chunk),
            vmem(lat_total, 2 * y_chunk),
            vmem(2, planes),
            pltpu.SemaphoreType.DMA,
            dma(8),
            dma(8),
            pltpu.SemaphoreType.DMA,
            pltpu.SemaphoreType.DMA,
            pltpu.SemaphoreType.DMA,
            pltpu.SemaphoreType.DMA,
            pltpu.SemaphoreType.DMA,
            pltpu.SemaphoreType.DMA,
            pltpu.SemaphoreType.DMA,
            pltpu.SemaphoreType.DMA,
        ],
        compiler_params=pltpu.CompilerParams(
            collective_id=0, has_side_effects=True, vmem_limit_bytes=24 * 1024 * 1024
        ),
        cost_estimate=pl.CostEstimate(
            flops=400 * cells * columns, bytes_accessed=8 * cells * columns, transcendentals=0
        ),
    )(pltpu.with_memory_space_constraint(volume.reshape(cells, columns), pltpu.HBM))
    return out.reshape(volume.shape)


def solution(mesh):
    placed = (P("depth", "lat", None),)
    return jax.shard_map(
        functools.partial(shards, mesh.shape["depth"], mesh.shape["lat"]),
        mesh=mesh,
        in_specs=placed,
        out_specs=P("depth", "lat", None),
        check_vma=False,
    )
```

```python
import functools

import jax
import jax.numpy as jnp
from jax import lax
from jax.experimental import pallas as pl
from jax.experimental.pallas import tpu as pltpu
from jax.sharding import PartitionSpec as P

TAU = 300.0
LAMBDA = 0.5
MESH = pl.DeviceIdType.MESH
SCALE = (64.0 * LAMBDA) ** 2
LEAF = 8


def recip(value):
    guess = pl.reciprocal(value, approx=True)
    return guess * (2.0 - value * guess)


def coupling(diff):
    return (3.0 * TAU * SCALE) * recip(SCALE + diff * diff)


def smooth_x(field):
    lane = lax.broadcasted_iota(jnp.int32, field.shape, 1)
    width = field.shape[1]
    before = jnp.where(lane == 0, 0.0, pltpu.roll(field, 1, 1))
    after = jnp.where(lane == width - 1, 0.0, pltpu.roll(field, width - 1, 1))
    return (before + after) + (field + field)


def eliminate(lo, hi, couple, source, keep):
    starts = list(range(lo, hi, LEAF))
    state = []
    for start in starts:
        state.append([1.0, couple(start - 1), source(start), None, None])
    for step in range(LEAF - 1):
        for part, start in enumerate(starts):
            excess, fill, src, excess_low, src_low = state[part]
            cell = start + step
            after = couple(cell)
            inverse = recip(excess + fill + after)
            onward = after * inverse
            back = fill * inverse
            keep(cell, onward, back, src * inverse)
            add_excess = back * excess
            add_src = back * src
            state[part] = [
                1.0 + onward * excess,
                onward * fill,
                source(cell + 1) + onward * src,
                add_excess if excess_low is None else excess_low + add_excess,
                add_src if src_low is None else src_low + add_src,
            ]
    blocks = [(start, start + LEAF, part) for start, part in zip(starts, state)]
    while len(blocks) > 1:
        merged = []
        for first, second in zip(blocks[::2], blocks[1::2]):
            e1, f1, s1, el1, sl1 = first[2]
            e2, f2, s2, el2, sl2 = second[2]
            excess = e1 + el2
            src = s1 + sl2
            inverse = recip(excess + f1 + f2)
            onward = f2 * inverse
            back = f1 * inverse
            keep(first[1] - 1, onward, back, src * inverse)
            merged.append(
                (
                    first[0],
                    second[1],
                    [
                        e2 + onward * excess,
                        onward * f1,
                        s2 + onward * src,
                        el1 + back * excess,
                        sl1 + back * src,
                    ],
                )
            )
        blocks = merged
    e, f, s, el, sl = blocks[0][2]
    return el, sl, f, e, s


def substitute(lo, hi, before, last, load, emit):
    known = {lo - 1: before, hi - 1: last}
    emit(hi - 1, last)
    size = hi - lo
    while size > LEAF:
        for start in range(lo, hi, size):
            middle = start + size // 2 - 1
            onward, back, part = load(middle)
            value = part + back * known[start - 1] + onward * known[start + size - 1]
            known[middle] = value
            emit(middle, value)
        size = size // 2
    current = {start: known[start + LEAF - 1] for start in range(lo, hi, LEAF)}
    for step in range(LEAF - 2, -1, -1):
        for start in range(lo, hi, LEAF):
            onward, back, part = load(start + step)
            value = part + back * known[start - 1] + onward * current[start]
            current[start] = value
            emit(start + step, value)


def solve_reduced(count, rows, got):
    excess = got(0, 3)
    src = got(0, 4)
    onwards, parts = [], []
    for k in range(count - 1):
        couple = got(k + 1, 2)
        excess = excess + got(k + 1, 0)
        src = src + got(k + 1, 1)
        inverse = recip(excess + couple)
        onward = couple * inverse
        onwards.append(onward)
        parts.append(src * inverse)
        excess = got(k + 1, 3) + onward * excess
        src = got(k + 1, 4) + onward * src
    value = src * recip(excess)
    values = [value]
    for k in range(count - 2, -1, -1):
        value = parts[k] + onwards[k] * value
        values.append(value)
    return values[::-1]


def kernel(
    depth_total, lat_total, planes, rows,
    source, out,
    vol, pack_one, pack_two, yh_one, yh_two, zh_one, zh_two, cn, sm_x, sm, yy, nn,
    vol_t, sm_t, x_out, xw, xv, xg, zw, zv, zg, yw, yv, yg,
    zsnd, zrcv, zret, zfin, zsep, ysnd, yrcv, yret, yfin, ysep,
    load_sem, halo_send, halo_recv, zs_send, zs_recv, zr_send, zr_recv,
    ys_send, ys_recv, yr_send, yr_recv,
):
    dm = lax.axis_index("depth")
    lm = lax.axis_index("lat")
    has = {
        (-1, 0): dm > 0,
        (1, 0): dm < depth_total - 1,
        (0, -1): lm > 0,
        (0, 1): lm < lat_total - 1,
    }
    for dz in (-1, 1):
        for dy in (-1, 1):
            has[(dz, dy)] = jnp.logical_and(has[(dz, 0)], has[(0, dy)])
    corners = [(dz, dy) for dz in (-1, 1) for dy in (-1, 1)]

    load = pltpu.make_async_copy(source, vol, load_sem)
    load.start()

    barrier = pltpu.get_barrier_semaphore()
    for step in range(1, lat_total):
        pl.semaphore_signal(
            barrier, inc=1, device_id=(dm, lax.rem(lm + step, lat_total)), device_id_type=MESH
        )
    for step in range(1, depth_total):
        pl.semaphore_signal(
            barrier, inc=1, device_id=(lax.rem(dm + step, depth_total), lm), device_id_type=MESH
        )
    expected = jnp.int32(lat_total + depth_total - 2)
    for dz, dy in corners:
        expected = expected + has[(dz, dy)].astype(jnp.int32)

        @pl.when(has[(dz, dy)])
        def _():
            pl.semaphore_signal(
                barrier, inc=1, device_id=(dm + dz, lm + dy), device_id_type=MESH
            )

    load.wait()
    pack_one[...] = vol[pl.ds(0, planes, stride=rows), :]
    for j in range(2):
        pack_two[pl.ds(j, planes, stride=2), :] = vol[pl.ds(rows - 2 + j, planes, stride=rows), :]
    pl.semaphore_wait(barrier, expected)

    def halo_copy(index, way):
        dz, dy = way
        zi, yi = (dz + 1) // 2, (dy + 1) // 2
        if dy == 0:
            src = vol.at[pl.ds(0, rows) if dz < 0 else pl.ds((planes - 2) * rows, 2 * rows)]
            dst = zh_one if dz < 0 else zh_two
        elif dz == 0:
            src, dst = (pack_one, yh_one) if dy < 0 else (pack_two, yh_two)
        else:
            pack, count = (pack_one, planes) if dy < 0 else (pack_two, 2 * planes)
            src = pack.at[pl.ds(0 if dz < 0 else count - 8, 8)]
            dst = cn.at[1 - zi, 1 - yi]
        return pltpu.make_async_remote_copy(
            src_ref=src,
            dst_ref=dst,
            send_sem=halo_send.at[index],
            recv_sem=halo_recv.at[index],
            device_id=(dm + dz, lm + dy),
            device_id_type=MESH,
        )

    ways = [(0, -1), (0, 1), (-1, 0), (1, 0)] + corners
    opposite = {way: ways.index((-way[0], -way[1])) for way in ways}
    for index, way in enumerate(ways):

        @pl.when(has[way])
        def _():
            halo_copy(index, way).start()

    def smooth_y(field):
        row = lax.broadcasted_iota(jnp.int32, field.shape, 0)
        before = jnp.where(row == 0, 0.0, pltpu.roll(field, 1, 0))
        after = jnp.where(row == rows - 1, 0.0, pltpu.roll(field, rows - 1, 0))
        return (before + after) + (field + field)

    def plane_at(plane):
        return pl.ds((plane + 1) * rows, rows)

    older = old = None
    for plane in range(planes + 1):
        new = None
        if plane < planes:
            where = pl.ds(plane * rows, rows)
            along_x = smooth_x(vol[where, :])
            sm_x[where, :] = along_x
            new = smooth_y(along_x)
            if plane == 0:
                sm[plane_at(-1), :] = new
        if old is not None:
            total = old + old
            total = total if older is None else total + older
            sm[plane_at(plane - 1), :] = total if new is None else total + new
        older, old = old, new
    tile = vol.shape[1]
    blocks = planes * rows // tile
    for block in range(blocks):
        where = pl.ds(block * tile, tile)
        vol_t[where, :] = vol[where, :].T

    for index, way in enumerate(ways):
        back = opposite[way]

        @pl.when(has[way])
        def _():
            halo_copy(back, ways[back]).wait_recv()

        @pl.when(jnp.logical_not(has[way]))
        def _():
            dz, dy = way
            zi, yi = (dz + 1) // 2, (dy + 1) // 2
            if dy == 0:
                ref = zh_two if dz < 0 else zh_one
                ref[...] = jnp.zeros(ref.shape, jnp.float32)
            elif dz == 0:
                ref = yh_two if dy < 0 else yh_one
                ref[...] = jnp.zeros(ref.shape, jnp.float32)
            else:
                cn[zi, yi] = jnp.zeros(cn.shape[2:], jnp.float32)

    far_x = smooth_x(zh_two[pl.ds(0, rows), :])
    low_x = smooth_x(zh_two[pl.ds(rows, rows), :])
    high_x = smooth_x(zh_one[...])
    low_y = smooth_y(low_x)
    sm[plane_at(-1), :] = sm[plane_at(-1), :] + smooth_y(far_x) + (low_y + low_y)
    sm[plane_at(0), :] = sm[plane_at(0), :] + low_y
    sm[plane_at(planes - 1), :] = sm[plane_at(planes - 1), :] + smooth_y(high_x)
    low_tile = smooth_x(cn[0, 0])
    high_tile = smooth_x(cn[1, 0])
    far_row = smooth_x(yh_two[pl.ds(0, planes, stride=2), :])
    low_row = smooth_x(yh_two[pl.ds(1, planes, stride=2), :])
    edge_row = sm_x[pl.ds(0, planes, stride=rows), :]
    yy[pl.ds(8, planes), :] = (far_row + edge_row) + (low_row + low_row)
    for where, plane_x, far_one, near_one in (
        (7, low_x, low_tile[6:7], low_tile[7:8]),
        (8 + planes, high_x, high_tile[0:1], high_tile[1:2]),
    ):
        yy[pl.ds(where, 1), :] = (far_one + plane_x[0:1]) + (near_one + near_one)
    low_side = (0, 0, low_row, low_tile[5:6], low_tile[7:8], high_tile[1:2])
    low_tile = smooth_x(cn[0, 1])
    high_tile = smooth_x(cn[1, 1])
    high_row = smooth_x(yh_one[...])
    high_side = (1, rows - 1, high_row, low_tile[6:7], low_tile[7:8], high_tile[0:1])
    for side, edge, row, two_before, before, after in (low_side, high_side):
        where = pl.ds(edge, 1)
        sm[where, :] = sm[where, :] + row[0:1] + two_before + (before + before)
        nn[side, pl.ds(8, planes), :] = row
        nn[side, pl.ds(7, 1), :] = before
        nn[side, pl.ds(8 + planes, 1), :] = after
        where = pl.ds(rows + edge, planes, stride=rows)
        ends = nn[side, pl.ds(7, planes), :] + nn[side, pl.ds(9, planes), :]
        sm[where, :] = sm[where, :] + ends + (row + row)

    def exchange(axis, src, dst, sems, total, me):
        for step in sorted(range(1, total), key=lambda step: abs(2 * step - total)):
            other = lax.rem(me + step, total)
            pltpu.make_async_remote_copy(
                src_ref=src.at[other],
                dst_ref=dst.at[me],
                send_sem=sems[0],
                recv_sem=sems[1],
                device_id=(other, lm) if axis == "depth" else (dm, other),
                device_id_type=MESH,
            ).start()
        dst[me] = src[me]

    def wait_all(ref, sem, total):
        some = ref.at[pl.ds(0, total - 1)]
        pltpu.make_async_copy(some, some, sem).wait()

    def row_smoothed(row):
        if 0 <= row < rows:
            return sm[pl.ds(rows + row, planes, stride=rows), :]
        middle = yy[pl.ds(8, planes), :]
        ends = yy[pl.ds(7, planes), :] + yy[pl.ds(9, planes), :]
        return ends + (middle + middle)

    y_couples = {}

    def y_couple(row):
        if row not in y_couples:
            value = coupling(row_smoothed(row + 1) - row_smoothed(row))
            if row == -1:
                value = value * jnp.where(has[(0, -1)], 1.0, 0.0)
            y_couples[row] = value
        return y_couples[row]

    def y_keep(row, onward, back, part):
        yw[row] = onward
        yv[row] = back
        yg[row] = part

    y_chunk = planes // lat_total
    results = eliminate(
        0, rows, y_couple, lambda row: vol[pl.ds(row, planes, stride=rows), :], y_keep
    )
    for q, value in enumerate(results):
        for k in range(lat_total):
            ysnd[k, pl.ds(q * y_chunk, y_chunk), :] = value[k * y_chunk : (k + 1) * y_chunk]
    exchange("lat", ysnd, yrcv, (ys_send, ys_recv), lat_total, lm)

    z_couples = {}

    def z_couple(plane):
        if plane not in z_couples:
            diff = sm[pl.ds((plane + 2) * rows, rows), :] - sm[pl.ds((plane + 1) * rows, rows), :]
            value = coupling(diff)
            if plane == -1:
                value = value * jnp.where(has[(-1, 0)], 1.0, 0.0)
            z_couples[plane] = value
        return z_couples[plane]

    def z_keep(plane, onward, back, part):
        zw[plane] = onward
        zv[plane] = back
        zg[plane] = part

    z_chunk = rows // depth_total
    results = eliminate(
        0, planes, z_couple, lambda plane: vol[pl.ds(plane * rows, rows), :], z_keep
    )
    for q, value in enumerate(results):
        for k in range(depth_total):
            zsnd[k, pl.ds(q * z_chunk, z_chunk), :] = value[k * z_chunk : (k + 1) * z_chunk]
    exchange("depth", zsnd, zrcv, (zs_send, zs_recv), depth_total, dm)

    for block in range(blocks):
        where = pl.ds(block * tile, tile)
        sm_t[where, :] = sm[pl.ds(rows + block * tile, tile), :].T
    cells = tile // 8
    spread = blocks * 8

    def x_at(cell):
        return pl.ds(cell, spread, stride=cells)

    def turn(field, by):
        return pltpu.roll(field.reshape(blocks, 8, tile), by, 1).reshape(spread, tile)

    x_couples = {}

    def x_couple(cell):
        if cell not in x_couples:
            if cell == -1:
                value = turn(x_couple(cells - 1), 1)
            elif cell == cells - 1:
                sub = lax.rem(lax.broadcasted_iota(jnp.int32, (spread, tile), 0), 8)
                diff = turn(sm_t[x_at(0), :], 7) - sm_t[x_at(cell), :]
                value = jnp.where(sub == 7, 0.0, coupling(diff))
            else:
                value = coupling(sm_t[x_at(cell + 1), :] - sm_t[x_at(cell), :])
            x_couples[cell] = value
        return x_couples[cell]

    def x_keep(cell, onward, back, part):
        xw[cell] = onward
        xv[cell] = back
        xg[cell] = part

    excess_low, src_low, couple, excess, src = eliminate(
        0, cells, x_couple, lambda cell: vol_t[x_at(cell), :], x_keep
    )
    diag = excess + turn(excess_low, 7) + couple
    src = src + turn(src_low, 7)
    couple = turn(couple, 7)
    diag = diag + couple
    offset = 1
    while offset < 8:
        inverse = recip(diag)
        scaled = couple * inverse
        after = couple * turn(inverse, 8 - offset)
        new_diag = diag - turn(couple * scaled, offset) - couple * after
        src = src + turn(scaled * src, offset) + couple * turn(inverse * src, 8 - offset)
        if 2 * offset < 8:
            couple = couple * turn(scaled, 8 - offset)
        diag = new_diag
        offset = offset * 2
    last = src * recip(diag)

    def x_emit(cell, value):
        x_out[x_at(cell), :] = value

    substitute(0, cells, turn(last, 1), last, lambda c: (xw[c], xv[c], xg[c]), x_emit)
    for block in range(blocks):
        where = pl.ds(block * tile, tile)
        out[where, :] = x_out[where, :].T

    def reduce_and_return(axis, rcv, ret, fin, recv, sems, total, me, chunk):
        wait_all(rcv, recv, total)
        values = solve_reduced(
            total, chunk, lambda k, q: rcv[k, pl.ds(q * chunk, chunk), :]
        )
        for k in range(total):
            ret[k, pl.ds(0, chunk), :] = values[k - 1] if k else jnp.zeros_like(values[0])
            ret[k, pl.ds(chunk, chunk), :] = values[k]
        exchange(axis, ret, fin, sems, total, me)

    y_sems = (yr_send, yr_recv)
    z_sems = (zr_send, zr_recv)
    reduce_and_return("lat", yrcv, yret, yfin, ys_recv, y_sems, lat_total, lm, y_chunk)
    reduce_and_return("depth", zrcv, zret, zfin, zs_recv, z_sems, depth_total, dm, z_chunk)

    def gather(fin, sep, total, chunk):
        for k in range(total):
            for q in range(2):
                sep[q, pl.ds(k * chunk, chunk), :] = fin[k, pl.ds(q * chunk, chunk), :]

    wait_all(zfin, zr_recv, depth_total)
    gather(zfin, zsep, depth_total, z_chunk)

    def z_emit(plane, value):
        where = pl.ds(plane * rows, rows)
        out[where, :] = out[where, :] + value

    substitute(
        0, planes, zsep[0], zsep[1], lambda p: (zw[p], zv[p], zg[p]), z_emit
    )
    wait_all(yfin, yr_recv, lat_total)
    gather(yfin, ysep, lat_total, y_chunk)

    def y_emit(row, value):
        where = pl.ds(row, planes, stride=rows)
        out[where, :] = (out[where, :] + value) * (1.0 / 3.0)

    substitute(0, rows, ysep[0], ysep[1], lambda r: (yw[r], yv[r], yg[r]), y_emit)
    for ref, sem, total in (
        (ysnd, ys_send, lat_total),
        (yret, yr_send, lat_total),
        (zsnd, zs_send, depth_total),
        (zret, zr_send, depth_total),
    ):
        wait_all(ref, sem, total)
    for index, way in enumerate(ways):

        @pl.when(has[way])
        def _():
            halo_copy(index, way).wait_send()


def shards(depth_total, lat_total, volume):
    planes, rows, columns = volume.shape
    y_chunk = planes // lat_total
    z_chunk = rows // depth_total
    f32 = jnp.float32

    def vmem(*shape):
        return pltpu.VMEM(shape + (columns,), f32)

    def dma(count):
        return pltpu.SemaphoreType.DMA((count,))

    cells = planes * rows
    out = pl.pallas_call(
        functools.partial(kernel, depth_total, lat_total, planes, rows),
        out_shape=jax.ShapeDtypeStruct((cells, columns), f32),
        in_specs=[pl.BlockSpec(memory_space=pltpu.HBM)],
        out_specs=pl.BlockSpec(memory_space=pltpu.VMEM),
        scratch_shapes=[
            vmem(cells),
            vmem(planes),
            vmem(2 * planes),
            vmem(planes),
            vmem(2 * planes),
            vmem(rows),
            vmem(2 * rows),
            vmem(2, 2, 8),
            vmem(cells),
            vmem((planes + 1) * rows),
            vmem(planes + 16),
            vmem(2, planes + 16),
            vmem(cells),
            vmem(cells),
            vmem(cells),
            vmem(columns // 8, cells * 8 // columns),
            vmem(columns // 8, cells * 8 // columns),
            vmem(columns // 8, cells * 8 // columns),
            vmem(planes, rows),
            vmem(planes, rows),
            vmem(planes, rows),
            vmem(rows, planes),
            vmem(rows, planes),
            vmem(rows, planes),
            vmem(depth_total, 5 * z_chunk),
            vmem(depth_total, 5 * z_chunk),
            vmem(depth_total, 2 * z_chunk),
            vmem(depth_total, 2 * z_chunk),
            vmem(2, rows),
            vmem(lat_total, 5 * y_chunk),
            vmem(lat_total, 5 * y_chunk),
            vmem(lat_total, 2 * y_chunk),
            vmem(lat_total, 2 * y_chunk),
            vmem(2, planes),
            pltpu.SemaphoreType.DMA,
            dma(8),
            dma(8),
            pltpu.SemaphoreType.DMA,
            pltpu.SemaphoreType.DMA,
            pltpu.SemaphoreType.DMA,
            pltpu.SemaphoreType.DMA,
            pltpu.SemaphoreType.DMA,
            pltpu.SemaphoreType.DMA,
            pltpu.SemaphoreType.DMA,
            pltpu.SemaphoreType.DMA,
        ],
        compiler_params=pltpu.CompilerParams(
            collective_id=0, has_side_effects=True, vmem_limit_bytes=24 * 1024 * 1024
        ),
        cost_estimate=pl.CostEstimate(
            flops=400 * cells * columns, bytes_accessed=8 * cells * columns, transcendentals=0
        ),
    )(pltpu.with_memory_space_constraint(volume.reshape(cells, columns), pltpu.HBM))
    return out.reshape(volume.shape)


def solution(mesh):
    placed = (P("depth", "lat", None),)
    return jax.shard_map(
        functools.partial(shards, mesh.shape["depth"], mesh.shape["lat"]),
        mesh=mesh,
        in_specs=placed,
        out_specs=P("depth", "lat", None),
        check_vma=False,
    )
```

```python
import functools

import jax
import jax.numpy as jnp
from jax import lax
from jax.experimental import pallas as pl
from jax.experimental.pallas import tpu as pltpu
from jax.sharding import PartitionSpec as P

TAU = 300.0
LAMBDA = 0.5
MESH = pl.DeviceIdType.MESH
SCALE = (64.0 * LAMBDA) ** 2
LEAF = 8


def recip(value):
    guess = pl.reciprocal(value, approx=True)
    return guess * (2.0 - value * guess)


def coupling(diff):
    return (3.0 * TAU * SCALE) * recip(SCALE + diff * diff)


def smooth_x(field):
    lane = lax.broadcasted_iota(jnp.int32, field.shape, 1)
    width = field.shape[1]
    before = jnp.where(lane == 0, 0.0, pltpu.roll(field, 1, 1))
    after = jnp.where(lane == width - 1, 0.0, pltpu.roll(field, width - 1, 1))
    return (before + after) + (field + field)


def eliminate(lo, hi, couple, source, keep):
    starts = list(range(lo, hi, LEAF))
    init = []
    for start in starts:
        src = source(start)
        zero = jnp.zeros_like(src)
        init.append((zero + 1.0, couple(start - 1), src, zero, zero, couple(start)))

    def body(step, carry):
        state = []
        for start, (excess, fill, src, excess_low, src_low, after) in zip(starts, carry):
            cell = start + step
            inverse = recip(excess + fill + after)
            onward = after * inverse
            back = fill * inverse
            keep(cell, onward, back, src * inverse)
            state.append(
                (
                    1.0 + onward * excess,
                    onward * fill,
                    source(cell + 1) + onward * src,
                    excess_low + back * excess,
                    src_low + back * src,
                    couple(cell + 1),
                )
            )
        return tuple(state)

    state = lax.fori_loop(0, LEAF - 1, body, tuple(init))
    state = [part[:5] for part in state]
    blocks = [(start, start + LEAF, part) for start, part in zip(starts, state)]
    while len(blocks) > 1:
        merged = []
        for first, second in zip(blocks[::2], blocks[1::2]):
            e1, f1, s1, el1, sl1 = first[2]
            e2, f2, s2, el2, sl2 = second[2]
            excess = e1 + el2
            src = s1 + sl2
            inverse = recip(excess + f1 + f2)
            onward = f2 * inverse
            back = f1 * inverse
            keep(first[1] - 1, onward, back, src * inverse)
            merged.append(
                (
                    first[0],
                    second[1],
                    [
                        e2 + onward * excess,
                        onward * f1,
                        s2 + onward * src,
                        el1 + back * excess,
                        sl1 + back * src,
                    ],
                )
            )
        blocks = merged
    e, f, s, el, sl = blocks[0][2]
    return el, sl, f, e, s


def substitute(lo, hi, before, last, load, emit):
    known = {lo - 1: before, hi - 1: last}
    emit(hi - 1, last)
    size = hi - lo
    while size > LEAF:
        for start in range(lo, hi, size):
            middle = start + size // 2 - 1
            onward, back, part = load(middle)
            value = part + back * known[start - 1] + onward * known[start + size - 1]
            known[middle] = value
            emit(middle, value)
        size = size // 2
    starts = list(range(lo, hi, LEAF))

    def body(step, carry):
        current = []
        for start, later in zip(starts, carry):
            cell = start + (LEAF - 2) - step
            onward, back, part = load(cell)
            value = part + back * known[start - 1] + onward * later
            current.append(value)
            emit(cell, value)
        return tuple(current)

    lax.fori_loop(0, LEAF - 1, body, tuple(known[start + LEAF - 1] for start in starts))


def solve_reduced(count, rows, got):
    excess = got(0, 3)
    src = got(0, 4)
    onwards, parts = [], []
    for k in range(count - 1):
        couple = got(k + 1, 2)
        excess = excess + got(k + 1, 0)
        src = src + got(k + 1, 1)
        inverse = recip(excess + couple)
        onward = couple * inverse
        onwards.append(onward)
        parts.append(src * inverse)
        excess = got(k + 1, 3) + onward * excess
        src = got(k + 1, 4) + onward * src
    value = src * recip(excess)
    values = [value]
    for k in range(count - 2, -1, -1):
        value = parts[k] + onwards[k] * value
        values.append(value)
    return values[::-1]


def kernel(
    depth_total, lat_total, planes, rows,
    source, out,
    vol, pack_one, pack_two, yh_one, yh_two, zh_one, zh_two, cn, sm_x, sm, yy, nn,
    vol_t, sm_t, x_out, xw, xv, xg, zw, zv, zg, yw, yv, yg,
    zsnd, zrcv, zret, zfin, zsep, ysnd, yrcv, yret, yfin, ysep,
    load_sem, halo_send, halo_recv, zs_send, zs_recv, zr_send, zr_recv,
    ys_send, ys_recv, yr_send, yr_recv,
):
    dm = lax.axis_index("depth")
    lm = lax.axis_index("lat")
    has = {
        (-1, 0): dm > 0,
        (1, 0): dm < depth_total - 1,
        (0, -1): lm > 0,
        (0, 1): lm < lat_total - 1,
    }
    for dz in (-1, 1):
        for dy in (-1, 1):
            has[(dz, dy)] = jnp.logical_and(has[(dz, 0)], has[(0, dy)])
    corners = [(dz, dy) for dz in (-1, 1) for dy in (-1, 1)]

    load = pltpu.make_async_copy(source, vol, load_sem)
    load.start()

    barrier = pltpu.get_barrier_semaphore()
    for step in range(1, lat_total):
        pl.semaphore_signal(
            barrier, inc=1, device_id=(dm, lax.rem(lm + step, lat_total)), device_id_type=MESH
        )
    for step in range(1, depth_total):
        pl.semaphore_signal(
            barrier, inc=1, device_id=(lax.rem(dm + step, depth_total), lm), device_id_type=MESH
        )
    expected = jnp.int32(lat_total + depth_total - 2)
    for dz, dy in corners:
        expected = expected + has[(dz, dy)].astype(jnp.int32)

        @pl.when(has[(dz, dy)])
        def _():
            pl.semaphore_signal(
                barrier, inc=1, device_id=(dm + dz, lm + dy), device_id_type=MESH
            )

    load.wait()
    pack_one[...] = vol[pl.ds(0, planes, stride=rows), :]
    for j in range(2):
        pack_two[pl.ds(j, planes, stride=2), :] = vol[pl.ds(rows - 2 + j, planes, stride=rows), :]
    pl.semaphore_wait(barrier, expected)

    def halo_copy(index, way):
        dz, dy = way
        zi, yi = (dz + 1) // 2, (dy + 1) // 2
        if dy == 0:
            src = vol.at[pl.ds(0, rows) if dz < 0 else pl.ds((planes - 2) * rows, 2 * rows)]
            dst = zh_one if dz < 0 else zh_two
        elif dz == 0:
            src, dst = (pack_one, yh_one) if dy < 0 else (pack_two, yh_two)
        else:
            pack, count = (pack_one, planes) if dy < 0 else (pack_two, 2 * planes)
            src = pack.at[pl.ds(0 if dz < 0 else count - 8, 8)]
            dst = cn.at[1 - zi, 1 - yi]
        return pltpu.make_async_remote_copy(
            src_ref=src,
            dst_ref=dst,
            send_sem=halo_send.at[index],
            recv_sem=halo_recv.at[index],
            device_id=(dm + dz, lm + dy),
            device_id_type=MESH,
        )

    ways = [(0, -1), (0, 1), (-1, 0), (1, 0)] + corners
    opposite = {way: ways.index((-way[0], -way[1])) for way in ways}
    for index, way in enumerate(ways):

        @pl.when(has[way])
        def _():
            halo_copy(index, way).start()

    def smooth_y(field):
        row = lax.broadcasted_iota(jnp.int32, field.shape, 0)
        before = jnp.where(row == 0, 0.0, pltpu.roll(field, 1, 0))
        after = jnp.where(row == rows - 1, 0.0, pltpu.roll(field, rows - 1, 0))
        return (before + after) + (field + field)

    def plane_at(plane):
        return pl.ds((plane + 1) * rows, rows)

    group = 4

    def smooth_planes(step, carry):
        older, old = carry
        for plane in range(group):
            start = pl.multiple_of((step * group + plane) * rows, rows)
            along_x = smooth_x(vol[pl.ds(start, rows), :])
            sm_x[pl.ds(start, rows), :] = along_x
            new = smooth_y(along_x)
            sm[pl.ds(start, rows), :] = (older + new) + (old + old)
            older, old = old, new
        return older, old

    zero = jnp.zeros((rows, vol.shape[1]), jnp.float32)
    older, old = lax.fori_loop(0, planes // group, smooth_planes, (zero, zero))
    sm[plane_at(planes - 1), :] = older + (old + old)
    tile = vol.shape[1]
    blocks = planes * rows // tile

    def turn_tiles(src, shift, dst):
        def body(block, carry):
            start = pl.multiple_of(block * tile, tile)
            dst[pl.ds(start, tile), :] = src[pl.ds(shift + start, tile), :].T
            return carry

        lax.fori_loop(0, blocks, body, 0)

    turn_tiles(vol, 0, vol_t)

    for index, way in enumerate(ways):
        back = opposite[way]

        @pl.when(has[way])
        def _():
            halo_copy(back, ways[back]).wait_recv()

        @pl.when(jnp.logical_not(has[way]))
        def _():
            dz, dy = way
            zi, yi = (dz + 1) // 2, (dy + 1) // 2
            if dy == 0:
                ref = zh_two if dz < 0 else zh_one
                ref[...] = jnp.zeros(ref.shape, jnp.float32)
            elif dz == 0:
                ref = yh_two if dy < 0 else yh_one
                ref[...] = jnp.zeros(ref.shape, jnp.float32)
            else:
                cn[zi, yi] = jnp.zeros(cn.shape[2:], jnp.float32)

    far_x = smooth_x(zh_two[pl.ds(0, rows), :])
    low_x = smooth_x(zh_two[pl.ds(rows, rows), :])
    high_x = smooth_x(zh_one[...])
    low_y = smooth_y(low_x)
    sm[plane_at(-1), :] = sm[plane_at(-1), :] + smooth_y(far_x) + (low_y + low_y)
    sm[plane_at(0), :] = sm[plane_at(0), :] + low_y
    sm[plane_at(planes - 1), :] = sm[plane_at(planes - 1), :] + smooth_y(high_x)
    low_tile = smooth_x(cn[0, 0])
    high_tile = smooth_x(cn[1, 0])
    far_row = smooth_x(yh_two[pl.ds(0, planes, stride=2), :])
    low_row = smooth_x(yh_two[pl.ds(1, planes, stride=2), :])
    edge_row = sm_x[pl.ds(0, planes, stride=rows), :]
    yy[pl.ds(8, planes), :] = (far_row + edge_row) + (low_row + low_row)
    for where, plane_x, far_one, near_one in (
        (7, low_x, low_tile[6:7], low_tile[7:8]),
        (8 + planes, high_x, high_tile[0:1], high_tile[1:2]),
    ):
        yy[pl.ds(where, 1), :] = (far_one + plane_x[0:1]) + (near_one + near_one)
    low_side = (0, 0, low_row, low_tile[5:6], low_tile[7:8], high_tile[1:2])
    low_tile = smooth_x(cn[0, 1])
    high_tile = smooth_x(cn[1, 1])
    high_row = smooth_x(yh_one[...])
    high_side = (1, rows - 1, high_row, low_tile[6:7], low_tile[7:8], high_tile[0:1])
    for side, edge, row, two_before, before, after in (low_side, high_side):
        where = pl.ds(edge, 1)
        sm[where, :] = sm[where, :] + row[0:1] + two_before + (before + before)
        nn[side, pl.ds(8, planes), :] = row
        nn[side, pl.ds(7, 1), :] = before
        nn[side, pl.ds(8 + planes, 1), :] = after
        where = pl.ds(rows + edge, planes, stride=rows)
        ends = nn[side, pl.ds(7, planes), :] + nn[side, pl.ds(9, planes), :]
        sm[where, :] = sm[where, :] + ends + (row + row)

    def exchange(axis, src, dst, sems, total, me):
        for step in sorted(range(1, total), key=lambda step: abs(2 * step - total)):
            other = lax.rem(me + step, total)
            pltpu.make_async_remote_copy(
                src_ref=src.at[other],
                dst_ref=dst.at[me],
                send_sem=sems[0],
                recv_sem=sems[1],
                device_id=(other, lm) if axis == "depth" else (dm, other),
                device_id_type=MESH,
            ).start()
        dst[me] = src[me]

    def wait_all(ref, sem, total):
        some = ref.at[pl.ds(0, total - 1)]
        pltpu.make_async_copy(some, some, sem).wait()

    def row_smoothed(row):
        return sm[pl.ds(rows + row, planes, stride=rows), :]

    def y_couple(row):
        if isinstance(row, int) and row == -1:
            middle = yy[pl.ds(8, planes), :]
            ends = yy[pl.ds(7, planes), :] + yy[pl.ds(9, planes), :]
            value = coupling(row_smoothed(0) - (ends + (middle + middle)))
            return value * jnp.where(has[(0, -1)], 1.0, 0.0)
        return coupling(row_smoothed(row + 1) - row_smoothed(row))

    def y_keep(row, onward, back, part):
        yw[row] = onward
        yv[row] = back
        yg[row] = part

    y_chunk = planes // lat_total
    results = eliminate(
        0, rows, y_couple, lambda row: vol[pl.ds(row, planes, stride=rows), :], y_keep
    )
    for q, value in enumerate(results):
        for k in range(lat_total):
            ysnd[k, pl.ds(q * y_chunk, y_chunk), :] = value[k * y_chunk : (k + 1) * y_chunk]
    exchange("lat", ysnd, yrcv, (ys_send, ys_recv), lat_total, lm)

    def from_plane(plane):
        return pl.ds(pl.multiple_of(plane * rows, rows), rows)

    def z_couple(plane):
        value = coupling(sm[from_plane(plane + 2), :] - sm[from_plane(plane + 1), :])
        if isinstance(plane, int) and plane == -1:
            value = value * jnp.where(has[(-1, 0)], 1.0, 0.0)
        return value

    def z_keep(plane, onward, back, part):
        zw[plane] = onward
        zv[plane] = back
        zg[plane] = part

    z_chunk = rows // depth_total
    results = eliminate(
        0, planes, z_couple, lambda plane: vol[from_plane(plane), :], z_keep
    )
    for q, value in enumerate(results):
        for k in range(depth_total):
            zsnd[k, pl.ds(q * z_chunk, z_chunk), :] = value[k * z_chunk : (k + 1) * z_chunk]
    exchange("depth", zsnd, zrcv, (zs_send, zs_recv), depth_total, dm)

    turn_tiles(sm, rows, sm_t)
    cells = tile // 8
    spread = blocks * 8

    def x_at(cell):
        return pl.ds(cell, spread, stride=cells)

    def turn(field, by):
        return pltpu.roll(field.reshape(blocks, 8, tile), by, 1).reshape(spread, tile)

    def x_couple(cell):
        if isinstance(cell, int) and cell == -1:
            sub = lax.rem(lax.broadcasted_iota(jnp.int32, (spread, tile), 0), 8)
            before = turn(sm_t[x_at(cells - 1), :], 1)
            return jnp.where(sub == 0, 0.0, coupling(sm_t[x_at(0), :] - before))
        return coupling(sm_t[x_at(cell + 1), :] - sm_t[x_at(cell), :])

    def x_keep(cell, onward, back, part):
        xw[cell] = onward
        xv[cell] = back
        xg[cell] = part

    excess_low, src_low, couple, excess, src = eliminate(
        0, cells, x_couple, lambda cell: vol_t[x_at(cell), :], x_keep
    )
    diag = excess + turn(excess_low, 7) + couple
    src = src + turn(src_low, 7)
    couple = turn(couple, 7)
    diag = diag + couple
    offset = 1
    while offset < 8:
        inverse = recip(diag)
        scaled = couple * inverse
        after = couple * turn(inverse, 8 - offset)
        new_diag = diag - turn(couple * scaled, offset) - couple * after
        src = src + turn(scaled * src, offset) + couple * turn(inverse * src, 8 - offset)
        if 2 * offset < 8:
            couple = couple * turn(scaled, 8 - offset)
        diag = new_diag
        offset = offset * 2
    last = src * recip(diag)

    def x_emit(cell, value):
        x_out[x_at(cell), :] = value

    substitute(0, cells, turn(last, 1), last, lambda c: (xw[c], xv[c], xg[c]), x_emit)
    turn_tiles(x_out, 0, out)

    def reduce_and_return(axis, rcv, ret, fin, recv, sems, total, me, chunk):
        wait_all(rcv, recv, total)
        values = solve_reduced(
            total, chunk, lambda k, q: rcv[k, pl.ds(q * chunk, chunk), :]
        )
        for k in range(total):
            ret[k, pl.ds(0, chunk), :] = values[k - 1] if k else jnp.zeros_like(values[0])
            ret[k, pl.ds(chunk, chunk), :] = values[k]
        exchange(axis, ret, fin, sems, total, me)

    y_sems = (yr_send, yr_recv)
    z_sems = (zr_send, zr_recv)
    reduce_and_return("lat", yrcv, yret, yfin, ys_recv, y_sems, lat_total, lm, y_chunk)
    reduce_and_return("depth", zrcv, zret, zfin, zs_recv, z_sems, depth_total, dm, z_chunk)

    def gather(fin, sep, total, chunk):
        for k in range(total):
            for q in range(2):
                sep[q, pl.ds(k * chunk, chunk), :] = fin[k, pl.ds(q * chunk, chunk), :]

    wait_all(zfin, zr_recv, depth_total)
    gather(zfin, zsep, depth_total, z_chunk)

    def z_emit(plane, value):
        where = from_plane(plane)
        out[where, :] = out[where, :] + value

    substitute(
        0, planes, zsep[0], zsep[1], lambda p: (zw[p], zv[p], zg[p]), z_emit
    )
    wait_all(yfin, yr_recv, lat_total)
    gather(yfin, ysep, lat_total, y_chunk)

    def y_emit(row, value):
        where = pl.ds(row, planes, stride=rows)
        out[where, :] = (out[where, :] + value) * (1.0 / 3.0)

    substitute(0, rows, ysep[0], ysep[1], lambda r: (yw[r], yv[r], yg[r]), y_emit)
    for ref, sem, total in (
        (ysnd, ys_send, lat_total),
        (yret, yr_send, lat_total),
        (zsnd, zs_send, depth_total),
        (zret, zr_send, depth_total),
    ):
        wait_all(ref, sem, total)
    for index, way in enumerate(ways):

        @pl.when(has[way])
        def _():
            halo_copy(index, way).wait_send()


def shards(depth_total, lat_total, volume):
    planes, rows, columns = volume.shape
    y_chunk = planes // lat_total
    z_chunk = rows // depth_total
    f32 = jnp.float32

    def vmem(*shape):
        return pltpu.VMEM(shape + (columns,), f32)

    def dma(count):
        return pltpu.SemaphoreType.DMA((count,))

    cells = planes * rows
    out = pl.pallas_call(
        functools.partial(kernel, depth_total, lat_total, planes, rows),
        out_shape=jax.ShapeDtypeStruct((cells, columns), f32),
        in_specs=[pl.BlockSpec(memory_space=pltpu.HBM)],
        out_specs=pl.BlockSpec(memory_space=pltpu.VMEM),
        scratch_shapes=[
            vmem(cells),
            vmem(planes),
            vmem(2 * planes),
            vmem(planes),
            vmem(2 * planes),
            vmem(rows),
            vmem(2 * rows),
            vmem(2, 2, 8),
            vmem(cells),
            vmem((planes + 2) * rows),
            vmem(planes + 16),
            vmem(2, planes + 16),
            vmem(cells),
            vmem(cells + 8),
            vmem(cells),
            vmem(columns // 8, cells * 8 // columns),
            vmem(columns // 8, cells * 8 // columns),
            vmem(columns // 8, cells * 8 // columns),
            vmem(planes, rows),
            vmem(planes, rows),
            vmem(planes, rows),
            vmem(rows, planes),
            vmem(rows, planes),
            vmem(rows, planes),
            vmem(depth_total, 5 * z_chunk),
            vmem(depth_total, 5 * z_chunk),
            vmem(depth_total, 2 * z_chunk),
            vmem(depth_total, 2 * z_chunk),
            vmem(2, rows),
            vmem(lat_total, 5 * y_chunk),
            vmem(lat_total, 5 * y_chunk),
            vmem(lat_total, 2 * y_chunk),
            vmem(lat_total, 2 * y_chunk),
            vmem(2, planes),
            pltpu.SemaphoreType.DMA,
            dma(8),
            dma(8),
            pltpu.SemaphoreType.DMA,
            pltpu.SemaphoreType.DMA,
            pltpu.SemaphoreType.DMA,
            pltpu.SemaphoreType.DMA,
            pltpu.SemaphoreType.DMA,
            pltpu.SemaphoreType.DMA,
            pltpu.SemaphoreType.DMA,
            pltpu.SemaphoreType.DMA,
        ],
        compiler_params=pltpu.CompilerParams(
            collective_id=0, has_side_effects=True, vmem_limit_bytes=24 * 1024 * 1024
        ),
        cost_estimate=pl.CostEstimate(
            flops=400 * cells * columns, bytes_accessed=8 * cells * columns, transcendentals=0
        ),
    )(pltpu.with_memory_space_constraint(volume.reshape(cells, columns), pltpu.HBM))
    return out.reshape(volume.shape)


def solution(mesh):
    placed = (P("depth", "lat", None),)
    return jax.shard_map(
        functools.partial(shards, mesh.shape["depth"], mesh.shape["lat"]),
        mesh=mesh,
        in_specs=placed,
        out_specs=P("depth", "lat", None),
        check_vma=False,
    )
```

```python
import functools

import jax
import jax.numpy as jnp
from jax import lax
from jax.experimental import pallas as pl
from jax.experimental.pallas import tpu as pltpu
from jax.sharding import PartitionSpec as P

TAU = 300.0
LAMBDA = 0.5
MESH = pl.DeviceIdType.MESH
SCALE = (64.0 * LAMBDA) ** 2
LEAF = 8


def recip(value):
    guess = pl.reciprocal(value, approx=True)
    return guess * (2.0 - value * guess)


def coupling(diff):
    return (3.0 * TAU * SCALE) * recip(SCALE + diff * diff)


def smooth_x(field):
    lane = lax.broadcasted_iota(jnp.int32, field.shape, 1)
    width = field.shape[1]
    before = jnp.where(lane == 0, 0.0, pltpu.roll(field, 1, 1))
    after = jnp.where(lane == width - 1, 0.0, pltpu.roll(field, width - 1, 1))
    return (before + after) + (field + field)


def eliminate(lo, hi, couple, source, keep):
    starts = list(range(lo, hi, LEAF))
    state = []
    for start in starts:
        state.append([1.0, couple(start - 1), source(start), None, None])
    for step in range(LEAF - 1):
        for part, start in enumerate(starts):
            excess, fill, src, excess_low, src_low = state[part]
            cell = start + step
            after = couple(cell)
            inverse = recip(excess + fill + after)
            onward = after * inverse
            back = fill * inverse
            keep(cell, onward, back, src * inverse)
            add_excess = back * excess
            add_src = back * src
            state[part] = [
                1.0 + onward * excess,
                onward * fill,
                source(cell + 1) + onward * src,
                add_excess if excess_low is None else excess_low + add_excess,
                add_src if src_low is None else src_low + add_src,
            ]
    blocks = [(start, start + LEAF, part) for start, part in zip(starts, state)]
    while len(blocks) > 1:
        merged = []
        for first, second in zip(blocks[::2], blocks[1::2]):
            e1, f1, s1, el1, sl1 = first[2]
            e2, f2, s2, el2, sl2 = second[2]
            excess = e1 + el2
            src = s1 + sl2
            inverse = recip(excess + f1 + f2)
            onward = f2 * inverse
            back = f1 * inverse
            keep(first[1] - 1, onward, back, src * inverse)
            merged.append(
                (
                    first[0],
                    second[1],
                    [
                        e2 + onward * excess,
                        onward * f1,
                        s2 + onward * src,
                        el1 + back * excess,
                        sl1 + back * src,
                    ],
                )
            )
        blocks = merged
    e, f, s, el, sl = blocks[0][2]
    return el, sl, f, e, s


def substitute(lo, hi, before, last, load, emit):
    known = {lo - 1: before, hi - 1: last}
    emit(hi - 1, last)
    size = hi - lo
    while size > LEAF:
        for start in range(lo, hi, size):
            middle = start + size // 2 - 1
            onward, back, part = load(middle)
            value = part + back * known[start - 1] + onward * known[start + size - 1]
            known[middle] = value
            emit(middle, value)
        size = size // 2
    current = {start: known[start + LEAF - 1] for start in range(lo, hi, LEAF)}
    for step in range(LEAF - 2, -1, -1):
        for start in range(lo, hi, LEAF):
            onward, back, part = load(start + step)
            value = part + back * known[start - 1] + onward * current[start]
            current[start] = value
            emit(start + step, value)


def solve_reduced(count, rows, got):
    excess = got(0, 3)
    src = got(0, 4)
    onwards, parts = [], []
    for k in range(count - 1):
        couple = got(k + 1, 2)
        excess = excess + got(k + 1, 0)
        src = src + got(k + 1, 1)
        inverse = recip(excess + couple)
        onward = couple * inverse
        onwards.append(onward)
        parts.append(src * inverse)
        excess = got(k + 1, 3) + onward * excess
        src = got(k + 1, 4) + onward * src
    value = src * recip(excess)
    values = [value]
    for k in range(count - 2, -1, -1):
        value = parts[k] + onwards[k] * value
        values.append(value)
    return values[::-1]


def lat_solvers(lat_total):
    solvers = max(lat_total // 2, 1)
    return (lat_total - solvers) // 2, solvers


def kernel(
    depth_total, lat_total, planes, rows,
    source, out,
    vol, pack_one, pack_two, yh_one, yh_two, zh_one, zh_two, cn, sm_x, sm, yy, nn,
    vol_t, sm_t, x_out, xw, xv, xg, zw, zv, zg, yw, yv, yg,
    zsnd, zrcv, zret, zfin, zsep, ysnd, yrcv, yret, yfin, ysep,
    load_sem, halo_send, halo_recv, zs_send, zs_recv, zr_send, zr_recv,
    ys_send, ys_recv, yr_send, yr_recv,
):
    dm = lax.axis_index("depth")
    lm = lax.axis_index("lat")
    has = {
        (-1, 0): dm > 0,
        (1, 0): dm < depth_total - 1,
        (0, -1): lm > 0,
        (0, 1): lm < lat_total - 1,
    }
    for dz in (-1, 1):
        for dy in (-1, 1):
            has[(dz, dy)] = jnp.logical_and(has[(dz, 0)], has[(0, dy)])
    corners = [(dz, dy) for dz in (-1, 1) for dy in (-1, 1)]

    load = pltpu.make_async_copy(source, vol, load_sem)
    load.start()

    barrier = pltpu.get_barrier_semaphore()
    first_solver, solvers = lat_solvers(lat_total)

    def solves(index):
        return jnp.logical_and(index >= first_solver, index < first_solver + solvers)

    expected = jnp.int32(depth_total - 1)
    for step in range(1, lat_total):
        other = lax.rem(lm + step, lat_total)
        meets = jnp.logical_or(
            jnp.logical_or(solves(lm), solves(other)),
            jnp.logical_or(other == lm + 1, other == lm - 1),
        )
        expected = expected + meets.astype(jnp.int32)

        @pl.when(meets)
        def _():
            pl.semaphore_signal(barrier, inc=1, device_id=(dm, other), device_id_type=MESH)

    for step in range(1, depth_total):
        pl.semaphore_signal(
            barrier, inc=1, device_id=(lax.rem(dm + step, depth_total), lm), device_id_type=MESH
        )
    for dz, dy in corners:
        expected = expected + has[(dz, dy)].astype(jnp.int32)

        @pl.when(has[(dz, dy)])
        def _():
            pl.semaphore_signal(
                barrier, inc=1, device_id=(dm + dz, lm + dy), device_id_type=MESH
            )

    load.wait()
    pack_one[...] = vol[pl.ds(0, planes, stride=rows), :]
    for j in range(2):
        pack_two[pl.ds(j, planes, stride=2), :] = vol[pl.ds(rows - 2 + j, planes, stride=rows), :]
    pl.semaphore_wait(barrier, expected)

    def halo_copy(index, way):
        dz, dy = way
        zi, yi = (dz + 1) // 2, (dy + 1) // 2
        if dy == 0:
            src = vol.at[pl.ds(0, rows) if dz < 0 else pl.ds((planes - 2) * rows, 2 * rows)]
            dst = zh_one if dz < 0 else zh_two
        elif dz == 0:
            src, dst = (pack_one, yh_one) if dy < 0 else (pack_two, yh_two)
        else:
            pack, count = (pack_one, planes) if dy < 0 else (pack_two, 2 * planes)
            src = pack.at[pl.ds(0 if dz < 0 else count - 8, 8)]
            dst = cn.at[1 - zi, 1 - yi]
        return pltpu.make_async_remote_copy(
            src_ref=src,
            dst_ref=dst,
            send_sem=halo_send.at[index],
            recv_sem=halo_recv.at[index],
            device_id=(dm + dz, lm + dy),
            device_id_type=MESH,
        )

    ways = [(0, -1), (0, 1), (-1, 0), (1, 0)] + corners
    opposite = {way: ways.index((-way[0], -way[1])) for way in ways}
    for index, way in enumerate(ways):

        @pl.when(has[way])
        def _():
            halo_copy(index, way).start()

    def smooth_y(field):
        row = lax.broadcasted_iota(jnp.int32, field.shape, 0)
        before = jnp.where(row == 0, 0.0, pltpu.roll(field, 1, 0))
        after = jnp.where(row == rows - 1, 0.0, pltpu.roll(field, rows - 1, 0))
        return (before + after) + (field + field)

    def plane_at(plane):
        return pl.ds((plane + 1) * rows, rows)

    older = old = None
    for plane in range(planes + 1):
        new = None
        if plane < planes:
            where = pl.ds(plane * rows, rows)
            along_x = smooth_x(vol[where, :])
            sm_x[where, :] = along_x
            new = smooth_y(along_x)
            if plane == 0:
                sm[plane_at(-1), :] = new
        if old is not None:
            total = old + old
            total = total if older is None else total + older
            sm[plane_at(plane - 1), :] = total if new is None else total + new
        older, old = old, new
    tile = vol.shape[1]
    blocks = planes * rows // tile
    for block in range(blocks):
        where = pl.ds(block * tile, tile)
        vol_t[where, :] = vol[where, :].T

    for index, way in enumerate(ways):
        back = opposite[way]

        @pl.when(has[way])
        def _():
            halo_copy(back, ways[back]).wait_recv()

        @pl.when(jnp.logical_not(has[way]))
        def _():
            dz, dy = way
            zi, yi = (dz + 1) // 2, (dy + 1) // 2
            if dy == 0:
                ref = zh_two if dz < 0 else zh_one
                ref[...] = jnp.zeros(ref.shape, jnp.float32)
            elif dz == 0:
                ref = yh_two if dy < 0 else yh_one
                ref[...] = jnp.zeros(ref.shape, jnp.float32)
            else:
                cn[zi, yi] = jnp.zeros(cn.shape[2:], jnp.float32)

    far_x = smooth_x(zh_two[pl.ds(0, rows), :])
    low_x = smooth_x(zh_two[pl.ds(rows, rows), :])
    high_x = smooth_x(zh_one[...])
    low_y = smooth_y(low_x)
    sm[plane_at(-1), :] = sm[plane_at(-1), :] + smooth_y(far_x) + (low_y + low_y)
    sm[plane_at(0), :] = sm[plane_at(0), :] + low_y
    sm[plane_at(planes - 1), :] = sm[plane_at(planes - 1), :] + smooth_y(high_x)
    low_tile = smooth_x(cn[0, 0])
    high_tile = smooth_x(cn[1, 0])
    far_row = smooth_x(yh_two[pl.ds(0, planes, stride=2), :])
    low_row = smooth_x(yh_two[pl.ds(1, planes, stride=2), :])
    edge_row = sm_x[pl.ds(0, planes, stride=rows), :]
    yy[pl.ds(8, planes), :] = (far_row + edge_row) + (low_row + low_row)
    for where, plane_x, far_one, near_one in (
        (7, low_x, low_tile[6:7], low_tile[7:8]),
        (8 + planes, high_x, high_tile[0:1], high_tile[1:2]),
    ):
        yy[pl.ds(where, 1), :] = (far_one + plane_x[0:1]) + (near_one + near_one)
    low_side = (0, 0, low_row, low_tile[5:6], low_tile[7:8], high_tile[1:2])
    low_tile = smooth_x(cn[0, 1])
    high_tile = smooth_x(cn[1, 1])
    high_row = smooth_x(yh_one[...])
    high_side = (1, rows - 1, high_row, low_tile[6:7], low_tile[7:8], high_tile[0:1])
    for side, edge, row, two_before, before, after in (low_side, high_side):
        where = pl.ds(edge, 1)
        sm[where, :] = sm[where, :] + row[0:1] + two_before + (before + before)
        nn[side, pl.ds(8, planes), :] = row
        nn[side, pl.ds(7, 1), :] = before
        nn[side, pl.ds(8 + planes, 1), :] = after
        where = pl.ds(rows + edge, planes, stride=rows)
        ends = nn[side, pl.ds(7, planes), :] + nn[side, pl.ds(9, planes), :]
        sm[where, :] = sm[where, :] + ends + (row + row)

    def exchange(axis, src, dst, sems, total, me):
        for step in sorted(range(1, total), key=lambda step: abs(2 * step - total)):
            other = lax.rem(me + step, total)
            pltpu.make_async_remote_copy(
                src_ref=src.at[other],
                dst_ref=dst.at[me],
                send_sem=sems[0],
                recv_sem=sems[1],
                device_id=(other, lm) if axis == "depth" else (dm, other),
                device_id_type=MESH,
            ).start()
        dst[me] = src[me]

    def wait_all(ref, sem, total):
        some = ref.at[pl.ds(0, total - 1)]
        pltpu.make_async_copy(some, some, sem).wait()

    def row_smoothed(row):
        if 0 <= row < rows:
            return sm[pl.ds(rows + row, planes, stride=rows), :]
        middle = yy[pl.ds(8, planes), :]
        ends = yy[pl.ds(7, planes), :] + yy[pl.ds(9, planes), :]
        return ends + (middle + middle)

    y_couples = {}

    def y_couple(row):
        if row not in y_couples:
            value = coupling(row_smoothed(row + 1) - row_smoothed(row))
            if row == -1:
                value = value * jnp.where(has[(0, -1)], 1.0, 0.0)
            y_couples[row] = value
        return y_couples[row]

    def y_keep(row, onward, back, part):
        yw[row] = onward
        yv[row] = back
        yg[row] = part

    y_chunk = planes // solvers
    results = eliminate(
        0, rows, y_couple, lambda row: vol[pl.ds(row, planes, stride=rows), :], y_keep
    )
    for q, value in enumerate(results):
        for k in range(solvers):
            ysnd[k, pl.ds(q * y_chunk, y_chunk), :] = value[k * y_chunk : (k + 1) * y_chunk]

    def to_solver(k):
        return pltpu.make_async_remote_copy(
            src_ref=ysnd.at[k],
            dst_ref=yrcv.at[lm],
            send_sem=ys_send,
            recv_sem=ys_recv,
            device_id=(dm, first_solver + k),
            device_id_type=MESH,
        )

    def from_solver(k):
        return pltpu.make_async_remote_copy(
            src_ref=yret.at[k],
            dst_ref=yfin.at[lm - first_solver],
            send_sem=yr_send,
            recv_sem=yr_recv,
            device_id=(dm, k),
            device_id_type=MESH,
        )

    for k in range(solvers):

        @pl.when(lm != first_solver + k)
        def _():
            to_solver(k).start()

    @pl.when(solves(lm))
    def _():
        yrcv[lm] = ysnd[lm - first_solver]


    z_couples = {}

    def z_couple(plane):
        if plane not in z_couples:
            diff = sm[pl.ds((plane + 2) * rows, rows), :] - sm[pl.ds((plane + 1) * rows, rows), :]
            value = coupling(diff)
            if plane == -1:
                value = value * jnp.where(has[(-1, 0)], 1.0, 0.0)
            z_couples[plane] = value
        return z_couples[plane]

    def z_keep(plane, onward, back, part):
        zw[plane] = onward
        zv[plane] = back
        zg[plane] = part

    z_chunk = rows // depth_total
    results = eliminate(
        0, planes, z_couple, lambda plane: vol[pl.ds(plane * rows, rows), :], z_keep
    )
    for q, value in enumerate(results):
        for k in range(depth_total):
            zsnd[k, pl.ds(q * z_chunk, z_chunk), :] = value[k * z_chunk : (k + 1) * z_chunk]
    exchange("depth", zsnd, zrcv, (zs_send, zs_recv), depth_total, dm)

    for block in range(blocks):
        where = pl.ds(block * tile, tile)
        sm_t[where, :] = sm[pl.ds(rows + block * tile, tile), :].T
    cells = tile // 8
    spread = blocks * 8

    def x_at(cell):
        return pl.ds(cell, spread, stride=cells)

    def turn(field, by):
        return pltpu.roll(field.reshape(blocks, 8, tile), by, 1).reshape(spread, tile)

    x_couples = {}

    def x_couple(cell):
        if cell not in x_couples:
            if cell == -1:
                value = turn(x_couple(cells - 1), 1)
            elif cell == cells - 1:
                sub = lax.rem(lax.broadcasted_iota(jnp.int32, (spread, tile), 0), 8)
                diff = turn(sm_t[x_at(0), :], 7) - sm_t[x_at(cell), :]
                value = jnp.where(sub == 7, 0.0, coupling(diff))
            else:
                value = coupling(sm_t[x_at(cell + 1), :] - sm_t[x_at(cell), :])
            x_couples[cell] = value
        return x_couples[cell]

    def x_keep(cell, onward, back, part):
        xw[cell] = onward
        xv[cell] = back
        xg[cell] = part

    excess_low, src_low, couple, excess, src = eliminate(
        0, cells, x_couple, lambda cell: vol_t[x_at(cell), :], x_keep
    )
    diag = excess + turn(excess_low, 7) + couple
    src = src + turn(src_low, 7)
    couple = turn(couple, 7)
    diag = diag + couple
    offset = 1
    while offset < 8:
        inverse = recip(diag)
        scaled = couple * inverse
        after = couple * turn(inverse, 8 - offset)
        new_diag = diag - turn(couple * scaled, offset) - couple * after
        src = src + turn(scaled * src, offset) + couple * turn(inverse * src, 8 - offset)
        if 2 * offset < 8:
            couple = couple * turn(scaled, 8 - offset)
        diag = new_diag
        offset = offset * 2
    last = src * recip(diag)

    def x_emit(cell, value):
        x_out[x_at(cell), :] = value

    substitute(0, cells, turn(last, 1), last, lambda c: (xw[c], xv[c], xg[c]), x_emit)
    for block in range(blocks):
        where = pl.ds(block * tile, tile)
        out[where, :] = x_out[where, :].T

    def reduce_and_return(axis, rcv, ret, fin, recv, sems, total, me, chunk):
        wait_all(rcv, recv, total)
        reduce_into(rcv, ret, total, chunk)
        exchange(axis, ret, fin, sems, total, me)

    def reduce_into(rcv, ret, total, chunk):
        values = solve_reduced(
            total, chunk, lambda k, q: rcv[k, pl.ds(q * chunk, chunk), :]
        )
        for k in range(total):
            ret[k, pl.ds(0, chunk), :] = values[k - 1] if k else jnp.zeros_like(values[0])
            ret[k, pl.ds(chunk, chunk), :] = values[k]

    z_sems = (zr_send, zr_recv)
    reduce_and_return("depth", zrcv, zret, zfin, zs_recv, z_sems, depth_total, dm, z_chunk)

    @pl.when(solves(lm))
    def _():
        wait_all(yrcv, ys_recv, lat_total)
        reduce_into(yrcv, yret, lat_total, y_chunk)
        for k in sorted(range(lat_total), key=lambda k: -abs(2 * k + 1 - lat_total)):

            @pl.when(lm != k)
            def _():
                from_solver(k).start()

        yfin[lm - first_solver] = yret[lm]


    def gather(fin, sep, total, chunk):
        for k in range(total):
            for q in range(2):
                sep[q, pl.ds(k * chunk, chunk), :] = fin[k, pl.ds(q * chunk, chunk), :]

    wait_all(zfin, zr_recv, depth_total)
    gather(zfin, zsep, depth_total, z_chunk)

    def z_emit(plane, value):
        where = pl.ds(plane * rows, rows)
        out[where, :] = out[where, :] + value

    substitute(
        0, planes, zsep[0], zsep[1], lambda p: (zw[p], zv[p], zg[p]), z_emit
    )

    def wait_solvers(ref, sem):
        @pl.when(solves(lm))
        def _():
            wait_all(ref, sem, solvers)

        @pl.when(jnp.logical_not(solves(lm)))
        def _():
            wait_all(ref, sem, solvers + 1)

    wait_solvers(yfin, yr_recv)
    gather(yfin, ysep, solvers, y_chunk)

    def y_emit(row, value):
        where = pl.ds(row, planes, stride=rows)
        out[where, :] = (out[where, :] + value) * (1.0 / 3.0)

    substitute(0, rows, ysep[0], ysep[1], lambda r: (yw[r], yv[r], yg[r]), y_emit)
    wait_all(zsnd, zs_send, depth_total)
    wait_all(zret, zr_send, depth_total)
    wait_solvers(ysnd, ys_send)

    @pl.when(solves(lm))
    def _():
        wait_all(yret, yr_send, lat_total)

    for index, way in enumerate(ways):

        @pl.when(has[way])
        def _():
            halo_copy(index, way).wait_send()


def shards(depth_total, lat_total, volume):
    planes, rows, columns = volume.shape
    solvers = lat_solvers(lat_total)[1]
    y_chunk = planes // solvers
    z_chunk = rows // depth_total
    f32 = jnp.float32

    def vmem(*shape):
        return pltpu.VMEM(shape + (columns,), f32)

    def dma(count):
        return pltpu.SemaphoreType.DMA((count,))

    cells = planes * rows
    out = pl.pallas_call(
        functools.partial(kernel, depth_total, lat_total, planes, rows),
        out_shape=jax.ShapeDtypeStruct((cells, columns), f32),
        in_specs=[pl.BlockSpec(memory_space=pltpu.HBM)],
        out_specs=pl.BlockSpec(memory_space=pltpu.VMEM),
        scratch_shapes=[
            vmem(cells),
            vmem(planes),
            vmem(2 * planes),
            vmem(planes),
            vmem(2 * planes),
            vmem(rows),
            vmem(2 * rows),
            vmem(2, 2, 8),
            vmem(cells),
            vmem((planes + 1) * rows),
            vmem(planes + 16),
            vmem(2, planes + 16),
            vmem(cells),
            vmem(cells),
            vmem(cells),
            vmem(columns // 8, cells * 8 // columns),
            vmem(columns // 8, cells * 8 // columns),
            vmem(columns // 8, cells * 8 // columns),
            vmem(planes, rows),
            vmem(planes, rows),
            vmem(planes, rows),
            vmem(rows, planes),
            vmem(rows, planes),
            vmem(rows, planes),
            vmem(depth_total, 5 * z_chunk),
            vmem(depth_total, 5 * z_chunk),
            vmem(depth_total, 2 * z_chunk),
            vmem(depth_total, 2 * z_chunk),
            vmem(2, rows),
            vmem(solvers, 5 * y_chunk),
            vmem(lat_total, 5 * y_chunk),
            vmem(lat_total, 2 * y_chunk),
            vmem(solvers, 2 * y_chunk),
            vmem(2, planes),
            pltpu.SemaphoreType.DMA,
            dma(8),
            dma(8),
            pltpu.SemaphoreType.DMA,
            pltpu.SemaphoreType.DMA,
            pltpu.SemaphoreType.DMA,
            pltpu.SemaphoreType.DMA,
            pltpu.SemaphoreType.DMA,
            pltpu.SemaphoreType.DMA,
            pltpu.SemaphoreType.DMA,
            pltpu.SemaphoreType.DMA,
        ],
        compiler_params=pltpu.CompilerParams(
            collective_id=0, has_side_effects=True, vmem_limit_bytes=24 * 1024 * 1024
        ),
        cost_estimate=pl.CostEstimate(
            flops=400 * cells * columns, bytes_accessed=8 * cells * columns, transcendentals=0
        ),
    )(pltpu.with_memory_space_constraint(volume.reshape(cells, columns), pltpu.HBM))
    return out.reshape(volume.shape)


def solution(mesh):
    placed = (P("depth", "lat", None),)
    return jax.shard_map(
        functools.partial(shards, mesh.shape["depth"], mesh.shape["lat"]),
        mesh=mesh,
        in_specs=placed,
        out_specs=P("depth", "lat", None),
        check_vma=False,
    )
```

```python
import functools

import jax
import jax.numpy as jnp
from jax import lax
from jax.experimental import pallas as pl
from jax.experimental.pallas import tpu as pltpu
from jax.sharding import PartitionSpec as P

TAU = 300.0
LAMBDA = 0.5
MESH = pl.DeviceIdType.MESH
SCALE = (64.0 * LAMBDA) ** 2
LEAF = 8


def recip(value):
    guess = pl.reciprocal(value, approx=True)
    return guess * (2.0 - value * guess)


def coupling(diff):
    return (3.0 * TAU * SCALE) * recip(SCALE + diff * diff)


def smooth_x(field):
    lane = lax.broadcasted_iota(jnp.int32, field.shape, 1)
    width = field.shape[1]
    before = jnp.where(lane == 0, 0.0, pltpu.roll(field, 1, 1))
    after = jnp.where(lane == width - 1, 0.0, pltpu.roll(field, width - 1, 1))
    return (before + after) + (field + field)


def eliminate(lo, hi, couple, source, keep):
    starts = list(range(lo, hi, LEAF))
    state = []
    for start in starts:
        state.append([1.0, couple(start - 1), source(start), None, None])
    for step in range(LEAF - 1):
        for part, start in enumerate(starts):
            excess, fill, src, excess_low, src_low = state[part]
            cell = start + step
            after = couple(cell)
            inverse = recip(excess + fill + after)
            onward = after * inverse
            back = fill * inverse
            keep(cell, onward, back, src * inverse)
            add_excess = back * excess
            add_src = back * src
            state[part] = [
                1.0 + onward * excess,
                onward * fill,
                source(cell + 1) + onward * src,
                add_excess if excess_low is None else excess_low + add_excess,
                add_src if src_low is None else src_low + add_src,
            ]
    blocks = [(start, start + LEAF, part) for start, part in zip(starts, state)]
    while len(blocks) > 1:
        merged = []
        for first, second in zip(blocks[::2], blocks[1::2]):
            e1, f1, s1, el1, sl1 = first[2]
            e2, f2, s2, el2, sl2 = second[2]
            excess = e1 + el2
            src = s1 + sl2
            inverse = recip(excess + f1 + f2)
            onward = f2 * inverse
            back = f1 * inverse
            keep(first[1] - 1, onward, back, src * inverse)
            merged.append(
                (
                    first[0],
                    second[1],
                    [
                        e2 + onward * excess,
                        onward * f1,
                        s2 + onward * src,
                        el1 + back * excess,
                        sl1 + back * src,
                    ],
                )
            )
        blocks = merged
    e, f, s, el, sl = blocks[0][2]
    return el, sl, f, e, s


def substitute(lo, hi, before, last, load, emit):
    known = {lo - 1: before, hi - 1: last}
    emit(hi - 1, last)
    size = hi - lo
    while size > LEAF:
        for start in range(lo, hi, size):
            middle = start + size // 2 - 1
            onward, back, part = load(middle)
            value = part + back * known[start - 1] + onward * known[start + size - 1]
            known[middle] = value
            emit(middle, value)
        size = size // 2
    current = {start: known[start + LEAF - 1] for start in range(lo, hi, LEAF)}
    for step in range(LEAF - 2, -1, -1):
        for start in range(lo, hi, LEAF):
            onward, back, part = load(start + step)
            value = part + back * known[start - 1] + onward * current[start]
            current[start] = value
            emit(start + step, value)


def solve_reduced(count, got):
    middle = count // 2
    excess, src = [], []
    for k in range(count):
        more = k + 1 < count
        excess.append(got(k, 3) + got(k + 1, 0) if more else got(k, 3))
        src.append(got(k, 4) + got(k + 1, 1) if more else got(k, 4))
    towards, parts = {}, {}

    def fold(k, into):
        couple = got(max(k, into), 2)
        inverse = recip(excess[k] + couple)
        towards[k] = couple * inverse
        parts[k] = src[k] * inverse
        excess[into] = excess[into] + towards[k] * excess[k]
        src[into] = src[into] + towards[k] * src[k]

    for step in range(middle):
        fold(step, step + 1)
        if count - 1 - step > middle:
            fold(count - 1 - step, count - 2 - step)
    values = {middle: src[middle] * recip(excess[middle])}
    for step in range(1, middle + 1):
        values[middle - step] = parts[middle - step] + towards[middle - step] * values[middle - step + 1]
        if middle + step < count:
            values[middle + step] = (
                parts[middle + step] + towards[middle + step] * values[middle + step - 1]
            )
    return [values[k] for k in range(count)]


def lat_solvers(lat_total):
    solvers = max(lat_total // 2, 1)
    return (lat_total - solvers) // 2, solvers


def kernel(
    depth_total, lat_total, planes, rows,
    source, out,
    vol, pack_one, pack_two, yh_one, yh_two, zh_one, zh_two, cn, sm_x, sm, yy, nn,
    vol_t, sm_t, x_out, xw, xv, xg, zw, zv, zg, yw, yv, yg,
    zsnd, zrcv, zret, zfin, zsep, ysnd, yrcv, yret, yfin, ysep,
    load_sem, halo_send, halo_recv, zs_send, zs_recv, zr_send, zr_recv,
    ys_send, ys_recv, yr_send, yr_recv,
):
    dm = lax.axis_index("depth")
    lm = lax.axis_index("lat")
    has = {
        (-1, 0): dm > 0,
        (1, 0): dm < depth_total - 1,
        (0, -1): lm > 0,
        (0, 1): lm < lat_total - 1,
    }
    for dz in (-1, 1):
        for dy in (-1, 1):
            has[(dz, dy)] = jnp.logical_and(has[(dz, 0)], has[(0, dy)])
    corners = [(dz, dy) for dz in (-1, 1) for dy in (-1, 1)]

    load = pltpu.make_async_copy(source, vol, load_sem)
    load.start()

    barrier = pltpu.get_barrier_semaphore()
    first_solver, solvers = lat_solvers(lat_total)

    def solves(index):
        return jnp.logical_and(index >= first_solver, index < first_solver + solvers)

    expected = jnp.int32(depth_total - 1)
    for step in range(1, lat_total):
        other = lax.rem(lm + step, lat_total)
        meets = jnp.logical_or(
            jnp.logical_or(solves(lm), solves(other)),
            jnp.logical_or(other == lm + 1, other == lm - 1),
        )
        expected = expected + meets.astype(jnp.int32)

        @pl.when(meets)
        def _():
            pl.semaphore_signal(barrier, inc=1, device_id=(dm, other), device_id_type=MESH)

    for step in range(1, depth_total):
        pl.semaphore_signal(
            barrier, inc=1, device_id=(lax.rem(dm + step, depth_total), lm), device_id_type=MESH
        )
    for dz, dy in corners:
        expected = expected + has[(dz, dy)].astype(jnp.int32)

        @pl.when(has[(dz, dy)])
        def _():
            pl.semaphore_signal(
                barrier, inc=1, device_id=(dm + dz, lm + dy), device_id_type=MESH
            )

    load.wait()
    pack_one[...] = vol[pl.ds(0, planes, stride=rows), :]
    for j in range(2):
        pack_two[pl.ds(j, planes, stride=2), :] = vol[pl.ds(rows - 2 + j, planes, stride=rows), :]
    pl.semaphore_wait(barrier, expected)

    def halo_copy(index, way):
        dz, dy = way
        zi, yi = (dz + 1) // 2, (dy + 1) // 2
        if dy == 0:
            src = vol.at[pl.ds(0, rows) if dz < 0 else pl.ds((planes - 2) * rows, 2 * rows)]
            dst = zh_one if dz < 0 else zh_two
        elif dz == 0:
            src, dst = (pack_one, yh_one) if dy < 0 else (pack_two, yh_two)
        else:
            pack, count = (pack_one, planes) if dy < 0 else (pack_two, 2 * planes)
            src = pack.at[pl.ds(0 if dz < 0 else count - 8, 8)]
            dst = cn.at[1 - zi, 1 - yi]
        return pltpu.make_async_remote_copy(
            src_ref=src,
            dst_ref=dst,
            send_sem=halo_send.at[index],
            recv_sem=halo_recv.at[index],
            device_id=(dm + dz, lm + dy),
            device_id_type=MESH,
        )

    ways = [(0, -1), (0, 1), (-1, 0), (1, 0)] + corners
    opposite = {way: ways.index((-way[0], -way[1])) for way in ways}
    for index, way in enumerate(ways):

        @pl.when(has[way])
        def _():
            halo_copy(index, way).start()

    def smooth_y(field):
        row = lax.broadcasted_iota(jnp.int32, field.shape, 0)
        before = jnp.where(row == 0, 0.0, pltpu.roll(field, 1, 0))
        after = jnp.where(row == rows - 1, 0.0, pltpu.roll(field, rows - 1, 0))
        return (before + after) + (field + field)

    def plane_at(plane):
        return pl.ds((plane + 1) * rows, rows)

    older = old = None
    for plane in range(planes + 1):
        new = None
        if plane < planes:
            where = pl.ds(plane * rows, rows)
            along_x = smooth_x(vol[where, :])
            sm_x[where, :] = along_x
            new = smooth_y(along_x)
            if plane == 0:
                sm[plane_at(-1), :] = new
        if old is not None:
            total = old + old
            total = total if older is None else total + older
            sm[plane_at(plane - 1), :] = total if new is None else total + new
        older, old = old, new
    tile = vol.shape[1]
    blocks = planes * rows // tile
    for block in range(blocks):
        where = pl.ds(block * tile, tile)
        vol_t[where, :] = vol[where, :].T

    for index, way in enumerate(ways):
        back = opposite[way]

        @pl.when(has[way])
        def _():
            halo_copy(back, ways[back]).wait_recv()

        @pl.when(jnp.logical_not(has[way]))
        def _():
            dz, dy = way
            zi, yi = (dz + 1) // 2, (dy + 1) // 2
            if dy == 0:
                ref = zh_two if dz < 0 else zh_one
                ref[...] = jnp.zeros(ref.shape, jnp.float32)
            elif dz == 0:
                ref = yh_two if dy < 0 else yh_one
                ref[...] = jnp.zeros(ref.shape, jnp.float32)
            else:
                cn[zi, yi] = jnp.zeros(cn.shape[2:], jnp.float32)

    far_x = smooth_x(zh_two[pl.ds(0, rows), :])
    low_x = smooth_x(zh_two[pl.ds(rows, rows), :])
    high_x = smooth_x(zh_one[...])
    low_y = smooth_y(low_x)
    sm[plane_at(-1), :] = sm[plane_at(-1), :] + smooth_y(far_x) + (low_y + low_y)
    sm[plane_at(0), :] = sm[plane_at(0), :] + low_y
    sm[plane_at(planes - 1), :] = sm[plane_at(planes - 1), :] + smooth_y(high_x)
    low_tile = smooth_x(cn[0, 0])
    high_tile = smooth_x(cn[1, 0])
    far_row = smooth_x(yh_two[pl.ds(0, planes, stride=2), :])
    low_row = smooth_x(yh_two[pl.ds(1, planes, stride=2), :])
    edge_row = sm_x[pl.ds(0, planes, stride=rows), :]
    yy[pl.ds(8, planes), :] = (far_row + edge_row) + (low_row + low_row)
    for where, plane_x, far_one, near_one in (
        (7, low_x, low_tile[6:7], low_tile[7:8]),
        (8 + planes, high_x, high_tile[0:1], high_tile[1:2]),
    ):
        yy[pl.ds(where, 1), :] = (far_one + plane_x[0:1]) + (near_one + near_one)
    low_side = (0, 0, low_row, low_tile[5:6], low_tile[7:8], high_tile[1:2])
    low_tile = smooth_x(cn[0, 1])
    high_tile = smooth_x(cn[1, 1])
    high_row = smooth_x(yh_one[...])
    high_side = (1, rows - 1, high_row, low_tile[6:7], low_tile[7:8], high_tile[0:1])
    for side, edge, row, two_before, before, after in (low_side, high_side):
        where = pl.ds(edge, 1)
        sm[where, :] = sm[where, :] + row[0:1] + two_before + (before + before)
        nn[side, pl.ds(8, planes), :] = row
        nn[side, pl.ds(7, 1), :] = before
        nn[side, pl.ds(8 + planes, 1), :] = after
        where = pl.ds(rows + edge, planes, stride=rows)
        ends = nn[side, pl.ds(7, planes), :] + nn[side, pl.ds(9, planes), :]
        sm[where, :] = sm[where, :] + ends + (row + row)

    def exchange(axis, src, dst, sems, total, me):
        for step in sorted(range(1, total), key=lambda step: abs(2 * step - total)):
            other = lax.rem(me + step, total)
            pltpu.make_async_remote_copy(
                src_ref=src.at[other],
                dst_ref=dst.at[me],
                send_sem=sems[0],
                recv_sem=sems[1],
                device_id=(other, lm) if axis == "depth" else (dm, other),
                device_id_type=MESH,
            ).start()
        dst[me] = src[me]

    def wait_all(ref, sem, total):
        some = ref.at[pl.ds(0, total - 1)]
        pltpu.make_async_copy(some, some, sem).wait()

    def row_smoothed(row):
        if 0 <= row < rows:
            return sm[pl.ds(rows + row, planes, stride=rows), :]
        middle = yy[pl.ds(8, planes), :]
        ends = yy[pl.ds(7, planes), :] + yy[pl.ds(9, planes), :]
        return ends + (middle + middle)

    y_couples = {}

    def y_couple(row):
        if row not in y_couples:
            value = coupling(row_smoothed(row + 1) - row_smoothed(row))
            if row == -1:
                value = value * jnp.where(has[(0, -1)], 1.0, 0.0)
            y_couples[row] = value
        return y_couples[row]

    def y_keep(row, onward, back, part):
        yw[row] = onward
        yv[row] = back
        yg[row] = part

    y_chunk = planes // solvers
    results = eliminate(
        0, rows, y_couple, lambda row: vol[pl.ds(row, planes, stride=rows), :], y_keep
    )
    for q, value in enumerate(results):
        for k in range(solvers):
            ysnd[k, pl.ds(q * y_chunk, y_chunk), :] = value[k * y_chunk : (k + 1) * y_chunk]

    def to_solver(k):
        return pltpu.make_async_remote_copy(
            src_ref=ysnd.at[k],
            dst_ref=yrcv.at[lm],
            send_sem=ys_send,
            recv_sem=ys_recv,
            device_id=(dm, first_solver + k),
            device_id_type=MESH,
        )

    def from_solver(k):
        return pltpu.make_async_remote_copy(
            src_ref=yret.at[k],
            dst_ref=yfin.at[lm - first_solver],
            send_sem=yr_send,
            recv_sem=yr_recv,
            device_id=(dm, k),
            device_id_type=MESH,
        )

    for k in range(solvers):

        @pl.when(lm != first_solver + k)
        def _():
            to_solver(k).start()

    @pl.when(solves(lm))
    def _():
        yrcv[lm] = ysnd[lm - first_solver]


    z_couples = {}

    def z_couple(plane):
        if plane not in z_couples:
            diff = sm[pl.ds((plane + 2) * rows, rows), :] - sm[pl.ds((plane + 1) * rows, rows), :]
            value = coupling(diff)
            if plane == -1:
                value = value * jnp.where(has[(-1, 0)], 1.0, 0.0)
            z_couples[plane] = value
        return z_couples[plane]

    def z_keep(plane, onward, back, part):
        zw[plane] = onward
        zv[plane] = back
        zg[plane] = part

    z_chunk = rows // depth_total
    results = eliminate(
        0, planes, z_couple, lambda plane: vol[pl.ds(plane * rows, rows), :], z_keep
    )
    for q, value in enumerate(results):
        for k in range(depth_total):
            zsnd[k, pl.ds(q * z_chunk, z_chunk), :] = value[k * z_chunk : (k + 1) * z_chunk]
    exchange("depth", zsnd, zrcv, (zs_send, zs_recv), depth_total, dm)

    for block in range(blocks):
        where = pl.ds(block * tile, tile)
        sm_t[where, :] = sm[pl.ds(rows + block * tile, tile), :].T
    cells = tile // 8
    spread = blocks * 8

    def x_at(cell):
        return pl.ds(cell, spread, stride=cells)

    def turn(field, by):
        return pltpu.roll(field.reshape(blocks, 8, tile), by, 1).reshape(spread, tile)

    x_couples = {}

    def x_couple(cell):
        if cell not in x_couples:
            if cell == -1:
                value = turn(x_couple(cells - 1), 1)
            elif cell == cells - 1:
                sub = lax.rem(lax.broadcasted_iota(jnp.int32, (spread, tile), 0), 8)
                diff = turn(sm_t[x_at(0), :], 7) - sm_t[x_at(cell), :]
                value = jnp.where(sub == 7, 0.0, coupling(diff))
            else:
                value = coupling(sm_t[x_at(cell + 1), :] - sm_t[x_at(cell), :])
            x_couples[cell] = value
        return x_couples[cell]

    def x_keep(cell, onward, back, part):
        xw[cell] = onward
        xv[cell] = back
        xg[cell] = part

    excess_low, src_low, couple, excess, src = eliminate(
        0, cells, x_couple, lambda cell: vol_t[x_at(cell), :], x_keep
    )
    x_ends = (excess_low, src_low, couple, excess, src)

    def reduce_and_return(axis, rcv, ret, fin, recv, sems, total, me, chunk):
        wait_all(rcv, recv, total)
        reduce_into(rcv, ret, total, chunk)
        exchange(axis, ret, fin, sems, total, me)

    def reduce_into(rcv, ret, total, chunk):
        values = solve_reduced(total, lambda k, q: rcv[k, pl.ds(q * chunk, chunk), :])
        for k in range(total):
            ret[k, pl.ds(0, chunk), :] = values[k - 1] if k else jnp.zeros_like(values[0])
            ret[k, pl.ds(chunk, chunk), :] = values[k]

    z_sems = (zr_send, zr_recv)
    reduce_and_return("depth", zrcv, zret, zfin, zs_recv, z_sems, depth_total, dm, z_chunk)

    @pl.when(solves(lm))
    def _():
        wait_all(yrcv, ys_recv, lat_total)
        reduce_into(yrcv, yret, lat_total, y_chunk)
        for k in sorted(range(lat_total), key=lambda k: -abs(2 * k + 1 - lat_total)):

            @pl.when(lm != k)
            def _():
                from_solver(k).start()

        yfin[lm - first_solver] = yret[lm]


    def gather(fin, sep, total, chunk):
        for k in range(total):
            for q in range(2):
                sep[q, pl.ds(k * chunk, chunk), :] = fin[k, pl.ds(q * chunk, chunk), :]

    excess_low, src_low, couple, excess, src = x_ends
    diag = excess + turn(excess_low, 7) + couple
    src = src + turn(src_low, 7)
    couple = turn(couple, 7)
    diag = diag + couple
    offset = 1
    while offset < 8:
        inverse = recip(diag)
        scaled = couple * inverse
        after = couple * turn(inverse, 8 - offset)
        new_diag = diag - turn(couple * scaled, offset) - couple * after
        src = src + turn(scaled * src, offset) + couple * turn(inverse * src, 8 - offset)
        if 2 * offset < 8:
            couple = couple * turn(scaled, 8 - offset)
        diag = new_diag
        offset = offset * 2
    last = src * recip(diag)

    def x_emit(cell, value):
        x_out[x_at(cell), :] = value

    substitute(0, cells, turn(last, 1), last, lambda c: (xw[c], xv[c], xg[c]), x_emit)
    for block in range(blocks):
        where = pl.ds(block * tile, tile)
        out[where, :] = x_out[where, :].T

    wait_all(zfin, zr_recv, depth_total)
    gather(zfin, zsep, depth_total, z_chunk)

    def z_emit(plane, value):
        where = pl.ds(plane * rows, rows)
        out[where, :] = out[where, :] + value

    substitute(
        0, planes, zsep[0], zsep[1], lambda p: (zw[p], zv[p], zg[p]), z_emit
    )

    def wait_solvers(ref, sem):
        @pl.when(solves(lm))
        def _():
            wait_all(ref, sem, solvers)

        @pl.when(jnp.logical_not(solves(lm)))
        def _():
            wait_all(ref, sem, solvers + 1)

    wait_solvers(yfin, yr_recv)
    gather(yfin, ysep, solvers, y_chunk)

    def y_emit(row, value):
        where = pl.ds(row, planes, stride=rows)
        out[where, :] = (out[where, :] + value) * (1.0 / 3.0)

    substitute(0, rows, ysep[0], ysep[1], lambda r: (yw[r], yv[r], yg[r]), y_emit)
    wait_all(zsnd, zs_send, depth_total)
    wait_all(zret, zr_send, depth_total)
    wait_solvers(ysnd, ys_send)

    @pl.when(solves(lm))
    def _():
        wait_all(yret, yr_send, lat_total)

    for index, way in enumerate(ways):

        @pl.when(has[way])
        def _():
            halo_copy(index, way).wait_send()


def shards(depth_total, lat_total, volume):
    planes, rows, columns = volume.shape
    solvers = lat_solvers(lat_total)[1]
    y_chunk = planes // solvers
    z_chunk = rows // depth_total
    f32 = jnp.float32

    def vmem(*shape):
        return pltpu.VMEM(shape + (columns,), f32)

    def dma(count):
        return pltpu.SemaphoreType.DMA((count,))

    cells = planes * rows
    out = pl.pallas_call(
        functools.partial(kernel, depth_total, lat_total, planes, rows),
        out_shape=jax.ShapeDtypeStruct((cells, columns), f32),
        in_specs=[pl.BlockSpec(memory_space=pltpu.HBM)],
        out_specs=pl.BlockSpec(memory_space=pltpu.VMEM),
        scratch_shapes=[
            vmem(cells),
            vmem(planes),
            vmem(2 * planes),
            vmem(planes),
            vmem(2 * planes),
            vmem(rows),
            vmem(2 * rows),
            vmem(2, 2, 8),
            vmem(cells),
            vmem((planes + 1) * rows),
            vmem(planes + 16),
            vmem(2, planes + 16),
            vmem(cells),
            vmem(cells),
            vmem(cells),
            vmem(columns // 8, cells * 8 // columns),
            vmem(columns // 8, cells * 8 // columns),
            vmem(columns // 8, cells * 8 // columns),
            vmem(planes, rows),
            vmem(planes, rows),
            vmem(planes, rows),
            vmem(rows, planes),
            vmem(rows, planes),
            vmem(rows, planes),
            vmem(depth_total, 5 * z_chunk),
            vmem(depth_total, 5 * z_chunk),
            vmem(depth_total, 2 * z_chunk),
            vmem(depth_total, 2 * z_chunk),
            vmem(2, rows),
            vmem(solvers, 5 * y_chunk),
            vmem(lat_total, 5 * y_chunk),
            vmem(lat_total, 2 * y_chunk),
            vmem(solvers, 2 * y_chunk),
            vmem(2, planes),
            pltpu.SemaphoreType.DMA,
            dma(8),
            dma(8),
            pltpu.SemaphoreType.DMA,
            pltpu.SemaphoreType.DMA,
            pltpu.SemaphoreType.DMA,
            pltpu.SemaphoreType.DMA,
            pltpu.SemaphoreType.DMA,
            pltpu.SemaphoreType.DMA,
            pltpu.SemaphoreType.DMA,
            pltpu.SemaphoreType.DMA,
        ],
        compiler_params=pltpu.CompilerParams(
            collective_id=0, has_side_effects=True, vmem_limit_bytes=24 * 1024 * 1024
        ),
        cost_estimate=pl.CostEstimate(
            flops=400 * cells * columns, bytes_accessed=8 * cells * columns, transcendentals=0
        ),
    )(pltpu.with_memory_space_constraint(volume.reshape(cells, columns), pltpu.HBM))
    return out.reshape(volume.shape)


def solution(mesh):
    placed = (P("depth", "lat", None),)
    return jax.shard_map(
        functools.partial(shards, mesh.shape["depth"], mesh.shape["lat"]),
        mesh=mesh,
        in_specs=placed,
        out_specs=P("depth", "lat", None),
        check_vma=False,
    )
```

```python
import functools

import jax
import jax.numpy as jnp
from jax import lax
from jax.experimental import pallas as pl
from jax.experimental.pallas import tpu as pltpu
from jax.sharding import PartitionSpec as P

TAU = 300.0
LAMBDA = 0.5
MESH = pl.DeviceIdType.MESH
SCALE = (64.0 * LAMBDA) ** 2
LEAF = 8


def recip(value):
    guess = pl.reciprocal(value, approx=True)
    return guess * (2.0 - value * guess)


def coupling(diff):
    return (3.0 * TAU * SCALE) * recip(SCALE + diff * diff)


def smooth_x(field):
    lane = lax.broadcasted_iota(jnp.int32, field.shape, 1)
    width = field.shape[1]
    before = jnp.where(lane == 0, 0.0, pltpu.roll(field, 1, 1))
    after = jnp.where(lane == width - 1, 0.0, pltpu.roll(field, width - 1, 1))
    return (before + after) + (field + field)


def eliminate(lo, hi, couple, source, keep):
    starts = list(range(lo, hi, LEAF))
    state = []
    for start in starts:
        state.append([1.0, couple(start - 1), source(start), None, None])
    for step in range(LEAF - 1):
        for part, start in enumerate(starts):
            excess, fill, src, excess_low, src_low = state[part]
            cell = start + step
            after = couple(cell)
            inverse = recip(excess + fill + after)
            onward = after * inverse
            back = fill * inverse
            keep(cell, onward, back, src * inverse)
            add_excess = back * excess
            add_src = back * src
            state[part] = [
                1.0 + onward * excess,
                onward * fill,
                source(cell + 1) + onward * src,
                add_excess if excess_low is None else excess_low + add_excess,
                add_src if src_low is None else src_low + add_src,
            ]
    blocks = [(start, start + LEAF, part) for start, part in zip(starts, state)]
    while len(blocks) > 1:
        merged = []
        for first, second in zip(blocks[::2], blocks[1::2]):
            e1, f1, s1, el1, sl1 = first[2]
            e2, f2, s2, el2, sl2 = second[2]
            excess = e1 + el2
            src = s1 + sl2
            inverse = recip(excess + f1 + f2)
            onward = f2 * inverse
            back = f1 * inverse
            keep(first[1] - 1, onward, back, src * inverse)
            merged.append(
                (
                    first[0],
                    second[1],
                    [
                        e2 + onward * excess,
                        onward * f1,
                        s2 + onward * src,
                        el1 + back * excess,
                        sl1 + back * src,
                    ],
                )
            )
        blocks = merged
    e, f, s, el, sl = blocks[0][2]
    return el, sl, f, e, s


def substitute(lo, hi, before, last, load, emit):
    known = {lo - 1: before, hi - 1: last}
    emit(hi - 1, last)
    size = hi - lo
    while size > LEAF:
        for start in range(lo, hi, size):
            middle = start + size // 2 - 1
            onward, back, part = load(middle)
            value = part + back * known[start - 1] + onward * known[start + size - 1]
            known[middle] = value
            emit(middle, value)
        size = size // 2
    current = {start: known[start + LEAF - 1] for start in range(lo, hi, LEAF)}
    for step in range(LEAF - 2, -1, -1):
        for start in range(lo, hi, LEAF):
            onward, back, part = load(start + step)
            value = part + back * known[start - 1] + onward * current[start]
            current[start] = value
            emit(start + step, value)


def solve_reduced(count, got):
    middle = count // 2
    excess, src = [], []
    for k in range(count):
        more = k + 1 < count
        excess.append(got(k, 3) + got(k + 1, 0) if more else got(k, 3))
        src.append(got(k, 4) + got(k + 1, 1) if more else got(k, 4))
    towards, parts = {}, {}

    def fold(k, into):
        couple = got(max(k, into), 2)
        inverse = recip(excess[k] + couple)
        towards[k] = couple * inverse
        parts[k] = src[k] * inverse
        excess[into] = excess[into] + towards[k] * excess[k]
        src[into] = src[into] + towards[k] * src[k]

    for step in range(middle):
        fold(step, step + 1)
        if count - 1 - step > middle:
            fold(count - 1 - step, count - 2 - step)
    values = {middle: src[middle] * recip(excess[middle])}
    for step in range(1, middle + 1):
        values[middle - step] = parts[middle - step] + towards[middle - step] * values[middle - step + 1]
        if middle + step < count:
            values[middle + step] = (
                parts[middle + step] + towards[middle + step] * values[middle + step - 1]
            )
    return [values[k] for k in range(count)]


def lat_solvers(lat_total):
    solvers = max(lat_total // 2, 1)
    return (lat_total - solvers) // 2, solvers


def kernel(
    depth_total, lat_total, planes, rows,
    source, out,
    vol, pack_one, pack_two, yh_one, yh_two, zh_one, zh_two, cn, sm_x, sm, yy, nn,
    vol_y, sm_y, part_y,
    vol_t, sm_t, x_out, xw, xv, xg, zw, zv, zg, yw, yv, yg,
    zsnd, zrcv, zret, zfin, zsep, ysnd, yrcv, yret, yfin, ysep,
    load_sem, halo_send, halo_recv, zs_send, zs_recv, zr_send, zr_recv,
    ys_send, ys_recv, yr_send, yr_recv,
):
    dm = lax.axis_index("depth")
    lm = lax.axis_index("lat")
    has = {
        (-1, 0): dm > 0,
        (1, 0): dm < depth_total - 1,
        (0, -1): lm > 0,
        (0, 1): lm < lat_total - 1,
    }
    for dz in (-1, 1):
        for dy in (-1, 1):
            has[(dz, dy)] = jnp.logical_and(has[(dz, 0)], has[(0, dy)])
    corners = [(dz, dy) for dz in (-1, 1) for dy in (-1, 1)]

    load = pltpu.make_async_copy(source, vol, load_sem)
    load.start()

    barrier = pltpu.get_barrier_semaphore()
    first_solver, solvers = lat_solvers(lat_total)

    def solves(index):
        return jnp.logical_and(index >= first_solver, index < first_solver + solvers)

    expected = jnp.int32(depth_total - 1)
    for step in range(1, lat_total):
        other = lax.rem(lm + step, lat_total)
        meets = jnp.logical_or(
            jnp.logical_or(solves(lm), solves(other)),
            jnp.logical_or(other == lm + 1, other == lm - 1),
        )
        expected = expected + meets.astype(jnp.int32)

        @pl.when(meets)
        def _():
            pl.semaphore_signal(barrier, inc=1, device_id=(dm, other), device_id_type=MESH)

    for step in range(1, depth_total):
        pl.semaphore_signal(
            barrier, inc=1, device_id=(lax.rem(dm + step, depth_total), lm), device_id_type=MESH
        )
    for dz, dy in corners:
        expected = expected + has[(dz, dy)].astype(jnp.int32)

        @pl.when(has[(dz, dy)])
        def _():
            pl.semaphore_signal(
                barrier, inc=1, device_id=(dm + dz, lm + dy), device_id_type=MESH
            )

    load.wait()
    pack_one[...] = vol[pl.ds(0, planes, stride=rows), :]
    for j in range(2):
        pack_two[pl.ds(j, planes, stride=2), :] = vol[pl.ds(rows - 2 + j, planes, stride=rows), :]
    pl.semaphore_wait(barrier, expected)

    def halo_copy(index, way):
        dz, dy = way
        zi, yi = (dz + 1) // 2, (dy + 1) // 2
        if dy == 0:
            src = vol.at[pl.ds(0, rows) if dz < 0 else pl.ds((planes - 2) * rows, 2 * rows)]
            dst = zh_one if dz < 0 else zh_two
        elif dz == 0:
            src, dst = (pack_one, yh_one) if dy < 0 else (pack_two, yh_two)
        else:
            pack, count = (pack_one, planes) if dy < 0 else (pack_two, 2 * planes)
            src = pack.at[pl.ds(0 if dz < 0 else count - 8, 8)]
            dst = cn.at[1 - zi, 1 - yi]
        return pltpu.make_async_remote_copy(
            src_ref=src,
            dst_ref=dst,
            send_sem=halo_send.at[index],
            recv_sem=halo_recv.at[index],
            device_id=(dm + dz, lm + dy),
            device_id_type=MESH,
        )

    ways = [(0, -1), (0, 1), (-1, 0), (1, 0)] + corners
    opposite = {way: ways.index((-way[0], -way[1])) for way in ways}
    for index, way in enumerate(ways):

        @pl.when(has[way])
        def _():
            halo_copy(index, way).start()

    def smooth_y(field):
        row = lax.broadcasted_iota(jnp.int32, field.shape, 0)
        before = jnp.where(row == 0, 0.0, pltpu.roll(field, 1, 0))
        after = jnp.where(row == rows - 1, 0.0, pltpu.roll(field, rows - 1, 0))
        return (before + after) + (field + field)

    def plane_at(plane):
        return pl.ds((plane + 1) * rows, rows)

    older = old = None
    for plane in range(planes + 1):
        new = None
        if plane < planes:
            where = pl.ds(plane * rows, rows)
            along_x = smooth_x(vol[where, :])
            sm_x[where, :] = along_x
            new = smooth_y(along_x)
            if plane == 0:
                sm[plane_at(-1), :] = new
        if old is not None:
            total = old + old
            total = total if older is None else total + older
            sm[plane_at(plane - 1), :] = total if new is None else total + new
        older, old = old, new
    def row_at(row):
        return pl.ds(row * planes, planes)

    for row in range(rows):
        vol_y[row_at(row), :] = vol[pl.ds(row, planes, stride=rows), :]
        sm_y[row_at(row), :] = sm[pl.ds(rows + row, planes, stride=rows), :]

    for index, way in enumerate(ways):
        back = opposite[way]

        @pl.when(has[way])
        def _():
            halo_copy(back, ways[back]).wait_recv()

        @pl.when(jnp.logical_not(has[way]))
        def _():
            dz, dy = way
            zi, yi = (dz + 1) // 2, (dy + 1) // 2
            if dy == 0:
                ref = zh_two if dz < 0 else zh_one
                ref[...] = jnp.zeros(ref.shape, jnp.float32)
            elif dz == 0:
                ref = yh_two if dy < 0 else yh_one
                ref[...] = jnp.zeros(ref.shape, jnp.float32)
            else:
                cn[zi, yi] = jnp.zeros(cn.shape[2:], jnp.float32)

    far_x = smooth_x(zh_two[pl.ds(0, rows), :])
    low_x = smooth_x(zh_two[pl.ds(rows, rows), :])
    high_x = smooth_x(zh_one[...])
    low_y = smooth_y(low_x)
    sm[plane_at(-1), :] = sm[plane_at(-1), :] + smooth_y(far_x) + (low_y + low_y)
    sm[plane_at(0), :] = sm[plane_at(0), :] + low_y
    high_y = smooth_y(high_x)
    sm[plane_at(planes - 1), :] = sm[plane_at(planes - 1), :] + high_y
    for plane, change in ((0, low_y), (planes - 1, high_y)):
        where = pl.ds(plane, rows, stride=planes)
        sm_y[where, :] = sm_y[where, :] + change
    low_tile = smooth_x(cn[0, 0])
    high_tile = smooth_x(cn[1, 0])
    far_row = smooth_x(yh_two[pl.ds(0, planes, stride=2), :])
    low_row = smooth_x(yh_two[pl.ds(1, planes, stride=2), :])
    edge_row = sm_x[pl.ds(0, planes, stride=rows), :]
    yy[pl.ds(8, planes), :] = (far_row + edge_row) + (low_row + low_row)
    for where, plane_x, far_one, near_one in (
        (7, low_x, low_tile[6:7], low_tile[7:8]),
        (8 + planes, high_x, high_tile[0:1], high_tile[1:2]),
    ):
        yy[pl.ds(where, 1), :] = (far_one + plane_x[0:1]) + (near_one + near_one)
    low_side = (0, 0, low_row, low_tile[5:6], low_tile[7:8], high_tile[1:2])
    low_tile = smooth_x(cn[0, 1])
    high_tile = smooth_x(cn[1, 1])
    high_row = smooth_x(yh_one[...])
    high_side = (1, rows - 1, high_row, low_tile[6:7], low_tile[7:8], high_tile[0:1])
    for side, edge, row, two_before, before, after in (low_side, high_side):
        where = pl.ds(edge, 1)
        sm[where, :] = sm[where, :] + row[0:1] + two_before + (before + before)
        nn[side, pl.ds(8, planes), :] = row
        nn[side, pl.ds(7, 1), :] = before
        nn[side, pl.ds(8 + planes, 1), :] = after
        where = pl.ds(rows + edge, planes, stride=rows)
        ends = nn[side, pl.ds(7, planes), :] + nn[side, pl.ds(9, planes), :]
        change = ends + (row + row)
        sm[where, :] = sm[where, :] + change
        sm_y[row_at(edge), :] = sm_y[row_at(edge), :] + change

    def exchange(axis, src, dst, sems, total, me):
        for step in sorted(range(1, total), key=lambda step: abs(2 * step - total)):
            other = lax.rem(me + step, total)
            pltpu.make_async_remote_copy(
                src_ref=src.at[other],
                dst_ref=dst.at[me],
                send_sem=sems[0],
                recv_sem=sems[1],
                device_id=(other, lm) if axis == "depth" else (dm, other),
                device_id_type=MESH,
            ).start()
        dst[me] = src[me]

    def wait_all(ref, sem, total):
        some = ref.at[pl.ds(0, total - 1)]
        pltpu.make_async_copy(some, some, sem).wait()

    def row_smoothed(row):
        if row >= 0:
            return sm_y[row_at(row), :]
        middle = yy[pl.ds(8, planes), :]
        ends = yy[pl.ds(7, planes), :] + yy[pl.ds(9, planes), :]
        return ends + (middle + middle)

    y_couples = {}

    def y_couple(row):
        if row not in y_couples:
            value = coupling(row_smoothed(row + 1) - row_smoothed(row))
            if row == -1:
                value = value * jnp.where(has[(0, -1)], 1.0, 0.0)
            y_couples[row] = value
        return y_couples[row]

    def y_keep(row, onward, back, part):
        yw[row] = onward
        yv[row] = back
        yg[row] = part

    y_chunk = planes // solvers
    results = eliminate(
        0, rows, y_couple, lambda row: vol_y[row_at(row), :], y_keep
    )
    for q, value in enumerate(results):
        for k in range(solvers):
            ysnd[k, pl.ds(q * y_chunk, y_chunk), :] = value[k * y_chunk : (k + 1) * y_chunk]

    def to_solver(k):
        return pltpu.make_async_remote_copy(
            src_ref=ysnd.at[k],
            dst_ref=yrcv.at[lm],
            send_sem=ys_send,
            recv_sem=ys_recv,
            device_id=(dm, first_solver + k),
            device_id_type=MESH,
        )

    def from_solver(k):
        return pltpu.make_async_remote_copy(
            src_ref=yret.at[k],
            dst_ref=yfin.at[lm - first_solver],
            send_sem=yr_send,
            recv_sem=yr_recv,
            device_id=(dm, k),
            device_id_type=MESH,
        )

    for k in range(solvers):

        @pl.when(lm != first_solver + k)
        def _():
            to_solver(k).start()

    @pl.when(solves(lm))
    def _():
        yrcv[lm] = ysnd[lm - first_solver]


    z_couples = {}

    def z_couple(plane):
        if plane not in z_couples:
            diff = sm[pl.ds((plane + 2) * rows, rows), :] - sm[pl.ds((plane + 1) * rows, rows), :]
            value = coupling(diff)
            if plane == -1:
                value = value * jnp.where(has[(-1, 0)], 1.0, 0.0)
            z_couples[plane] = value
        return z_couples[plane]

    def z_keep(plane, onward, back, part):
        zw[plane] = onward
        zv[plane] = back
        zg[plane] = part

    z_chunk = rows // depth_total
    results = eliminate(
        0, planes, z_couple, lambda plane: vol[pl.ds(plane * rows, rows), :], z_keep
    )
    for q, value in enumerate(results):
        for k in range(depth_total):
            zsnd[k, pl.ds(q * z_chunk, z_chunk), :] = value[k * z_chunk : (k + 1) * z_chunk]
    exchange("depth", zsnd, zrcv, (zs_send, zs_recv), depth_total, dm)

    tile = vol.shape[1]
    blocks = planes * rows // tile
    for block in range(blocks):
        where = pl.ds(block * tile, tile)
        vol_t[where, :] = vol[where, :].T
        sm_t[where, :] = sm[pl.ds(rows + block * tile, tile), :].T
    cells = tile // 8
    spread = blocks * 8

    def x_at(cell):
        return pl.ds(cell, spread, stride=cells)

    def turn(field, by):
        return pltpu.roll(field.reshape(blocks, 8, tile), by, 1).reshape(spread, tile)

    x_couples = {}

    def x_couple(cell):
        if cell not in x_couples:
            if cell == -1:
                value = turn(x_couple(cells - 1), 1)
            elif cell == cells - 1:
                sub = lax.rem(lax.broadcasted_iota(jnp.int32, (spread, tile), 0), 8)
                diff = turn(sm_t[x_at(0), :], 7) - sm_t[x_at(cell), :]
                value = jnp.where(sub == 7, 0.0, coupling(diff))
            else:
                value = coupling(sm_t[x_at(cell + 1), :] - sm_t[x_at(cell), :])
            x_couples[cell] = value
        return x_couples[cell]

    def x_keep(cell, onward, back, part):
        xw[cell] = onward
        xv[cell] = back
        xg[cell] = part

    excess_low, src_low, couple, excess, src = eliminate(
        0, cells, x_couple, lambda cell: vol_t[x_at(cell), :], x_keep
    )
    x_ends = (excess_low, src_low, couple, excess, src)

    def reduce_and_return(axis, rcv, ret, fin, recv, sems, total, me, chunk):
        wait_all(rcv, recv, total)
        reduce_into(rcv, ret, total, chunk)
        exchange(axis, ret, fin, sems, total, me)

    def reduce_into(rcv, ret, total, chunk):
        values = solve_reduced(total, lambda k, q: rcv[k, pl.ds(q * chunk, chunk), :])
        for k in range(total):
            ret[k, pl.ds(0, chunk), :] = values[k - 1] if k else jnp.zeros_like(values[0])
            ret[k, pl.ds(chunk, chunk), :] = values[k]

    z_sems = (zr_send, zr_recv)
    reduce_and_return("depth", zrcv, zret, zfin, zs_recv, z_sems, depth_total, dm, z_chunk)

    @pl.when(solves(lm))
    def _():
        wait_all(yrcv, ys_recv, lat_total)
        reduce_into(yrcv, yret, lat_total, y_chunk)
        for k in sorted(range(lat_total), key=lambda k: -abs(2 * k + 1 - lat_total)):

            @pl.when(lm != k)
            def _():
                from_solver(k).start()

        yfin[lm - first_solver] = yret[lm]


    def gather(fin, sep, total, chunk):
        for k in range(total):
            for q in range(2):
                sep[q, pl.ds(k * chunk, chunk), :] = fin[k, pl.ds(q * chunk, chunk), :]

    excess_low, src_low, couple, excess, src = x_ends
    diag = excess + turn(excess_low, 7) + couple
    src = src + turn(src_low, 7)
    couple = turn(couple, 7)
    diag = diag + couple
    offset = 1
    while offset < 8:
        inverse = recip(diag)
        scaled = couple * inverse
        after = couple * turn(inverse, 8 - offset)
        new_diag = diag - turn(couple * scaled, offset) - couple * after
        src = src + turn(scaled * src, offset) + couple * turn(inverse * src, 8 - offset)
        if 2 * offset < 8:
            couple = couple * turn(scaled, 8 - offset)
        diag = new_diag
        offset = offset * 2
    last = src * recip(diag)

    def x_emit(cell, value):
        x_out[x_at(cell), :] = value

    substitute(0, cells, turn(last, 1), last, lambda c: (xw[c], xv[c], xg[c]), x_emit)
    for block in range(blocks):
        where = pl.ds(block * tile, tile)
        out[where, :] = x_out[where, :].T

    wait_all(zfin, zr_recv, depth_total)
    gather(zfin, zsep, depth_total, z_chunk)

    def z_emit(plane, value):
        where = pl.ds(plane * rows, rows)
        out[where, :] = out[where, :] + value

    substitute(
        0, planes, zsep[0], zsep[1], lambda p: (zw[p], zv[p], zg[p]), z_emit
    )

    for row in range(rows):
        part_y[row_at(row), :] = out[pl.ds(row, planes, stride=rows), :] * (1.0 / 3.0)

    def wait_solvers(ref, sem):
        @pl.when(solves(lm))
        def _():
            wait_all(ref, sem, solvers)

        @pl.when(jnp.logical_not(solves(lm)))
        def _():
            wait_all(ref, sem, solvers + 1)

    wait_solvers(yfin, yr_recv)
    gather(yfin, ysep, solvers, y_chunk)

    def y_emit(row, value):
        out[pl.ds(row, planes, stride=rows), :] = part_y[row_at(row), :] + value * (1.0 / 3.0)

    substitute(0, rows, ysep[0], ysep[1], lambda r: (yw[r], yv[r], yg[r]), y_emit)
    wait_all(zsnd, zs_send, depth_total)
    wait_all(zret, zr_send, depth_total)
    wait_solvers(ysnd, ys_send)

    @pl.when(solves(lm))
    def _():
        wait_all(yret, yr_send, lat_total)

    for index, way in enumerate(ways):

        @pl.when(has[way])
        def _():
            halo_copy(index, way).wait_send()


def shards(depth_total, lat_total, volume):
    planes, rows, columns = volume.shape
    solvers = lat_solvers(lat_total)[1]
    y_chunk = planes // solvers
    z_chunk = rows // depth_total
    f32 = jnp.float32

    def vmem(*shape):
        return pltpu.VMEM(shape + (columns,), f32)

    def dma(count):
        return pltpu.SemaphoreType.DMA((count,))

    cells = planes * rows
    out = pl.pallas_call(
        functools.partial(kernel, depth_total, lat_total, planes, rows),
        out_shape=jax.ShapeDtypeStruct((cells, columns), f32),
        in_specs=[pl.BlockSpec(memory_space=pltpu.HBM)],
        out_specs=pl.BlockSpec(memory_space=pltpu.VMEM),
        scratch_shapes=[
            vmem(cells),
            vmem(planes),
            vmem(2 * planes),
            vmem(planes),
            vmem(2 * planes),
            vmem(rows),
            vmem(2 * rows),
            vmem(2, 2, 8),
            vmem(cells),
            vmem((planes + 1) * rows),
            vmem(planes + 16),
            vmem(2, planes + 16),
            vmem(cells),
            vmem(cells),
            vmem(cells),
            vmem(cells),
            vmem(cells),
            vmem(cells),
            vmem(columns // 8, cells * 8 // columns),
            vmem(columns // 8, cells * 8 // columns),
            vmem(columns // 8, cells * 8 // columns),
            vmem(planes, rows),
            vmem(planes, rows),
            vmem(planes, rows),
            vmem(rows, planes),
            vmem(rows, planes),
            vmem(rows, planes),
            vmem(depth_total, 5 * z_chunk),
            vmem(depth_total, 5 * z_chunk),
            vmem(depth_total, 2 * z_chunk),
            vmem(depth_total, 2 * z_chunk),
            vmem(2, rows),
            vmem(solvers, 5 * y_chunk),
            vmem(lat_total, 5 * y_chunk),
            vmem(lat_total, 2 * y_chunk),
            vmem(solvers, 2 * y_chunk),
            vmem(2, planes),
            pltpu.SemaphoreType.DMA,
            dma(8),
            dma(8),
            pltpu.SemaphoreType.DMA,
            pltpu.SemaphoreType.DMA,
            pltpu.SemaphoreType.DMA,
            pltpu.SemaphoreType.DMA,
            pltpu.SemaphoreType.DMA,
            pltpu.SemaphoreType.DMA,
            pltpu.SemaphoreType.DMA,
            pltpu.SemaphoreType.DMA,
        ],
        compiler_params=pltpu.CompilerParams(
            collective_id=0, has_side_effects=True, vmem_limit_bytes=24 * 1024 * 1024
        ),
        cost_estimate=pl.CostEstimate(
            flops=400 * cells * columns, bytes_accessed=8 * cells * columns, transcendentals=0
        ),
    )(pltpu.with_memory_space_constraint(volume.reshape(cells, columns), pltpu.HBM))
    return out.reshape(volume.shape)


def solution(mesh):
    placed = (P("depth", "lat", None),)
    return jax.shard_map(
        functools.partial(shards, mesh.shape["depth"], mesh.shape["lat"]),
        mesh=mesh,
        in_specs=placed,
        out_specs=P("depth", "lat", None),
        check_vma=False,
    )
```

```python
import functools

import jax
import jax.numpy as jnp
from jax import lax
from jax.experimental import pallas as pl
from jax.experimental.pallas import tpu as pltpu
from jax.sharding import PartitionSpec as P

TAU = 300.0
LAMBDA = 0.5
MESH = pl.DeviceIdType.MESH
SCALE = (64.0 * LAMBDA) ** 2
LEAF = 8


def recip(value):
    guess = pl.reciprocal(value, approx=True)
    return guess * (2.0 - value * guess)


def coupling(diff):
    return (3.0 * TAU * SCALE) * recip(SCALE + diff * diff)


def smooth_x(field):
    lane = lax.broadcasted_iota(jnp.int32, field.shape, 1)
    width = field.shape[1]
    before = jnp.where(lane == 0, 0.0, pltpu.roll(field, 1, 1))
    after = jnp.where(lane == width - 1, 0.0, pltpu.roll(field, width - 1, 1))
    return (before + after) + (field + field)


def eliminate(lo, hi, couple, source, keep):
    starts = list(range(lo, hi, LEAF))
    state = []
    for start in starts:
        state.append([1.0, couple(start - 1), source(start), None, None])
    for step in range(LEAF - 1):
        for part, start in enumerate(starts):
            excess, fill, src, excess_low, src_low = state[part]
            cell = start + step
            after = couple(cell)
            inverse = recip(excess + fill + after)
            onward = after * inverse
            back = fill * inverse
            keep(cell, onward, back, src * inverse)
            add_excess = back * excess
            add_src = back * src
            state[part] = [
                1.0 + onward * excess,
                onward * fill,
                source(cell + 1) + onward * src,
                add_excess if excess_low is None else excess_low + add_excess,
                add_src if src_low is None else src_low + add_src,
            ]
    blocks = [(start, start + LEAF, part) for start, part in zip(starts, state)]
    while len(blocks) > 1:
        merged = []
        for first, second in zip(blocks[::2], blocks[1::2]):
            e1, f1, s1, el1, sl1 = first[2]
            e2, f2, s2, el2, sl2 = second[2]
            excess = e1 + el2
            src = s1 + sl2
            inverse = recip(excess + f1 + f2)
            onward = f2 * inverse
            back = f1 * inverse
            keep(first[1] - 1, onward, back, src * inverse)
            merged.append(
                (
                    first[0],
                    second[1],
                    [
                        e2 + onward * excess,
                        onward * f1,
                        s2 + onward * src,
                        el1 + back * excess,
                        sl1 + back * src,
                    ],
                )
            )
        blocks = merged
    e, f, s, el, sl = blocks[0][2]
    return el, sl, f, e, s


def substitute(lo, hi, before, last, load, emit):
    known = {lo - 1: before, hi - 1: last}
    emit(hi - 1, last)
    size = hi - lo
    while size > LEAF:
        for start in range(lo, hi, size):
            middle = start + size // 2 - 1
            onward, back, part = load(middle)
            value = part + back * known[start - 1] + onward * known[start + size - 1]
            known[middle] = value
            emit(middle, value)
        size = size // 2
    current = {start: known[start + LEAF - 1] for start in range(lo, hi, LEAF)}
    for step in range(LEAF - 2, -1, -1):
        for start in range(lo, hi, LEAF):
            onward, back, part = load(start + step)
            value = part + back * known[start - 1] + onward * current[start]
            current[start] = value
            emit(start + step, value)


def solve_reduced(count, got):
    middle = count // 2
    excess, src = [], []
    for k in range(count):
        more = k + 1 < count
        excess.append(got(k, 3) + got(k + 1, 0) if more else got(k, 3))
        src.append(got(k, 4) + got(k + 1, 1) if more else got(k, 4))
    towards, parts = {}, {}

    def fold(k, into):
        couple = got(max(k, into), 2)
        inverse = recip(excess[k] + couple)
        towards[k] = couple * inverse
        parts[k] = src[k] * inverse
        excess[into] = excess[into] + towards[k] * excess[k]
        src[into] = src[into] + towards[k] * src[k]

    for step in range(middle):
        fold(step, step + 1)
        if count - 1 - step > middle:
            fold(count - 1 - step, count - 2 - step)
    values = {middle: src[middle] * recip(excess[middle])}
    for step in range(1, middle + 1):
        values[middle - step] = parts[middle - step] + towards[middle - step] * values[middle - step + 1]
        if middle + step < count:
            values[middle + step] = (
                parts[middle + step] + towards[middle + step] * values[middle + step - 1]
            )
    return [values[k] for k in range(count)]


def lat_solvers(lat_total):
    solvers = max(lat_total // 2, 1)
    return (lat_total - solvers) // 2, solvers


def kernel(
    depth_total, lat_total, planes, rows,
    source, out,
    vol, pack_one, pack_two, yh_one, yh_two, zh_one, zh_two, cn, sm_x, sm, yy, nn,
    vol_y, sm_y, part_y,
    vol_t, sm_t, x_out, xw, xv, xg, zw, zv, zg, yw, yv, yg,
    zsnd, zrcv, zret, zfin, zsep, ysnd, yrcv, yret, yfin, ysep,
    load_sem, halo_send, halo_recv, zs_send, zs_recv, zr_send, zr_recv,
    ys_send, ys_recv, yr_send, yr_recv,
):
    dm = lax.axis_index("depth")
    lm = lax.axis_index("lat")
    has = {
        (-1, 0): dm > 0,
        (1, 0): dm < depth_total - 1,
        (0, -1): lm > 0,
        (0, 1): lm < lat_total - 1,
    }
    for dz in (-1, 1):
        for dy in (-1, 1):
            has[(dz, dy)] = jnp.logical_and(has[(dz, 0)], has[(0, dy)])
    corners = [(dz, dy) for dz in (-1, 1) for dy in (-1, 1)]

    load = pltpu.make_async_copy(source, vol, load_sem)
    load.start()

    barrier = pltpu.get_barrier_semaphore()
    first_solver, solvers = lat_solvers(lat_total)

    def solves(index):
        return jnp.logical_and(index >= first_solver, index < first_solver + solvers)

    expected = jnp.int32(depth_total - 1)
    for step in range(1, lat_total):
        other = lax.rem(lm + step, lat_total)
        meets = jnp.logical_or(
            jnp.logical_or(solves(lm), solves(other)),
            jnp.logical_or(other == lm + 1, other == lm - 1),
        )
        expected = expected + meets.astype(jnp.int32)

        @pl.when(meets)
        def _():
            pl.semaphore_signal(barrier, inc=1, device_id=(dm, other), device_id_type=MESH)

    for step in range(1, depth_total):
        pl.semaphore_signal(
            barrier, inc=1, device_id=(lax.rem(dm + step, depth_total), lm), device_id_type=MESH
        )
    for dz, dy in corners:
        expected = expected + has[(dz, dy)].astype(jnp.int32)

        @pl.when(has[(dz, dy)])
        def _():
            pl.semaphore_signal(
                barrier, inc=1, device_id=(dm + dz, lm + dy), device_id_type=MESH
            )

    load.wait()
    pack_one[...] = vol[pl.ds(0, planes, stride=rows), :]
    for j in range(2):
        pack_two[pl.ds(j, planes, stride=2), :] = vol[pl.ds(rows - 2 + j, planes, stride=rows), :]
    pl.semaphore_wait(barrier, expected)

    def halo_copy(index, way):
        dz, dy = way
        zi, yi = (dz + 1) // 2, (dy + 1) // 2
        if dy == 0:
            src = vol.at[pl.ds(0, rows) if dz < 0 else pl.ds((planes - 2) * rows, 2 * rows)]
            dst = zh_one if dz < 0 else zh_two
        elif dz == 0:
            src, dst = (pack_one, yh_one) if dy < 0 else (pack_two, yh_two)
        else:
            pack, count = (pack_one, planes) if dy < 0 else (pack_two, 2 * planes)
            src = pack.at[pl.ds(0 if dz < 0 else count - 8, 8)]
            dst = cn.at[1 - zi, 1 - yi]
        return pltpu.make_async_remote_copy(
            src_ref=src,
            dst_ref=dst,
            send_sem=halo_send.at[index],
            recv_sem=halo_recv.at[index],
            device_id=(dm + dz, lm + dy),
            device_id_type=MESH,
        )

    ways = [(0, -1), (0, 1)] + corners + [(-1, 0), (1, 0)]
    opposite = {way: ways.index((-way[0], -way[1])) for way in ways}
    for index, way in enumerate(ways):

        @pl.when(has[way])
        def _():
            halo_copy(index, way).start()

    def smooth_y(field):
        row = lax.broadcasted_iota(jnp.int32, field.shape, 0)
        before = jnp.where(row == 0, 0.0, pltpu.roll(field, 1, 0))
        after = jnp.where(row == rows - 1, 0.0, pltpu.roll(field, rows - 1, 0))
        return (before + after) + (field + field)

    def plane_at(plane):
        return pl.ds((plane + 1) * rows, rows)

    older = old = None
    for plane in range(planes + 1):
        new = None
        if plane < planes:
            where = pl.ds(plane * rows, rows)
            along_x = smooth_x(vol[where, :])
            sm_x[where, :] = along_x
            new = smooth_y(along_x)
            if plane == 0:
                sm[plane_at(-1), :] = new
        if old is not None:
            total = old + old
            total = total if older is None else total + older
            sm[plane_at(plane - 1), :] = total if new is None else total + new
        older, old = old, new
    def row_at(row):
        return pl.ds(row * planes, planes)

    for row in range(rows):
        vol_y[row_at(row), :] = vol[pl.ds(row, planes, stride=rows), :]
        sm_y[row_at(row), :] = sm[pl.ds(rows + row, planes, stride=rows), :]

    def wait_halos(chosen):
        for way in chosen:
            back = opposite[way]

            @pl.when(has[way])
            def _():
                halo_copy(back, ways[back]).wait_recv()

            @pl.when(jnp.logical_not(has[way]))
            def _():
                dz, dy = way
                zi, yi = (dz + 1) // 2, (dy + 1) // 2
                if dy == 0:
                    ref = zh_two if dz < 0 else zh_one
                    ref[...] = jnp.zeros(ref.shape, jnp.float32)
                elif dz == 0:
                    ref = yh_two if dy < 0 else yh_one
                    ref[...] = jnp.zeros(ref.shape, jnp.float32)
                else:
                    cn[zi, yi] = jnp.zeros(cn.shape[2:], jnp.float32)

    y_chunk = planes // solvers

    def row_smoothed(row, spans):
        parts = []
        for lo, hi in spans:
            if row >= 0:
                parts.append(sm_y[pl.ds(row * planes + lo, hi - lo), :])
            else:
                middle = yy[pl.ds(8 + lo, hi - lo), :]
                ends = yy[pl.ds(7 + lo, hi - lo), :] + yy[pl.ds(9 + lo, hi - lo), :]
                parts.append(ends + (middle + middle))
        return jnp.concatenate(parts, axis=0)

    def to_solver(k):
        return pltpu.make_async_remote_copy(
            src_ref=ysnd.at[k],
            dst_ref=yrcv.at[lm],
            send_sem=ys_send,
            recv_sem=ys_recv,
            device_id=(dm, first_solver + k),
            device_id_type=MESH,
        )

    def eliminate_rows(spans):
        couples = {}

        def couple(row):
            if row not in couples:
                value = coupling(row_smoothed(row + 1, spans) - row_smoothed(row, spans))
                if row == -1:
                    value = value * jnp.where(has[(0, -1)], 1.0, 0.0)
                couples[row] = value
            return couples[row]

        def source(row):
            return jnp.concatenate(
                [vol_y[pl.ds(row * planes + lo, hi - lo), :] for lo, hi in spans], axis=0
            )

        def keep(row, *values):
            for ref, value in zip((yw, yv, yg), values):
                base = 0
                for lo, hi in spans:
                    ref[row, pl.ds(lo, hi - lo), :] = value[base : base + hi - lo]
                    base += hi - lo

        results = eliminate(0, rows, couple, source, keep)
        used = []
        base = 0
        for lo, hi in spans:
            for plane in range(lo, hi, y_chunk):
                k = plane // y_chunk
                used.append(k)
                for q, value in enumerate(results):
                    ysnd[k, pl.ds(q * y_chunk, y_chunk), :] = value[base : base + y_chunk]
                base += y_chunk
        for k in used:

            @pl.when(lm != first_solver + k)
            def _():
                to_solver(k).start()

            @pl.when(lm == first_solver + k)
            def _():
                yrcv[lm] = ysnd[k]

    wait_halos(ways[:2])
    far_row = smooth_x(yh_two[pl.ds(0, planes, stride=2), :])
    low_row = smooth_x(yh_two[pl.ds(1, planes, stride=2), :])
    high_row = smooth_x(yh_one[...])
    edge_row = sm_x[pl.ds(0, planes, stride=rows), :]
    yy[pl.ds(8, planes), :] = (far_row + edge_row) + (low_row + low_row)
    for side, edge, row in ((0, 0, low_row), (1, rows - 1, high_row)):
        nn[side, pl.ds(8, planes), :] = row
        nn[side, pl.ds(0, 8), :] = jnp.zeros((8, vol.shape[1]), jnp.float32)
        nn[side, pl.ds(8 + planes, 8), :] = jnp.zeros((8, vol.shape[1]), jnp.float32)
        where = pl.ds(rows + edge, planes, stride=rows)
        ends = nn[side, pl.ds(7, planes), :] + nn[side, pl.ds(9, planes), :]
        change = ends + (row + row)
        sm[where, :] = sm[where, :] + change
        sm_y[row_at(edge), :] = sm_y[row_at(edge), :] + change

    eliminate_rows(((8, planes - 8),))

    wait_halos(ways[2:])
    far_x = smooth_x(zh_two[pl.ds(0, rows), :])
    low_x = smooth_x(zh_two[pl.ds(rows, rows), :])
    high_x = smooth_x(zh_one[...])
    low_y = smooth_y(low_x)
    high_y = smooth_y(high_x)
    low_tile = smooth_x(cn[0, 0])
    high_tile = smooth_x(cn[1, 0])
    for where, plane_x, far_one, near_one in (
        (7, low_x, low_tile[6:7], low_tile[7:8]),
        (8 + planes, high_x, high_tile[0:1], high_tile[1:2]),
    ):
        yy[pl.ds(where, 1), :] = (far_one + plane_x[0:1]) + (near_one + near_one)
    low_side = (0, low_row, low_tile[5:6], low_tile[7:8], high_tile[1:2])
    low_tile = smooth_x(cn[0, 1])
    high_tile = smooth_x(cn[1, 1])
    high_side = (rows - 1, high_row, low_tile[6:7], low_tile[7:8], high_tile[0:1])
    sm[plane_at(-1), :] = sm[plane_at(-1), :] + smooth_y(far_x) + (low_y + low_y)
    for edge, row, two_before, before, after in (low_side, high_side):
        where = pl.ds(edge, 1)
        sm[where, :] = sm[where, :] + row[0:1] + two_before + (before + before)
        for plane, change in ((0, before), (planes - 1, after)):
            where = pl.ds((plane + 1) * rows + edge, 1)
            sm[where, :] = sm[where, :] + change
            where = pl.ds(edge * planes + plane, 1)
            sm_y[where, :] = sm_y[where, :] + change
    for plane, change in ((0, low_y), (planes - 1, high_y)):
        sm[plane_at(plane), :] = sm[plane_at(plane), :] + change
        where = pl.ds(plane, rows, stride=planes)
        sm_y[where, :] = sm_y[where, :] + change
    eliminate_rows(((0, 8), (planes - 8, planes)))

    def exchange(axis, src, dst, sems, total, me):
        for step in sorted(range(1, total), key=lambda step: abs(2 * step - total)):
            other = lax.rem(me + step, total)
            pltpu.make_async_remote_copy(
                src_ref=src.at[other],
                dst_ref=dst.at[me],
                send_sem=sems[0],
                recv_sem=sems[1],
                device_id=(other, lm) if axis == "depth" else (dm, other),
                device_id_type=MESH,
            ).start()
        dst[me] = src[me]

    def wait_all(ref, sem, total):
        some = ref.at[pl.ds(0, total - 1)]
        pltpu.make_async_copy(some, some, sem).wait()

    def from_solver(k):
        return pltpu.make_async_remote_copy(
            src_ref=yret.at[k],
            dst_ref=yfin.at[lm - first_solver],
            send_sem=yr_send,
            recv_sem=yr_recv,
            device_id=(dm, k),
            device_id_type=MESH,
        )

    z_couples = {}

    def z_couple(plane):
        if plane not in z_couples:
            diff = sm[pl.ds((plane + 2) * rows, rows), :] - sm[pl.ds((plane + 1) * rows, rows), :]
            value = coupling(diff)
            if plane == -1:
                value = value * jnp.where(has[(-1, 0)], 1.0, 0.0)
            z_couples[plane] = value
        return z_couples[plane]

    def z_keep(plane, onward, back, part):
        zw[plane] = onward
        zv[plane] = back
        zg[plane] = part

    z_chunk = rows // depth_total
    results = eliminate(
        0, planes, z_couple, lambda plane: vol[pl.ds(plane * rows, rows), :], z_keep
    )
    for q, value in enumerate(results):
        for k in range(depth_total):
            zsnd[k, pl.ds(q * z_chunk, z_chunk), :] = value[k * z_chunk : (k + 1) * z_chunk]
    exchange("depth", zsnd, zrcv, (zs_send, zs_recv), depth_total, dm)

    tile = vol.shape[1]
    blocks = planes * rows // tile
    for block in range(blocks):
        where = pl.ds(block * tile, tile)
        vol_t[where, :] = vol[where, :].T
        sm_t[where, :] = sm[pl.ds(rows + block * tile, tile), :].T
    cells = tile // 8
    spread = blocks * 8

    def x_at(cell):
        return pl.ds(cell, spread, stride=cells)

    def turn(field, by):
        return pltpu.roll(field.reshape(blocks, 8, tile), by, 1).reshape(spread, tile)

    x_couples = {}

    def x_couple(cell):
        if cell not in x_couples:
            if cell == -1:
                value = turn(x_couple(cells - 1), 1)
            elif cell == cells - 1:
                sub = lax.rem(lax.broadcasted_iota(jnp.int32, (spread, tile), 0), 8)
                diff = turn(sm_t[x_at(0), :], 7) - sm_t[x_at(cell), :]
                value = jnp.where(sub == 7, 0.0, coupling(diff))
            else:
                value = coupling(sm_t[x_at(cell + 1), :] - sm_t[x_at(cell), :])
            x_couples[cell] = value
        return x_couples[cell]

    def x_keep(cell, onward, back, part):
        xw[cell] = onward
        xv[cell] = back
        xg[cell] = part

    excess_low, src_low, couple, excess, src = eliminate(
        0, cells, x_couple, lambda cell: vol_t[x_at(cell), :], x_keep
    )
    x_ends = (excess_low, src_low, couple, excess, src)

    def reduce_and_return(axis, rcv, ret, fin, recv, sems, total, me, chunk):
        wait_all(rcv, recv, total)
        reduce_into(rcv, ret, total, chunk)
        exchange(axis, ret, fin, sems, total, me)

    def reduce_into(rcv, ret, total, chunk):
        values = solve_reduced(total, lambda k, q: rcv[k, pl.ds(q * chunk, chunk), :])
        for k in range(total):
            ret[k, pl.ds(0, chunk), :] = values[k - 1] if k else jnp.zeros_like(values[0])
            ret[k, pl.ds(chunk, chunk), :] = values[k]

    z_sems = (zr_send, zr_recv)
    reduce_and_return("depth", zrcv, zret, zfin, zs_recv, z_sems, depth_total, dm, z_chunk)

    @pl.when(solves(lm))
    def _():
        wait_all(yrcv, ys_recv, lat_total)
        reduce_into(yrcv, yret, lat_total, y_chunk)
        for k in sorted(range(lat_total), key=lambda k: -abs(2 * k + 1 - lat_total)):

            @pl.when(lm != k)
            def _():
                from_solver(k).start()

        yfin[lm - first_solver] = yret[lm]


    def gather(fin, sep, total, chunk):
        for k in range(total):
            for q in range(2):
                sep[q, pl.ds(k * chunk, chunk), :] = fin[k, pl.ds(q * chunk, chunk), :]

    excess_low, src_low, couple, excess, src = x_ends
    diag = excess + turn(excess_low, 7) + couple
    src = src + turn(src_low, 7)
    couple = turn(couple, 7)
    diag = diag + couple
    offset = 1
    while offset < 8:
        inverse = recip(diag)
        scaled = couple * inverse
        after = couple * turn(inverse, 8 - offset)
        new_diag = diag - turn(couple * scaled, offset) - couple * after
        src = src + turn(scaled * src, offset) + couple * turn(inverse * src, 8 - offset)
        if 2 * offset < 8:
            couple = couple * turn(scaled, 8 - offset)
        diag = new_diag
        offset = offset * 2
    last = src * recip(diag)

    def x_emit(cell, value):
        x_out[x_at(cell), :] = value

    substitute(0, cells, turn(last, 1), last, lambda c: (xw[c], xv[c], xg[c]), x_emit)
    for block in range(blocks):
        where = pl.ds(block * tile, tile)
        out[where, :] = x_out[where, :].T

    wait_all(zfin, zr_recv, depth_total)
    gather(zfin, zsep, depth_total, z_chunk)

    def z_emit(plane, value):
        where = pl.ds(plane * rows, rows)
        out[where, :] = out[where, :] + value

    substitute(
        0, planes, zsep[0], zsep[1], lambda p: (zw[p], zv[p], zg[p]), z_emit
    )

    for row in range(rows):
        part_y[row_at(row), :] = out[pl.ds(row, planes, stride=rows), :] * (1.0 / 3.0)

    def wait_solvers(ref, sem):
        @pl.when(solves(lm))
        def _():
            wait_all(ref, sem, solvers)

        @pl.when(jnp.logical_not(solves(lm)))
        def _():
            wait_all(ref, sem, solvers + 1)

    wait_solvers(yfin, yr_recv)
    gather(yfin, ysep, solvers, y_chunk)

    def y_emit(row, value):
        out[pl.ds(row, planes, stride=rows), :] = part_y[row_at(row), :] + value * (1.0 / 3.0)

    substitute(0, rows, ysep[0], ysep[1], lambda r: (yw[r], yv[r], yg[r]), y_emit)
    wait_all(zsnd, zs_send, depth_total)
    wait_all(zret, zr_send, depth_total)
    wait_solvers(ysnd, ys_send)

    @pl.when(solves(lm))
    def _():
        wait_all(yret, yr_send, lat_total)

    for index, way in enumerate(ways):

        @pl.when(has[way])
        def _():
            halo_copy(index, way).wait_send()


def shards(depth_total, lat_total, volume):
    planes, rows, columns = volume.shape
    solvers = lat_solvers(lat_total)[1]
    y_chunk = planes // solvers
    z_chunk = rows // depth_total
    f32 = jnp.float32

    def vmem(*shape):
        return pltpu.VMEM(shape + (columns,), f32)

    def dma(count):
        return pltpu.SemaphoreType.DMA((count,))

    cells = planes * rows
    out = pl.pallas_call(
        functools.partial(kernel, depth_total, lat_total, planes, rows),
        out_shape=jax.ShapeDtypeStruct((cells, columns), f32),
        in_specs=[pl.BlockSpec(memory_space=pltpu.HBM)],
        out_specs=pl.BlockSpec(memory_space=pltpu.VMEM),
        scratch_shapes=[
            vmem(cells),
            vmem(planes),
            vmem(2 * planes),
            vmem(planes),
            vmem(2 * planes),
            vmem(rows),
            vmem(2 * rows),
            vmem(2, 2, 8),
            vmem(cells),
            vmem((planes + 1) * rows),
            vmem(planes + 16),
            vmem(2, planes + 16),
            vmem(cells),
            vmem(cells),
            vmem(cells),
            vmem(cells),
            vmem(cells),
            vmem(cells),
            vmem(columns // 8, cells * 8 // columns),
            vmem(columns // 8, cells * 8 // columns),
            vmem(columns // 8, cells * 8 // columns),
            vmem(planes, rows),
            vmem(planes, rows),
            vmem(planes, rows),
            vmem(rows, planes),
            vmem(rows, planes),
            vmem(rows, planes),
            vmem(depth_total, 5 * z_chunk),
            vmem(depth_total, 5 * z_chunk),
            vmem(depth_total, 2 * z_chunk),
            vmem(depth_total, 2 * z_chunk),
            vmem(2, rows),
            vmem(solvers, 5 * y_chunk),
            vmem(lat_total, 5 * y_chunk),
            vmem(lat_total, 2 * y_chunk),
            vmem(solvers, 2 * y_chunk),
            vmem(2, planes),
            pltpu.SemaphoreType.DMA,
            dma(8),
            dma(8),
            pltpu.SemaphoreType.DMA,
            pltpu.SemaphoreType.DMA,
            pltpu.SemaphoreType.DMA,
            pltpu.SemaphoreType.DMA,
            pltpu.SemaphoreType.DMA,
            pltpu.SemaphoreType.DMA,
            pltpu.SemaphoreType.DMA,
            pltpu.SemaphoreType.DMA,
        ],
        compiler_params=pltpu.CompilerParams(
            collective_id=0, has_side_effects=True, vmem_limit_bytes=24 * 1024 * 1024
        ),
        cost_estimate=pl.CostEstimate(
            flops=400 * cells * columns, bytes_accessed=8 * cells * columns, transcendentals=0
        ),
    )(pltpu.with_memory_space_constraint(volume.reshape(cells, columns), pltpu.HBM))
    return out.reshape(volume.shape)


def solution(mesh):
    placed = (P("depth", "lat", None),)
    return jax.shard_map(
        functools.partial(shards, mesh.shape["depth"], mesh.shape["lat"]),
        mesh=mesh,
        in_specs=placed,
        out_specs=P("depth", "lat", None),
        check_vma=False,
    )
```

```python
import functools

import jax
import jax.numpy as jnp
from jax import lax
from jax.experimental import pallas as pl
from jax.experimental.pallas import tpu as pltpu
from jax.sharding import PartitionSpec as P

TAU = 300.0
LAMBDA = 0.5
MESH = pl.DeviceIdType.MESH
SCALE = (64.0 * LAMBDA) ** 2
LEAF = 8
ROW_LEAF = 4


def recip(value):
    guess = pl.reciprocal(value, approx=True)
    return guess * (2.0 - value * guess)


def coupling(diff):
    return (3.0 * TAU * SCALE) * recip(SCALE + diff * diff)


def smooth_x(field):
    lane = lax.broadcasted_iota(jnp.int32, field.shape, 1)
    width = field.shape[1]
    before = jnp.where(lane == 0, 0.0, pltpu.roll(field, 1, 1))
    after = jnp.where(lane == width - 1, 0.0, pltpu.roll(field, width - 1, 1))
    return (before + after) + (field + field)


def eliminate(lo, hi, leaf, couple, source, keep):
    starts = list(range(lo, hi, leaf))
    state = []
    for start in starts:
        state.append([1.0, couple(start - 1), source(start), None, None])
    for step in range(leaf - 1):
        for part, start in enumerate(starts):
            excess, fill, src, excess_low, src_low = state[part]
            cell = start + step
            after = couple(cell)
            inverse = recip(excess + fill + after)
            onward = after * inverse
            back = fill * inverse
            keep(cell, onward, back, src * inverse)
            add_excess = back * excess
            add_src = back * src
            state[part] = [
                1.0 + onward * excess,
                onward * fill,
                source(cell + 1) + onward * src,
                add_excess if excess_low is None else excess_low + add_excess,
                add_src if src_low is None else src_low + add_src,
            ]
    blocks = [(start, start + leaf, part) for start, part in zip(starts, state)]
    while len(blocks) > 1:
        merged = []
        for first, second in zip(blocks[::2], blocks[1::2]):
            e1, f1, s1, el1, sl1 = first[2]
            e2, f2, s2, el2, sl2 = second[2]
            excess = e1 + el2
            src = s1 + sl2
            inverse = recip(excess + f1 + f2)
            onward = f2 * inverse
            back = f1 * inverse
            keep(first[1] - 1, onward, back, src * inverse)
            merged.append(
                (
                    first[0],
                    second[1],
                    [
                        e2 + onward * excess,
                        onward * f1,
                        s2 + onward * src,
                        el1 + back * excess,
                        sl1 + back * src,
                    ],
                )
            )
        blocks = merged
    e, f, s, el, sl = blocks[0][2]
    return el, sl, f, e, s


def substitute(lo, hi, leaf, before, last, load, emit):
    known = {lo - 1: before, hi - 1: last}
    emit(hi - 1, last)
    size = hi - lo
    while size > leaf:
        for start in range(lo, hi, size):
            middle = start + size // 2 - 1
            onward, back, part = load(middle)
            value = part + back * known[start - 1] + onward * known[start + size - 1]
            known[middle] = value
            emit(middle, value)
        size = size // 2
    current = {start: known[start + leaf - 1] for start in range(lo, hi, leaf)}
    for step in range(leaf - 2, -1, -1):
        for start in range(lo, hi, leaf):
            onward, back, part = load(start + step)
            value = part + back * known[start - 1] + onward * current[start]
            current[start] = value
            emit(start + step, value)


def solve_reduced(count, got):
    middle = count // 2
    excess, src = [], []
    for k in range(count):
        more = k + 1 < count
        excess.append(got(k, 3) + got(k + 1, 0) if more else got(k, 3))
        src.append(got(k, 4) + got(k + 1, 1) if more else got(k, 4))
    towards, parts = {}, {}

    def fold(k, into):
        couple = got(max(k, into), 2)
        inverse = recip(excess[k] + couple)
        towards[k] = couple * inverse
        parts[k] = src[k] * inverse
        excess[into] = excess[into] + towards[k] * excess[k]
        src[into] = src[into] + towards[k] * src[k]

    for step in range(middle):
        fold(step, step + 1)
        if count - 1 - step > middle:
            fold(count - 1 - step, count - 2 - step)
    values = {middle: src[middle] * recip(excess[middle])}
    for step in range(1, middle + 1):
        values[middle - step] = parts[middle - step] + towards[middle - step] * values[middle - step + 1]
        if middle + step < count:
            values[middle + step] = (
                parts[middle + step] + towards[middle + step] * values[middle + step - 1]
            )
    return [values[k] for k in range(count)]


def lat_solvers(lat_total):
    solvers = max(lat_total // 2, 1)
    return (lat_total - solvers) // 2, solvers


def kernel(
    depth_total, lat_total, planes, rows,
    source, out,
    vol, pack_one, pack_two, yh_one, yh_two, zh_one, zh_two, cn, sm_x, sm, yy, nn,
    vol_y, sm_y, part_y,
    vol_t, sm_t, x_out, xw, xv, xg, zw, zv, zg, yw, yv, yg,
    zsnd, zrcv, zret, zfin, zsep, ysnd, yrcv, yret, yfin, ysep,
    load_sem, halo_send, halo_recv, zs_send, zs_recv, zr_send, zr_recv,
    ys_send, ys_recv, yr_send, yr_recv,
):
    dm = lax.axis_index("depth")
    lm = lax.axis_index("lat")
    has = {
        (-1, 0): dm > 0,
        (1, 0): dm < depth_total - 1,
        (0, -1): lm > 0,
        (0, 1): lm < lat_total - 1,
    }
    for dz in (-1, 1):
        for dy in (-1, 1):
            has[(dz, dy)] = jnp.logical_and(has[(dz, 0)], has[(0, dy)])
    corners = [(dz, dy) for dz in (-1, 1) for dy in (-1, 1)]

    load = pltpu.make_async_copy(source, vol, load_sem)
    load.start()

    barrier = pltpu.get_barrier_semaphore()
    first_solver, solvers = lat_solvers(lat_total)

    def solves(index):
        return jnp.logical_and(index >= first_solver, index < first_solver + solvers)

    expected = jnp.int32(depth_total - 1)
    for step in range(1, lat_total):
        other = lax.rem(lm + step, lat_total)
        meets = jnp.logical_or(
            jnp.logical_or(solves(lm), solves(other)),
            jnp.logical_or(other == lm + 1, other == lm - 1),
        )
        expected = expected + meets.astype(jnp.int32)

        @pl.when(meets)
        def _():
            pl.semaphore_signal(barrier, inc=1, device_id=(dm, other), device_id_type=MESH)

    for step in range(1, depth_total):
        pl.semaphore_signal(
            barrier, inc=1, device_id=(lax.rem(dm + step, depth_total), lm), device_id_type=MESH
        )
    for dz, dy in corners:
        expected = expected + has[(dz, dy)].astype(jnp.int32)

        @pl.when(has[(dz, dy)])
        def _():
            pl.semaphore_signal(
                barrier, inc=1, device_id=(dm + dz, lm + dy), device_id_type=MESH
            )

    load.wait()
    pack_one[...] = vol[pl.ds(0, planes, stride=rows), :]
    for j in range(2):
        pack_two[pl.ds(j, planes, stride=2), :] = vol[pl.ds(rows - 2 + j, planes, stride=rows), :]
    pl.semaphore_wait(barrier, expected)

    def halo_copy(index, way):
        dz, dy = way
        zi, yi = (dz + 1) // 2, (dy + 1) // 2
        if dy == 0:
            src = vol.at[pl.ds(0, rows) if dz < 0 else pl.ds((planes - 2) * rows, 2 * rows)]
            dst = zh_one if dz < 0 else zh_two
        elif dz == 0:
            src, dst = (pack_one, yh_one) if dy < 0 else (pack_two, yh_two)
        else:
            pack, count = (pack_one, planes) if dy < 0 else (pack_two, 2 * planes)
            src = pack.at[pl.ds(0 if dz < 0 else count - 8, 8)]
            dst = cn.at[1 - zi, 1 - yi]
        return pltpu.make_async_remote_copy(
            src_ref=src,
            dst_ref=dst,
            send_sem=halo_send.at[index],
            recv_sem=halo_recv.at[index],
            device_id=(dm + dz, lm + dy),
            device_id_type=MESH,
        )

    ways = [(0, -1), (0, 1)] + corners + [(-1, 0), (1, 0)]
    opposite = {way: ways.index((-way[0], -way[1])) for way in ways}
    for index, way in enumerate(ways):

        @pl.when(has[way])
        def _():
            halo_copy(index, way).start()

    def smooth_y(field):
        row = lax.broadcasted_iota(jnp.int32, field.shape, 0)
        before = jnp.where(row == 0, 0.0, pltpu.roll(field, 1, 0))
        after = jnp.where(row == rows - 1, 0.0, pltpu.roll(field, rows - 1, 0))
        return (before + after) + (field + field)

    def plane_at(plane):
        return pl.ds((plane + 1) * rows, rows)

    older = old = None
    for plane in range(planes + 1):
        new = None
        if plane < planes:
            where = pl.ds(plane * rows, rows)
            along_x = smooth_x(vol[where, :])
            sm_x[where, :] = along_x
            new = smooth_y(along_x)
            if plane == 0:
                sm[plane_at(-1), :] = new
        if old is not None:
            total = old + old
            total = total if older is None else total + older
            sm[plane_at(plane - 1), :] = total if new is None else total + new
        older, old = old, new
    def row_at(row):
        return pl.ds(row * planes, planes)

    for row in range(rows):
        vol_y[row_at(row), :] = vol[pl.ds(row, planes, stride=rows), :]
        sm_y[row_at(row), :] = sm[pl.ds(rows + row, planes, stride=rows), :]

    def wait_halos(chosen):
        for way in chosen:
            back = opposite[way]

            @pl.when(has[way])
            def _():
                halo_copy(back, ways[back]).wait_recv()

            @pl.when(jnp.logical_not(has[way]))
            def _():
                dz, dy = way
                zi, yi = (dz + 1) // 2, (dy + 1) // 2
                if dy == 0:
                    ref = zh_two if dz < 0 else zh_one
                    ref[...] = jnp.zeros(ref.shape, jnp.float32)
                elif dz == 0:
                    ref = yh_two if dy < 0 else yh_one
                    ref[...] = jnp.zeros(ref.shape, jnp.float32)
                else:
                    cn[zi, yi] = jnp.zeros(cn.shape[2:], jnp.float32)

    y_chunk = planes // solvers

    def row_smoothed(row, spans):
        parts = []
        for lo, hi in spans:
            if row >= 0:
                parts.append(sm_y[pl.ds(row * planes + lo, hi - lo), :])
            else:
                middle = yy[pl.ds(8 + lo, hi - lo), :]
                ends = yy[pl.ds(7 + lo, hi - lo), :] + yy[pl.ds(9 + lo, hi - lo), :]
                parts.append(ends + (middle + middle))
        return jnp.concatenate(parts, axis=0)

    def to_solver(k):
        return pltpu.make_async_remote_copy(
            src_ref=ysnd.at[k],
            dst_ref=yrcv.at[lm],
            send_sem=ys_send,
            recv_sem=ys_recv,
            device_id=(dm, first_solver + k),
            device_id_type=MESH,
        )

    def eliminate_rows(spans):
        couples = {}

        def couple(row):
            if row not in couples:
                value = coupling(row_smoothed(row + 1, spans) - row_smoothed(row, spans))
                if row == -1:
                    value = value * jnp.where(has[(0, -1)], 1.0, 0.0)
                couples[row] = value
            return couples[row]

        def source(row):
            return jnp.concatenate(
                [vol_y[pl.ds(row * planes + lo, hi - lo), :] for lo, hi in spans], axis=0
            )

        def keep(row, *values):
            for ref, value in zip((yw, yv, yg), values):
                base = 0
                for lo, hi in spans:
                    ref[row, pl.ds(lo, hi - lo), :] = value[base : base + hi - lo]
                    base += hi - lo

        results = eliminate(0, rows, ROW_LEAF, couple, source, keep)
        used = []
        base = 0
        for lo, hi in spans:
            for plane in range(lo, hi, y_chunk):
                k = plane // y_chunk
                used.append(k)
                for q, value in enumerate(results):
                    ysnd[k, pl.ds(q * y_chunk, y_chunk), :] = value[base : base + y_chunk]
                base += y_chunk
        for k in used:

            @pl.when(lm != first_solver + k)
            def _():
                to_solver(k).start()

            @pl.when(lm == first_solver + k)
            def _():
                yrcv[lm] = ysnd[k]

    wait_halos(ways[:2])
    far_row = smooth_x(yh_two[pl.ds(0, planes, stride=2), :])
    low_row = smooth_x(yh_two[pl.ds(1, planes, stride=2), :])
    high_row = smooth_x(yh_one[...])
    edge_row = sm_x[pl.ds(0, planes, stride=rows), :]
    yy[pl.ds(8, planes), :] = (far_row + edge_row) + (low_row + low_row)
    for side, edge, row in ((0, 0, low_row), (1, rows - 1, high_row)):
        nn[side, pl.ds(8, planes), :] = row
        nn[side, pl.ds(0, 8), :] = jnp.zeros((8, vol.shape[1]), jnp.float32)
        nn[side, pl.ds(8 + planes, 8), :] = jnp.zeros((8, vol.shape[1]), jnp.float32)
        where = pl.ds(rows + edge, planes, stride=rows)
        ends = nn[side, pl.ds(7, planes), :] + nn[side, pl.ds(9, planes), :]
        change = ends + (row + row)
        sm[where, :] = sm[where, :] + change
        sm_y[row_at(edge), :] = sm_y[row_at(edge), :] + change

    eliminate_rows(((8, planes - 8),))

    wait_halos(ways[2:])
    far_x = smooth_x(zh_two[pl.ds(0, rows), :])
    low_x = smooth_x(zh_two[pl.ds(rows, rows), :])
    high_x = smooth_x(zh_one[...])
    low_y = smooth_y(low_x)
    high_y = smooth_y(high_x)
    low_tile = smooth_x(cn[0, 0])
    high_tile = smooth_x(cn[1, 0])
    for where, plane_x, far_one, near_one in (
        (7, low_x, low_tile[6:7], low_tile[7:8]),
        (8 + planes, high_x, high_tile[0:1], high_tile[1:2]),
    ):
        yy[pl.ds(where, 1), :] = (far_one + plane_x[0:1]) + (near_one + near_one)
    low_side = (0, low_row, low_tile[5:6], low_tile[7:8], high_tile[1:2])
    low_tile = smooth_x(cn[0, 1])
    high_tile = smooth_x(cn[1, 1])
    high_side = (rows - 1, high_row, low_tile[6:7], low_tile[7:8], high_tile[0:1])
    sm[plane_at(-1), :] = sm[plane_at(-1), :] + smooth_y(far_x) + (low_y + low_y)
    for edge, row, two_before, before, after in (low_side, high_side):
        where = pl.ds(edge, 1)
        sm[where, :] = sm[where, :] + row[0:1] + two_before + (before + before)
        for plane, change in ((0, before), (planes - 1, after)):
            where = pl.ds((plane + 1) * rows + edge, 1)
            sm[where, :] = sm[where, :] + change
            where = pl.ds(edge * planes + plane, 1)
            sm_y[where, :] = sm_y[where, :] + change
    for plane, change in ((0, low_y), (planes - 1, high_y)):
        sm[plane_at(plane), :] = sm[plane_at(plane), :] + change
        where = pl.ds(plane, rows, stride=planes)
        sm_y[where, :] = sm_y[where, :] + change
    eliminate_rows(((0, 8), (planes - 8, planes)))

    def exchange(axis, src, dst, sems, total, me):
        for step in sorted(range(1, total), key=lambda step: abs(2 * step - total)):
            other = lax.rem(me + step, total)
            pltpu.make_async_remote_copy(
                src_ref=src.at[other],
                dst_ref=dst.at[me],
                send_sem=sems[0],
                recv_sem=sems[1],
                device_id=(other, lm) if axis == "depth" else (dm, other),
                device_id_type=MESH,
            ).start()
        dst[me] = src[me]

    def wait_all(ref, sem, total):
        some = ref.at[pl.ds(0, total - 1)]
        pltpu.make_async_copy(some, some, sem).wait()

    def from_solver(k):
        return pltpu.make_async_remote_copy(
            src_ref=yret.at[k],
            dst_ref=yfin.at[lm - first_solver],
            send_sem=yr_send,
            recv_sem=yr_recv,
            device_id=(dm, k),
            device_id_type=MESH,
        )

    z_couples = {}

    def z_couple(plane):
        if plane not in z_couples:
            diff = sm[pl.ds((plane + 2) * rows, rows), :] - sm[pl.ds((plane + 1) * rows, rows), :]
            value = coupling(diff)
            if plane == -1:
                value = value * jnp.where(has[(-1, 0)], 1.0, 0.0)
            z_couples[plane] = value
        return z_couples[plane]

    def z_keep(plane, onward, back, part):
        zw[plane] = onward
        zv[plane] = back
        zg[plane] = part

    z_chunk = rows // depth_total
    results = eliminate(
        0, planes, LEAF, z_couple, lambda plane: vol[pl.ds(plane * rows, rows), :], z_keep
    )
    for q, value in enumerate(results):
        for k in range(depth_total):
            zsnd[k, pl.ds(q * z_chunk, z_chunk), :] = value[k * z_chunk : (k + 1) * z_chunk]
    exchange("depth", zsnd, zrcv, (zs_send, zs_recv), depth_total, dm)

    tile = vol.shape[1]
    blocks = planes * rows // tile
    for block in range(blocks):
        where = pl.ds(block * tile, tile)
        vol_t[where, :] = vol[where, :].T
        sm_t[where, :] = sm[pl.ds(rows + block * tile, tile), :].T
    cells = tile // 8
    spread = blocks * 8

    def x_at(cell):
        return pl.ds(cell, spread, stride=cells)

    def turn(field, by):
        return pltpu.roll(field.reshape(blocks, 8, tile), by, 1).reshape(spread, tile)

    x_couples = {}

    def x_couple(cell):
        if cell not in x_couples:
            if cell == -1:
                value = turn(x_couple(cells - 1), 1)
            elif cell == cells - 1:
                sub = lax.rem(lax.broadcasted_iota(jnp.int32, (spread, tile), 0), 8)
                diff = turn(sm_t[x_at(0), :], 7) - sm_t[x_at(cell), :]
                value = jnp.where(sub == 7, 0.0, coupling(diff))
            else:
                value = coupling(sm_t[x_at(cell + 1), :] - sm_t[x_at(cell), :])
            x_couples[cell] = value
        return x_couples[cell]

    def x_keep(cell, onward, back, part):
        xw[cell] = onward
        xv[cell] = back
        xg[cell] = part

    excess_low, src_low, couple, excess, src = eliminate(
        0, cells, LEAF, x_couple, lambda cell: vol_t[x_at(cell), :], x_keep
    )
    x_ends = (excess_low, src_low, couple, excess, src)

    def reduce_and_return(axis, rcv, ret, fin, recv, sems, total, me, chunk):
        wait_all(rcv, recv, total)
        reduce_into(rcv, ret, total, chunk)
        exchange(axis, ret, fin, sems, total, me)

    def reduce_into(rcv, ret, total, chunk):
        values = solve_reduced(total, lambda k, q: rcv[k, pl.ds(q * chunk, chunk), :])
        for k in range(total):
            ret[k, pl.ds(0, chunk), :] = values[k - 1] if k else jnp.zeros_like(values[0])
            ret[k, pl.ds(chunk, chunk), :] = values[k]

    z_sems = (zr_send, zr_recv)
    reduce_and_return("depth", zrcv, zret, zfin, zs_recv, z_sems, depth_total, dm, z_chunk)

    @pl.when(solves(lm))
    def _():
        wait_all(yrcv, ys_recv, lat_total)
        reduce_into(yrcv, yret, lat_total, y_chunk)
        for k in sorted(range(lat_total), key=lambda k: -abs(2 * k + 1 - lat_total)):

            @pl.when(lm != k)
            def _():
                from_solver(k).start()

        yfin[lm - first_solver] = yret[lm]


    def gather(fin, sep, total, chunk):
        for k in range(total):
            for q in range(2):
                sep[q, pl.ds(k * chunk, chunk), :] = fin[k, pl.ds(q * chunk, chunk), :]

    excess_low, src_low, couple, excess, src = x_ends
    diag = excess + turn(excess_low, 7) + couple
    src = src + turn(src_low, 7)
    couple = turn(couple, 7)
    diag = diag + couple
    offset = 1
    while offset < 8:
        inverse = recip(diag)
        scaled = couple * inverse
        after = couple * turn(inverse, 8 - offset)
        new_diag = diag - turn(couple * scaled, offset) - couple * after
        src = src + turn(scaled * src, offset) + couple * turn(inverse * src, 8 - offset)
        if 2 * offset < 8:
            couple = couple * turn(scaled, 8 - offset)
        diag = new_diag
        offset = offset * 2
    last = src * recip(diag)

    def x_emit(cell, value):
        x_out[x_at(cell), :] = value

    substitute(0, cells, LEAF, turn(last, 1), last, lambda c: (xw[c], xv[c], xg[c]), x_emit)
    for block in range(blocks):
        where = pl.ds(block * tile, tile)
        out[where, :] = x_out[where, :].T

    wait_all(zfin, zr_recv, depth_total)
    gather(zfin, zsep, depth_total, z_chunk)

    def z_emit(plane, value):
        where = pl.ds(plane * rows, rows)
        out[where, :] = out[where, :] + value

    substitute(
        0, planes, LEAF, zsep[0], zsep[1], lambda p: (zw[p], zv[p], zg[p]), z_emit
    )

    for row in range(rows):
        part_y[row_at(row), :] = out[pl.ds(row, planes, stride=rows), :] * (1.0 / 3.0)

    def wait_solvers(ref, sem):
        @pl.when(solves(lm))
        def _():
            wait_all(ref, sem, solvers)

        @pl.when(jnp.logical_not(solves(lm)))
        def _():
            wait_all(ref, sem, solvers + 1)

    wait_solvers(yfin, yr_recv)
    gather(yfin, ysep, solvers, y_chunk)

    def y_emit(row, value):
        out[pl.ds(row, planes, stride=rows), :] = part_y[row_at(row), :] + value * (1.0 / 3.0)

    substitute(0, rows, ROW_LEAF, ysep[0], ysep[1], lambda r: (yw[r], yv[r], yg[r]), y_emit)
    wait_all(zsnd, zs_send, depth_total)
    wait_all(zret, zr_send, depth_total)
    wait_solvers(ysnd, ys_send)

    @pl.when(solves(lm))
    def _():
        wait_all(yret, yr_send, lat_total)

    for index, way in enumerate(ways):

        @pl.when(has[way])
        def _():
            halo_copy(index, way).wait_send()


def shards(depth_total, lat_total, volume):
    planes, rows, columns = volume.shape
    solvers = lat_solvers(lat_total)[1]
    y_chunk = planes // solvers
    z_chunk = rows // depth_total
    f32 = jnp.float32

    def vmem(*shape):
        return pltpu.VMEM(shape + (columns,), f32)

    def dma(count):
        return pltpu.SemaphoreType.DMA((count,))

    cells = planes * rows
    out = pl.pallas_call(
        functools.partial(kernel, depth_total, lat_total, planes, rows),
        out_shape=jax.ShapeDtypeStruct((cells, columns), f32),
        in_specs=[pl.BlockSpec(memory_space=pltpu.HBM)],
        out_specs=pl.BlockSpec(memory_space=pltpu.VMEM),
        scratch_shapes=[
            vmem(cells),
            vmem(planes),
            vmem(2 * planes),
            vmem(planes),
            vmem(2 * planes),
            vmem(rows),
            vmem(2 * rows),
            vmem(2, 2, 8),
            vmem(cells),
            vmem((planes + 1) * rows),
            vmem(planes + 16),
            vmem(2, planes + 16),
            vmem(cells),
            vmem(cells),
            vmem(cells),
            vmem(cells),
            vmem(cells),
            vmem(cells),
            vmem(columns // 8, cells * 8 // columns),
            vmem(columns // 8, cells * 8 // columns),
            vmem(columns // 8, cells * 8 // columns),
            vmem(planes, rows),
            vmem(planes, rows),
            vmem(planes, rows),
            vmem(rows, planes),
            vmem(rows, planes),
            vmem(rows, planes),
            vmem(depth_total, 5 * z_chunk),
            vmem(depth_total, 5 * z_chunk),
            vmem(depth_total, 2 * z_chunk),
            vmem(depth_total, 2 * z_chunk),
            vmem(2, rows),
            vmem(solvers, 5 * y_chunk),
            vmem(lat_total, 5 * y_chunk),
            vmem(lat_total, 2 * y_chunk),
            vmem(solvers, 2 * y_chunk),
            vmem(2, planes),
            pltpu.SemaphoreType.DMA,
            dma(8),
            dma(8),
            pltpu.SemaphoreType.DMA,
            pltpu.SemaphoreType.DMA,
            pltpu.SemaphoreType.DMA,
            pltpu.SemaphoreType.DMA,
            pltpu.SemaphoreType.DMA,
            pltpu.SemaphoreType.DMA,
            pltpu.SemaphoreType.DMA,
            pltpu.SemaphoreType.DMA,
        ],
        compiler_params=pltpu.CompilerParams(
            collective_id=0, has_side_effects=True, vmem_limit_bytes=24 * 1024 * 1024
        ),
        cost_estimate=pl.CostEstimate(
            flops=400 * cells * columns, bytes_accessed=8 * cells * columns, transcendentals=0
        ),
    )(pltpu.with_memory_space_constraint(volume.reshape(cells, columns), pltpu.HBM))
    return out.reshape(volume.shape)


def solution(mesh):
    placed = (P("depth", "lat", None),)
    return jax.shard_map(
        functools.partial(shards, mesh.shape["depth"], mesh.shape["lat"]),
        mesh=mesh,
        in_specs=placed,
        out_specs=P("depth", "lat", None),
        check_vma=False,
    )
```

```python
import functools

import jax
import jax.numpy as jnp
from jax import lax
from jax.experimental import pallas as pl
from jax.experimental.pallas import tpu as pltpu
from jax.sharding import PartitionSpec as P

TAU = 300.0
LAMBDA = 0.5
MESH = pl.DeviceIdType.MESH
SCALE = (64.0 * LAMBDA) ** 2
LEAF = 8
ROW_LEAF = 4


def recip(value):
    guess = pl.reciprocal(value, approx=True)
    return guess * (2.0 - value * guess)


def coupling(diff):
    return (3.0 * TAU * SCALE) * recip(SCALE + diff * diff)


def smooth_x(field):
    lane = lax.broadcasted_iota(jnp.int32, field.shape, 1)
    width = field.shape[1]
    before = jnp.where(lane == 0, 0.0, pltpu.roll(field, 1, 1))
    after = jnp.where(lane == width - 1, 0.0, pltpu.roll(field, width - 1, 1))
    return (before + after) + (field + field)


def eliminate(lo, hi, leaf, couple, source, keep):
    starts = list(range(lo, hi, leaf))
    state = []
    for start in starts:
        state.append([1.0, couple(start - 1), source(start), None, None])
    for step in range(leaf - 1):
        for part, start in enumerate(starts):
            excess, fill, src, excess_low, src_low = state[part]
            cell = start + step
            after = couple(cell)
            inverse = recip(excess + fill + after)
            onward = after * inverse
            back = fill * inverse
            keep(cell, onward, back, src * inverse)
            add_excess = back * excess
            add_src = back * src
            state[part] = [
                1.0 + onward * excess,
                onward * fill,
                source(cell + 1) + onward * src,
                add_excess if excess_low is None else excess_low + add_excess,
                add_src if src_low is None else src_low + add_src,
            ]
    blocks = [(start, start + leaf, part) for start, part in zip(starts, state)]
    while len(blocks) > 1:
        merged = []
        for first, second in zip(blocks[::2], blocks[1::2]):
            e1, f1, s1, el1, sl1 = first[2]
            e2, f2, s2, el2, sl2 = second[2]
            excess = e1 + el2
            src = s1 + sl2
            inverse = recip(excess + f1 + f2)
            onward = f2 * inverse
            back = f1 * inverse
            keep(first[1] - 1, onward, back, src * inverse)
            merged.append(
                (
                    first[0],
                    second[1],
                    [
                        e2 + onward * excess,
                        onward * f1,
                        s2 + onward * src,
                        el1 + back * excess,
                        sl1 + back * src,
                    ],
                )
            )
        blocks = merged
    e, f, s, el, sl = blocks[0][2]
    return el, sl, f, e, s


def substitute(lo, hi, leaf, before, last, load, emit):
    known = {lo - 1: before, hi - 1: last}
    emit(hi - 1, last)
    size = hi - lo
    while size > leaf:
        for start in range(lo, hi, size):
            middle = start + size // 2 - 1
            onward, back, part = load(middle)
            value = part + back * known[start - 1] + onward * known[start + size - 1]
            known[middle] = value
            emit(middle, value)
        size = size // 2
    current = {start: known[start + leaf - 1] for start in range(lo, hi, leaf)}
    for step in range(leaf - 2, -1, -1):
        for start in range(lo, hi, leaf):
            onward, back, part = load(start + step)
            value = part + back * known[start - 1] + onward * current[start]
            current[start] = value
            emit(start + step, value)


def solve_reduced(count, got):
    middle = count // 2
    excess, src = [], []
    for k in range(count):
        more = k + 1 < count
        excess.append(got(k, 3) + got(k + 1, 0) if more else got(k, 3))
        src.append(got(k, 4) + got(k + 1, 1) if more else got(k, 4))
    towards, parts = {}, {}

    def fold(k, into):
        couple = got(max(k, into), 2)
        inverse = recip(excess[k] + couple)
        towards[k] = couple * inverse
        parts[k] = src[k] * inverse
        excess[into] = excess[into] + towards[k] * excess[k]
        src[into] = src[into] + towards[k] * src[k]

    for step in range(middle):
        fold(step, step + 1)
        if count - 1 - step > middle:
            fold(count - 1 - step, count - 2 - step)
    values = {middle: src[middle] * recip(excess[middle])}
    for step in range(1, middle + 1):
        values[middle - step] = parts[middle - step] + towards[middle - step] * values[middle - step + 1]
        if middle + step < count:
            values[middle + step] = (
                parts[middle + step] + towards[middle + step] * values[middle + step - 1]
            )
    return [values[k] for k in range(count)]


def lat_solvers(lat_total):
    solvers = max(lat_total // 2, 1)
    return (lat_total - solvers) // 2, solvers


def kernel(
    depth_total, lat_total, planes, rows,
    source, out,
    vol, pack_one, pack_two, yh_one, yh_two, zh_one, zh_two, cn, sm_x, sm, yy, nn,
    vol_y, sm_y, part_y,
    vol_t, sm_t, x_out, xw, xv, xg, zw, zv, zg, yw, yv, yg,
    zsnd, zrcv, zret, zfin, zsep, ysnd, yrcv, yret, yfin, ysep,
    load_sem, halo_send, halo_recv, zs_send, zs_recv, zr_send, zr_recv,
    ys_send, ys_recv, yr_send, yr_recv,
):
    dm = lax.axis_index("depth")
    lm = lax.axis_index("lat")
    has = {
        (-1, 0): dm > 0,
        (1, 0): dm < depth_total - 1,
        (0, -1): lm > 0,
        (0, 1): lm < lat_total - 1,
    }
    for dz in (-1, 1):
        for dy in (-1, 1):
            has[(dz, dy)] = jnp.logical_and(has[(dz, 0)], has[(0, dy)])
    corners = [(dz, dy) for dz in (-1, 1) for dy in (-1, 1)]

    load = pltpu.make_async_copy(source, vol, load_sem)
    load.start()

    barrier = pltpu.get_barrier_semaphore()
    first_solver, solvers = lat_solvers(lat_total)

    def solves(index):
        return jnp.logical_and(index >= first_solver, index < first_solver + solvers)

    expected = jnp.int32(depth_total - 1)
    for step in range(1, lat_total):
        other = lax.rem(lm + step, lat_total)
        meets = jnp.logical_or(
            jnp.logical_or(solves(lm), solves(other)),
            jnp.logical_or(other == lm + 1, other == lm - 1),
        )
        expected = expected + meets.astype(jnp.int32)

        @pl.when(meets)
        def _():
            pl.semaphore_signal(barrier, inc=1, device_id=(dm, other), device_id_type=MESH)

    for step in range(1, depth_total):
        pl.semaphore_signal(
            barrier, inc=1, device_id=(lax.rem(dm + step, depth_total), lm), device_id_type=MESH
        )
    for dz, dy in corners:
        expected = expected + has[(dz, dy)].astype(jnp.int32)

        @pl.when(has[(dz, dy)])
        def _():
            pl.semaphore_signal(
                barrier, inc=1, device_id=(dm + dz, lm + dy), device_id_type=MESH
            )

    load.wait()
    pack_one[...] = vol[pl.ds(0, planes, stride=rows), :]
    for j in range(2):
        pack_two[pl.ds(j, planes, stride=2), :] = vol[pl.ds(rows - 2 + j, planes, stride=rows), :]
    pl.semaphore_wait(barrier, expected)

    def halo_copy(index, way):
        dz, dy = way
        zi, yi = (dz + 1) // 2, (dy + 1) // 2
        if dy == 0:
            src = vol.at[pl.ds(0, rows) if dz < 0 else pl.ds((planes - 2) * rows, 2 * rows)]
            dst = zh_one if dz < 0 else zh_two
        elif dz == 0:
            src, dst = (pack_one, yh_one) if dy < 0 else (pack_two, yh_two)
        else:
            pack, count = (pack_one, planes) if dy < 0 else (pack_two, 2 * planes)
            src = pack.at[pl.ds(0 if dz < 0 else count - 8, 8)]
            dst = cn.at[1 - zi, 1 - yi]
        return pltpu.make_async_remote_copy(
            src_ref=src,
            dst_ref=dst,
            send_sem=halo_send.at[index],
            recv_sem=halo_recv.at[index],
            device_id=(dm + dz, lm + dy),
            device_id_type=MESH,
        )

    ways = [(0, -1), (0, 1)] + corners + [(-1, 0), (1, 0)]
    opposite = {way: ways.index((-way[0], -way[1])) for way in ways}
    for index, way in enumerate(ways):

        @pl.when(has[way])
        def _():
            halo_copy(index, way).start()

    def smooth_y(field):
        row = lax.broadcasted_iota(jnp.int32, field.shape, 0)
        before = jnp.where(row == 0, 0.0, pltpu.roll(field, 1, 0))
        after = jnp.where(row == rows - 1, 0.0, pltpu.roll(field, rows - 1, 0))
        return (before + after) + (field + field)

    def plane_at(plane):
        return pl.ds((plane + 1) * rows, rows)

    older = old = None
    for plane in range(planes + 1):
        new = None
        if plane < planes:
            where = pl.ds(plane * rows, rows)
            along_x = smooth_x(vol[where, :])
            sm_x[where, :] = along_x
            new = smooth_y(along_x)
            if plane == 0:
                sm[plane_at(-1), :] = new
        if old is not None:
            total = old + old
            total = total if older is None else total + older
            sm[plane_at(plane - 1), :] = total if new is None else total + new
        older, old = old, new
    def row_at(row):
        return pl.ds(row * planes, planes)

    for row in range(rows):
        vol_y[row_at(row), :] = vol[pl.ds(row, planes, stride=rows), :]
        sm_y[row_at(row), :] = sm[pl.ds(rows + row, planes, stride=rows), :]

    def wait_halos(chosen):
        for way in chosen:
            back = opposite[way]

            @pl.when(has[way])
            def _():
                halo_copy(back, ways[back]).wait_recv()

            @pl.when(jnp.logical_not(has[way]))
            def _():
                dz, dy = way
                zi, yi = (dz + 1) // 2, (dy + 1) // 2
                if dy == 0:
                    ref = zh_two if dz < 0 else zh_one
                    ref[...] = jnp.zeros(ref.shape, jnp.float32)
                elif dz == 0:
                    ref = yh_two if dy < 0 else yh_one
                    ref[...] = jnp.zeros(ref.shape, jnp.float32)
                else:
                    cn[zi, yi] = jnp.zeros(cn.shape[2:], jnp.float32)

    y_chunk = planes // solvers

    def row_smoothed(row, spans):
        parts = []
        for lo, hi in spans:
            if row >= 0:
                parts.append(sm_y[pl.ds(row * planes + lo, hi - lo), :])
            else:
                middle = yy[pl.ds(8 + lo, hi - lo), :]
                ends = yy[pl.ds(7 + lo, hi - lo), :] + yy[pl.ds(9 + lo, hi - lo), :]
                parts.append(ends + (middle + middle))
        return jnp.concatenate(parts, axis=0)

    def to_solver(k):
        return pltpu.make_async_remote_copy(
            src_ref=ysnd.at[k],
            dst_ref=yrcv.at[lm],
            send_sem=ys_send,
            recv_sem=ys_recv,
            device_id=(dm, first_solver + k),
            device_id_type=MESH,
        )

    def eliminate_rows(spans):
        couples = {}

        def couple(row):
            if row not in couples:
                value = coupling(row_smoothed(row + 1, spans) - row_smoothed(row, spans))
                if row == -1:
                    value = value * jnp.where(has[(0, -1)], 1.0, 0.0)
                couples[row] = value
            return couples[row]

        def source(row):
            return jnp.concatenate(
                [vol_y[pl.ds(row * planes + lo, hi - lo), :] for lo, hi in spans], axis=0
            )

        def keep(row, *values):
            for ref, value in zip((yw, yv, yg), values):
                base = 0
                for lo, hi in spans:
                    ref[row, pl.ds(lo, hi - lo), :] = value[base : base + hi - lo]
                    base += hi - lo

        results = eliminate(0, rows, ROW_LEAF, couple, source, keep)
        used = []
        base = 0
        for lo, hi in spans:
            for plane in range(lo, hi, y_chunk):
                k = plane // y_chunk
                used.append(k)
                for q, value in enumerate(results):
                    ysnd[k, pl.ds(q * y_chunk, y_chunk), :] = value[base : base + y_chunk]
                base += y_chunk
        for k in used:

            @pl.when(lm != first_solver + k)
            def _():
                to_solver(k).start()

            @pl.when(lm == first_solver + k)
            def _():
                yrcv[lm] = ysnd[k]

    wait_halos(ways[:2])
    far_row = smooth_x(yh_two[pl.ds(0, planes, stride=2), :])
    low_row = smooth_x(yh_two[pl.ds(1, planes, stride=2), :])
    high_row = smooth_x(yh_one[...])
    edge_row = sm_x[pl.ds(0, planes, stride=rows), :]
    yy[pl.ds(8, planes), :] = (far_row + edge_row) + (low_row + low_row)
    for side, edge, row in ((0, 0, low_row), (1, rows - 1, high_row)):
        nn[side, pl.ds(8, planes), :] = row
        nn[side, pl.ds(0, 8), :] = jnp.zeros((8, vol.shape[1]), jnp.float32)
        nn[side, pl.ds(8 + planes, 8), :] = jnp.zeros((8, vol.shape[1]), jnp.float32)
        where = pl.ds(rows + edge, planes, stride=rows)
        ends = nn[side, pl.ds(7, planes), :] + nn[side, pl.ds(9, planes), :]
        change = ends + (row + row)
        sm[where, :] = sm[where, :] + change
        sm_y[row_at(edge), :] = sm_y[row_at(edge), :] + change

    eliminate_rows(((8, planes - 8),))

    wait_halos(ways[2:])
    far_x = smooth_x(zh_two[pl.ds(0, rows), :])
    low_x = smooth_x(zh_two[pl.ds(rows, rows), :])
    high_x = smooth_x(zh_one[...])
    low_y = smooth_y(low_x)
    high_y = smooth_y(high_x)
    low_tile = smooth_x(cn[0, 0])
    high_tile = smooth_x(cn[1, 0])
    for where, plane_x, far_one, near_one in (
        (7, low_x, low_tile[6:7], low_tile[7:8]),
        (8 + planes, high_x, high_tile[0:1], high_tile[1:2]),
    ):
        yy[pl.ds(where, 1), :] = (far_one + plane_x[0:1]) + (near_one + near_one)
    low_side = (0, low_row, low_tile[5:6], low_tile[7:8], high_tile[1:2])
    low_tile = smooth_x(cn[0, 1])
    high_tile = smooth_x(cn[1, 1])
    high_side = (rows - 1, high_row, low_tile[6:7], low_tile[7:8], high_tile[0:1])
    sm[plane_at(-1), :] = sm[plane_at(-1), :] + smooth_y(far_x) + (low_y + low_y)
    for edge, row, two_before, before, after in (low_side, high_side):
        where = pl.ds(edge, 1)
        sm[where, :] = sm[where, :] + row[0:1] + two_before + (before + before)
        for plane, change in ((0, before), (planes - 1, after)):
            where = pl.ds((plane + 1) * rows + edge, 1)
            sm[where, :] = sm[where, :] + change
            where = pl.ds(edge * planes + plane, 1)
            sm_y[where, :] = sm_y[where, :] + change
    for plane, change in ((0, low_y), (planes - 1, high_y)):
        sm[plane_at(plane), :] = sm[plane_at(plane), :] + change
        where = pl.ds(plane, rows, stride=planes)
        sm_y[where, :] = sm_y[where, :] + change
    eliminate_rows(((0, 8), (planes - 8, planes)))

    def exchange(axis, src, dst, sems, total, me):
        for step in sorted(range(1, total), key=lambda step: abs(2 * step - total)):
            other = lax.rem(me + step, total)
            pltpu.make_async_remote_copy(
                src_ref=src.at[other],
                dst_ref=dst.at[me],
                send_sem=sems[0],
                recv_sem=sems[1],
                device_id=(other, lm) if axis == "depth" else (dm, other),
                device_id_type=MESH,
            ).start()
        dst[me] = src[me]

    def wait_all(ref, sem, total):
        some = ref.at[pl.ds(0, total - 1)]
        pltpu.make_async_copy(some, some, sem).wait()

    def from_solver(k):
        return pltpu.make_async_remote_copy(
            src_ref=yret.at[k],
            dst_ref=yfin.at[lm - first_solver],
            send_sem=yr_send,
            recv_sem=yr_recv,
            device_id=(dm, k),
            device_id_type=MESH,
        )

    z_couples = {}

    def z_couple(plane):
        if plane not in z_couples:
            diff = sm[pl.ds((plane + 2) * rows, rows), :] - sm[pl.ds((plane + 1) * rows, rows), :]
            value = coupling(diff)
            if plane == -1:
                value = value * jnp.where(has[(-1, 0)], 1.0, 0.0)
            z_couples[plane] = value
        return z_couples[plane]

    def z_keep(plane, onward, back, part):
        zw[plane] = onward
        zv[plane] = back
        zg[plane] = part

    z_chunk = rows // depth_total
    results = eliminate(
        0, planes, LEAF, z_couple, lambda plane: vol[pl.ds(plane * rows, rows), :], z_keep
    )
    for q, value in enumerate(results):
        for k in range(depth_total):
            zsnd[k, pl.ds(q * z_chunk, z_chunk), :] = value[k * z_chunk : (k + 1) * z_chunk]
    exchange("depth", zsnd, zrcv, (zs_send, zs_recv), depth_total, dm)

    def reduce_and_return(axis, rcv, ret, fin, recv, sems, total, me, chunk):
        wait_all(rcv, recv, total)
        reduce_into(rcv, ret, total, chunk)
        exchange(axis, ret, fin, sems, total, me)

    def reduce_into(rcv, ret, total, chunk):
        values = solve_reduced(total, lambda k, q: rcv[k, pl.ds(q * chunk, chunk), :])
        for k in range(total):
            ret[k, pl.ds(0, chunk), :] = values[k - 1] if k else jnp.zeros_like(values[0])
            ret[k, pl.ds(chunk, chunk), :] = values[k]

    z_sems = (zr_send, zr_recv)
    reduce_and_return("depth", zrcv, zret, zfin, zs_recv, z_sems, depth_total, dm, z_chunk)

    @pl.when(solves(lm))
    def _():
        wait_all(yrcv, ys_recv, lat_total)
        reduce_into(yrcv, yret, lat_total, y_chunk)
        for k in sorted(range(lat_total), key=lambda k: -abs(2 * k + 1 - lat_total)):

            @pl.when(lm != k)
            def _():
                from_solver(k).start()

        yfin[lm - first_solver] = yret[lm]


    def gather(fin, sep, total, chunk):
        for k in range(total):
            for q in range(2):
                sep[q, pl.ds(k * chunk, chunk), :] = fin[k, pl.ds(q * chunk, chunk), :]

    tile = vol.shape[1]
    blocks = planes * rows // tile
    for block in range(blocks):
        where = pl.ds(block * tile, tile)
        vol_t[where, :] = vol[where, :].T
        sm_t[where, :] = sm[pl.ds(rows + block * tile, tile), :].T
    cells = tile // 8
    spread = blocks * 8

    def x_at(cell):
        return pl.ds(cell, spread, stride=cells)

    def turn(field, by):
        return pltpu.roll(field.reshape(blocks, 8, tile), by, 1).reshape(spread, tile)

    x_couples = {}

    def x_couple(cell):
        if cell not in x_couples:
            if cell == -1:
                value = turn(x_couple(cells - 1), 1)
            elif cell == cells - 1:
                sub = lax.rem(lax.broadcasted_iota(jnp.int32, (spread, tile), 0), 8)
                diff = turn(sm_t[x_at(0), :], 7) - sm_t[x_at(cell), :]
                value = jnp.where(sub == 7, 0.0, coupling(diff))
            else:
                value = coupling(sm_t[x_at(cell + 1), :] - sm_t[x_at(cell), :])
            x_couples[cell] = value
        return x_couples[cell]

    def x_keep(cell, onward, back, part):
        xw[cell] = onward
        xv[cell] = back
        xg[cell] = part

    excess_low, src_low, couple, excess, src = eliminate(
        0, cells, LEAF, x_couple, lambda cell: vol_t[x_at(cell), :], x_keep
    )
    diag = excess + turn(excess_low, 7) + couple
    src = src + turn(src_low, 7)
    couple = turn(couple, 7)
    diag = diag + couple
    offset = 1
    while offset < 8:
        inverse = recip(diag)
        scaled = couple * inverse
        after = couple * turn(inverse, 8 - offset)
        new_diag = diag - turn(couple * scaled, offset) - couple * after
        src = src + turn(scaled * src, offset) + couple * turn(inverse * src, 8 - offset)
        if 2 * offset < 8:
            couple = couple * turn(scaled, 8 - offset)
        diag = new_diag
        offset = offset * 2
    last = src * recip(diag)

    def x_emit(cell, value):
        x_out[x_at(cell), :] = value

    substitute(0, cells, LEAF, turn(last, 1), last, lambda c: (xw[c], xv[c], xg[c]), x_emit)
    for block in range(blocks):
        where = pl.ds(block * tile, tile)
        out[where, :] = x_out[where, :].T

    wait_all(zfin, zr_recv, depth_total)
    gather(zfin, zsep, depth_total, z_chunk)

    def z_emit(plane, value):
        where = pl.ds(plane * rows, rows)
        out[where, :] = out[where, :] + value

    substitute(
        0, planes, LEAF, zsep[0], zsep[1], lambda p: (zw[p], zv[p], zg[p]), z_emit
    )

    for row in range(rows):
        part_y[row_at(row), :] = out[pl.ds(row, planes, stride=rows), :] * (1.0 / 3.0)

    def wait_solvers(ref, sem):
        @pl.when(solves(lm))
        def _():
            wait_all(ref, sem, solvers)

        @pl.when(jnp.logical_not(solves(lm)))
        def _():
            wait_all(ref, sem, solvers + 1)

    wait_solvers(yfin, yr_recv)
    gather(yfin, ysep, solvers, y_chunk)

    def y_emit(row, value):
        out[pl.ds(row, planes, stride=rows), :] = part_y[row_at(row), :] + value * (1.0 / 3.0)

    substitute(0, rows, ROW_LEAF, ysep[0], ysep[1], lambda r: (yw[r], yv[r], yg[r]), y_emit)
    wait_all(zsnd, zs_send, depth_total)
    wait_all(zret, zr_send, depth_total)
    wait_solvers(ysnd, ys_send)

    @pl.when(solves(lm))
    def _():
        wait_all(yret, yr_send, lat_total)

    for index, way in enumerate(ways):

        @pl.when(has[way])
        def _():
            halo_copy(index, way).wait_send()


def shards(depth_total, lat_total, volume):
    planes, rows, columns = volume.shape
    solvers = lat_solvers(lat_total)[1]
    y_chunk = planes // solvers
    z_chunk = rows // depth_total
    f32 = jnp.float32

    def vmem(*shape):
        return pltpu.VMEM(shape + (columns,), f32)

    def dma(count):
        return pltpu.SemaphoreType.DMA((count,))

    cells = planes * rows
    out = pl.pallas_call(
        functools.partial(kernel, depth_total, lat_total, planes, rows),
        out_shape=jax.ShapeDtypeStruct((cells, columns), f32),
        in_specs=[pl.BlockSpec(memory_space=pltpu.HBM)],
        out_specs=pl.BlockSpec(memory_space=pltpu.VMEM),
        scratch_shapes=[
            vmem(cells),
            vmem(planes),
            vmem(2 * planes),
            vmem(planes),
            vmem(2 * planes),
            vmem(rows),
            vmem(2 * rows),
            vmem(2, 2, 8),
            vmem(cells),
            vmem((planes + 1) * rows),
            vmem(planes + 16),
            vmem(2, planes + 16),
            vmem(cells),
            vmem(cells),
            vmem(cells),
            vmem(cells),
            vmem(cells),
            vmem(cells),
            vmem(columns // 8, cells * 8 // columns),
            vmem(columns // 8, cells * 8 // columns),
            vmem(columns // 8, cells * 8 // columns),
            vmem(planes, rows),
            vmem(planes, rows),
            vmem(planes, rows),
            vmem(rows, planes),
            vmem(rows, planes),
            vmem(rows, planes),
            vmem(depth_total, 5 * z_chunk),
            vmem(depth_total, 5 * z_chunk),
            vmem(depth_total, 2 * z_chunk),
            vmem(depth_total, 2 * z_chunk),
            vmem(2, rows),
            vmem(solvers, 5 * y_chunk),
            vmem(lat_total, 5 * y_chunk),
            vmem(lat_total, 2 * y_chunk),
            vmem(solvers, 2 * y_chunk),
            vmem(2, planes),
            pltpu.SemaphoreType.DMA,
            dma(8),
            dma(8),
            pltpu.SemaphoreType.DMA,
            pltpu.SemaphoreType.DMA,
            pltpu.SemaphoreType.DMA,
            pltpu.SemaphoreType.DMA,
            pltpu.SemaphoreType.DMA,
            pltpu.SemaphoreType.DMA,
            pltpu.SemaphoreType.DMA,
            pltpu.SemaphoreType.DMA,
        ],
        compiler_params=pltpu.CompilerParams(
            collective_id=0, has_side_effects=True, vmem_limit_bytes=24 * 1024 * 1024
        ),
        cost_estimate=pl.CostEstimate(
            flops=400 * cells * columns, bytes_accessed=8 * cells * columns, transcendentals=0
        ),
    )(pltpu.with_memory_space_constraint(volume.reshape(cells, columns), pltpu.HBM))
    return out.reshape(volume.shape)


def solution(mesh):
    placed = (P("depth", "lat", None),)
    return jax.shard_map(
        functools.partial(shards, mesh.shape["depth"], mesh.shape["lat"]),
        mesh=mesh,
        in_specs=placed,
        out_specs=P("depth", "lat", None),
        check_vma=False,
    )
```
